128 devices in a mesh: row: 16 (over z, y_hi, core), col: 8 (over y_lo, x).
Axes of the slice: x: 4, y: 4 (y_hi: 2, y_lo: 2; y = y_hi * 2 + y_lo), z: 4, core: 2. Of those that a mesh axis runs over, the one named last changes fastest.
Arguments:
- colatitude: float32 [1024], P('row'), may hold values from 0.2 to 2.94
- longitude: float32 [1024], P('row'), may hold values from -3.140625 to 3.140625
- radius_ratio: float32 [1024], P('row'), may hold values from 0.998 to 1.002
- component: int32 [1024], P('row'), may hold values from 0 to 2
- obs_weight: float32 [1024], P('row'), may hold values from 0.0009765625 to 0.015625
- observed: float32 [1024], P('row'), may hold values from -6 to 6
- unknown_map: int32 [3, 98304], replicated, may hold values from 0 to 300, as said below
- slab_map: int32 [3, 4096], P(None, 'col'), may hold values from 0 to 300, as said below
- normal_slab: float32 [98304, 4096], P('row', 'col'), may hold values from -3 to 3
- right_side: float32 [98304], P(('row', 'col')), may hold values from -6 to 6
Outputs:
- normal_out: float32 [98304, 4096], P('row', 'col')
- right_out: float32 [98304], P(('row', 'col'))
The draws below stay inside these ranges and needn't reach their ends.
Inputs may be any that keep to these rules, and one draw needn't show every extreme that they name: `unknown_map`: row 0 is a degree, row 1 an order (at most the degree), row 2 a kind: 0 cosine, 1 sine (never for order 0), 2 an unused stored row (degree 2, order 0). The used rows hold every coefficient of degree 2 to 300 exactly once, in an order drawn from the seed. `slab_map`: rows as in unknown_map, kinds 0 or 1 only: 4096 consecutive unknowns of the order-wise numbering (order by order from 0; within an order the cosines of rising degree, then the sines), starting at a position drawn from the seed.
All inputs are finite; a program needn't handle non-finite values.
Results may differ from the reference program's by a relative error of at most 0.0003.
Values sent between devices are 32-bit elements; how exact they have to be, the bound alone decides.
A program may use at most 320 MiB of HBM per device.

```python
import math
import jax
import jax.numpy as jnp
import numpy as np
from jax import lax

NMAX = 300
N1 = 301
UNKNOWNS = 90597
NUP = 98304
SLAB = 4096
OBS_DEV = 64
NOBS = 1024
N_ROW = 16


def order_wise_table(top_degree):
    degrees = []
    orders = []
    kind_list = []
    for order_index in range(top_degree + 1):
        flags = [0] if order_index == 0 else [0, 1]
        for flag_value in flags:
            for degree_index in range(max(2, order_index), top_degree + 1):
                degrees.append(degree_index)
                orders.append(order_index)
                kind_list.append(flag_value)
    return np.array([degrees, orders, kind_list], dtype=np.int32)


def draw_unknown_map(key, part):
    listing = jnp.asarray(order_wise_table(NMAX))
    spare = NUP - UNKNOWNS
    filler = jnp.concatenate([jnp.full((1, spare), 2, jnp.int32), jnp.zeros((1, spare), jnp.int32), jnp.full((1, spare), 2, jnp.int32)], axis=0)
    whole = jnp.concatenate([listing, filler], axis=1)
    shuffle = jax.random.permutation(key, NUP)
    return jnp.take(whole, shuffle, axis=1)


def draw_slab_map(key, part):
    listing = jnp.asarray(order_wise_table(NMAX))
    first = jax.random.randint(key, (), 0, UNKNOWNS - SLAB + 1)
    return lax.dynamic_slice(listing, (jnp.int32(0), first.astype(jnp.int32)), (3, SLAB))


def plant(values, key, smallest, top_value):
    longest = values.shape.index(max(values.shape))
    spots = []
    for shift in (0, 1):
        where = [jax.random.randint(jax.random.fold_in(key, axis), (), 0, length) for axis, length in enumerate(values.shape)]
        where[longest] = (where[longest] + shift) % values.shape[longest]
        spots.append(tuple(where))
    return values.at[spots[0]].set(smallest).at[spots[1]].set(top_value)


def shard_levels(rng, shape, split, smallest, high):
    def one(axis_at, parts):
        heights = jax.random.uniform(jax.random.fold_in(jax.random.fold_in(rng, 6), axis_at), (parts,), jnp.float32, smallest / len(split), high / len(split))
        return jnp.repeat(jnp.exp(heights), shape[axis_at] // parts).reshape((-1,) + (1,) * (len(shape) - axis_at - 1))

    loudness = one(*split[0])
    for cut in split[1:]:
        loudness = loudness * one(*cut)
    return loudness


def gaussian(rng, dims, spread, limit, shards=(), held_as=jnp.bfloat16):
    drawn = spread * jax.random.normal(rng, dims, jnp.float32)
    if shards:
        drawn = drawn * shard_levels(rng, dims, shards, -0.22, 0.18)
    return jnp.clip(drawn, -limit, limit).astype(held_as)


def setup_inputs(seed: int = 0) -> dict:
    key_list = jax.random.split(jax.random.key(seed), 11)
    return {
        "colatitude": jnp.clip(0.2 + 2.74 * jax.random.uniform(key_list[0], (NOBS,), jnp.float32) ** shard_levels(key_list[0], (NOBS,), ((0, 16),), -0.2, 0.2), 0.2, 2.94),
        "longitude": jnp.clip(jax.random.uniform(key_list[1], (NOBS,), jnp.float32, -3.140625, 3.140625), -3.140625, 3.140625),
        "radius_ratio": jnp.clip(0.998 + 0.0039999485 * jax.random.uniform(key_list[2], (NOBS,), jnp.float32) ** shard_levels(key_list[2], (NOBS,), ((0, 16),), -0.2, 0.2), 0.998, 1.002),
        "component": plant(jax.random.randint(key_list[3], (NOBS,), 0, 3), jax.random.fold_in(key_list[3], 1), 0, 2).astype(jnp.int32),
        "obs_weight": jnp.clip(jnp.exp(math.log(0.015625) - 2.7725887 * jax.random.uniform(key_list[4], (NOBS,), jnp.float32) ** shard_levels(key_list[4], (NOBS,), ((0, 16),), -0.2, 0.2)), 0.0009765625, 0.015625),
        "observed": gaussian(key_list[5], (NOBS,), 1.0, 6.0, ((0, 16),), jnp.float32),
        "unknown_map": draw_unknown_map(jax.random.fold_in(key_list[10], 71), 0),
        "slab_map": draw_slab_map(jax.random.fold_in(key_list[10], 71), 0),
        "normal_slab": gaussian(key_list[8], (NUP, SLAB), 0.5, 3.0, ((0, 16), (1, 8)), jnp.float32),
        "right_side": gaussian(key_list[9], (NUP,), 1.0, 6.0, ((0, 128),), jnp.float32),
    }


def legendre(colatitude):
    cos_theta = jnp.cos(colatitude)
    sine_theta = jnp.sin(colatitude)
    order_grid = jnp.arange(N1).astype(jnp.float32)
    counter = jnp.arange(1, N1).astype(jnp.float32)
    log_steps = 0.5 * jnp.log((2.0 * counter + 1.0) / (2.0 * counter))
    log_start = jnp.concatenate([jnp.zeros((1,), jnp.float32), 0.5 * jnp.log(jnp.float32(2.0)) + jnp.cumsum(log_steps)])
    log_diagonal = log_start[None, :] + order_grid[None, :] * jnp.log(sine_theta)[:, None]
    zeros = jnp.zeros((colatitude.shape[0], N1), jnp.float32)

    def advance(carry, degree):
        latest, earlier, log_scale = carry
        degree_float = degree.astype(jnp.float32)
        denom = jnp.maximum((degree_float - order_grid) * (degree_float + order_grid), 1.0)
        rise_coef = jnp.sqrt((2.0 * degree_float - 1.0) * (2.0 * degree_float + 1.0) / denom)
        fall_num = jnp.maximum((2.0 * degree_float + 1.0) * (degree_float + order_grid - 1.0) * (degree_float - order_grid - 1.0), 0.0)
        fall_coef = jnp.sqrt(fall_num / (denom * jnp.maximum(2.0 * degree_float - 3.0, 1.0)))
        inside = order_grid < degree_float
        diagonal_mask = order_grid == degree_float
        fresh_value = rise_coef * cos_theta[:, None] * latest - fall_coef * earlier
        fresh_value = jnp.where(inside, fresh_value, jnp.where(diagonal_mask, 1.0, 0.0))
        latest = jnp.where(inside, latest, 0.0)
        log_scale = jnp.where(diagonal_mask, log_diagonal, log_scale)
        magnitude = jnp.where(order_grid <= degree_float, jnp.abs(fresh_value) + jnp.abs(latest), 1.0)
        output = fresh_value * jnp.exp(log_scale)
        return ((fresh_value / magnitude, latest / magnitude, log_scale + jnp.log(magnitude)), output)
    carry_start = (zeros, zeros, zeros)
    unused, legendre_table = lax.scan(advance, carry_start, jnp.arange(N1).astype(jnp.int32))
    return legendre_table

def design_rows(legendre_table, colatitude, longitude, radius_ratio, component, index_map):
    degrees = index_map[0]
    orders = index_map[1]
    kind_flag = index_map[2]
    current = legendre_table[degrees, :, orders]
    previous = legendre_table[degrees - 1, :, orders]
    degree_float = degrees.astype(jnp.float32)[:, None]
    order_float = orders.astype(jnp.float32)[:, None]
    cos_theta = jnp.cos(colatitude)[None, :]
    sine_theta = jnp.sin(colatitude)[None, :]
    slope_coef = jnp.sqrt(jnp.maximum((2.0 * degree_float + 1.0) * (degree_float * degree_float - order_float * order_float), 0.0) / (2.0 * degree_float - 1.0))
    slope = (degree_float * cos_theta * current - slope_coef * previous) / sine_theta
    radial_zz = current
    radial_yy = (-(degree_float + 1.0) * current + cos_theta / sine_theta * slope - order_float * order_float * current / (sine_theta * sine_theta)) / ((degree_float + 1.0) * (degree_float + 2.0))
    radial_xx = -radial_zz - radial_yy
    picked = component[None, :]
    component_value = jnp.where(picked == 2, radial_zz, jnp.where(picked == 1, radial_yy, radial_xx))
    attenuate = jnp.exp(-(degree_float + 3.0) * jnp.log(radius_ratio)[None, :])
    phase = order_float * longitude[None, :]
    flag = kind_flag[:, None]
    harmonic = jnp.where(flag == 0, jnp.cos(phase), jnp.where(flag == 1, jnp.sin(phase), 0.0))
    return (attenuate * component_value * harmonic).T

def reference(colatitude, longitude, radius_ratio, component, obs_weight, observed, unknown_map, slab_map, normal_slab, right_side):

    def one_block(block):
        theta_block, long_block, radius_block, comp_block = block
        legendre_table = legendre(theta_block)
        return (design_rows(legendre_table, theta_block, long_block, radius_block, comp_block, unknown_map), design_rows(legendre_table, theta_block, long_block, radius_block, comp_block, slab_map))
    blocks = (colatitude.reshape(N_ROW, OBS_DEV), longitude.reshape(N_ROW, OBS_DEV), radius_ratio.reshape(N_ROW, OBS_DEV), component.reshape(N_ROW, OBS_DEV))
    design, slab_design = lax.map(one_block, blocks)
    design = design.reshape(NOBS, NUP)
    slab_design = slab_design.reshape(NOBS, SLAB)
    weighted = slab_design * obs_weight[:, None]
    scaled = obs_weight * observed
    contract = (((0,), (0,)), ((), ()))
    update = lax.dot_general(design, weighted, contract, precision=lax.Precision.HIGHEST)
    normal_out = normal_slab + update
    right_out = right_side + lax.dot_general(design, scaled, contract, precision=lax.Precision.HIGHEST)
    return (normal_out, right_out)
```

```python
import jax
import jax.numpy as jnp
import numpy as np
from jax import lax
from jax.experimental import pallas as pl
from jax.experimental.pallas import tpu as pltpu
from jax.sharding import PartitionSpec as P

NMAX = 300
TOP = 304
GROUP = 8
GROUPS = TOP // GROUP
STEP = 16
SLOT = STEP + 1
BLOCKS = (NMAX + STEP) // STEP
OBS = 1024
PARTS = 8
UNROLL = 8
CHUNK = 256
SPARE = 310
BASE = 256
BIG = float(2.0**64)
SMALL = float(2.0**-64)
LOG_BIG = float(64.0 * np.log(2.0))
F32 = jnp.float32
BF16 = jnp.bfloat16


def diagonal_logs():
    counter = np.arange(1, TOP, dtype=np.float64)
    steps = 0.5 * np.log((2.0 * counter + 1.0) / (2.0 * counter))
    logs = np.concatenate([[0.0], 0.5 * np.log(2.0) + np.cumsum(steps)])
    return np.broadcast_to(logs[:, None], (TOP, 128)).astype(np.float32)


def inverse_squares():
    degree = np.arange(TOP + 2 * STEP, dtype=np.float64)
    return (1.0 / (degree * degree - 0.25)).astype(np.float32)


def row_facts(degree, order, kind):
    group = order // GROUP
    offset = degree - group * GROUP
    block = offset // STEP
    lane = order % GROUP
    at_value = (block * SLOT + 1 + offset % STEP) * 64 + lane
    at_scale = block * 64 + lane
    n = degree.astype(F32)
    m = order.astype(F32)
    first = group * GROUP + block * STEP
    upto = jnp.ones_like(n)
    before = jnp.ones_like(n)
    for q in range(STEP):
        j = first + q
        jf = j.astype(F32)
        ratio = jnp.where(j > order, (jf * jf - m * m) / (jf * jf - 0.25), 1.0)
        upto = jnp.where(j <= degree, upto * ratio, upto)
        before = jnp.where(j < degree, before * ratio, before)
    grow = lax.rsqrt(upto)
    grow_before = lax.rsqrt(before)
    denom = (n + 1.0) * (n + 2.0)
    mix = grow * (n - m * m) / denom
    slope = jnp.sqrt(jnp.maximum((2.0 * n + 1.0) * (n * n - m * m), 0.0) / (2.0 * n - 1.0))
    past = -grow_before * slope / denom
    return at_value, at_scale, degree * 2, order * 2 + kind, grow, mix, past


def group_starts(order):
    bounds = jnp.arange(GROUPS + 1, dtype=jnp.int32) * GROUP
    return jnp.sum((order[None, :] < bounds[:, None]).astype(jnp.int32), axis=1)


def kernel(
    col_ref, starts_ref, slab_starts_ref, inv_ref,
    rv_ref, rs_ref, rn_ref, rh_ref, rg_ref, rm_ref, rp_ref, rd_ref,
    sv_ref, ss_ref, sn_ref, sh_ref, sg_ref, sm_ref, sp_ref,
    params_ref, logs_ref, right_ref, normal_ref,
    out_ref, right_out_ref,
    value_buf, scale_buf, harm_buf, radial_buf, design_buf, slab_buf,
    slab_hi, slab_lo, in_buf, out_buf, in_sem, out_sem,
):
    rows = normal_ref.shape[0]
    chunks = rows // CHUNK

    def fetch(index, slot):
        return pltpu.make_async_copy(
            normal_ref.at[pl.ds(pl.multiple_of(index * CHUNK, CHUNK), CHUNK)], in_buf.at[slot], in_sem.at[slot]
        )

    def put(index, slot):
        return pltpu.make_async_copy(
            out_buf.at[slot], out_ref.at[pl.ds(pl.multiple_of(index * CHUNK, CHUNK), CHUNK)], out_sem.at[slot]
        )

    fetch(0, 0).start()
    fetch(1, 1).start()

    theta = params_ref[0]
    lon = params_ref[1]
    cos_t = jnp.cos(theta)
    sin_t = jnp.sin(theta)
    log_s = jnp.log(sin_t)
    comp = params_ref[3]
    weight = params_ref[4]
    scaled = weight * params_ref[5]
    part0 = jnp.where(comp == 2.0, 1.0, jnp.where(comp == 1.0, 0.0, -1.0))
    part1 = jnp.where(comp == 2.0, 0.0, jnp.where(comp == 1.0, 1.0, -1.0))
    part1q = part1 / (sin_t * sin_t)
    inv_r = 1.0 / params_ref[2]

    c1 = jnp.cos(lon)
    s1 = jnp.sin(lon)
    cs = [jnp.ones_like(c1)]
    sn = [jnp.zeros_like(c1)]
    for _ in range(8):
        cs.append(cs[-1] * c1 - sn[-1] * s1)
        sn.append(sn[-1] * c1 + cs[-2] * s1)
    c8, s8 = cs[8], sn[8]
    powers = [inv_r * inv_r * inv_r]
    step_r = inv_r
    for _ in range(7):
        powers.append(powers[-1] * inv_r)
    for _ in range(3):
        step_r = step_r * step_r

    def fill(block, carry):
        cc, ss, pw = carry
        base = block * 8
        for j in range(8):
            harm_buf[(base + j) * 2] = cc[j]
            harm_buf[(base + j) * 2 + 1] = ss[j]
            nf = (base + j).astype(F32)
            ratio = (2.0 * nf + 1.0) / ((nf + 1.0) * (nf + 2.0))
            radial_buf[(base + j) * 2] = pw[j] * (part0 - part1 * ratio)
            radial_buf[(base + j) * 2 + 1] = pw[j] * part1q
        return (
            tuple(cc[j] * c8 - ss[j] * s8 for j in range(8)),
            tuple(ss[j] * c8 + cc[j] * s8 for j in range(8)),
            tuple(pw[j] * step_r for j in range(8)),
        )

    lax.fori_loop(0, TOP // 8, fill, (tuple(cs[:8]), tuple(sn[:8]), tuple(powers)))

    sub = lax.broadcasted_iota(jnp.int32, (8, 128), 0)
    subf = sub.astype(F32)

    def spread(values, c):
        return jnp.broadcast_to(values[c : c + 1, :], (8, 128))

    twice = [spread(2.0 * cos_t, c) for c in range(PARTS)]
    logs = [spread(log_s, c) for c in range(PARTS)]

    def entry(v_ref, s_ref, n_ref, h_ref, g_ref, m_ref, p_ref, j):
        at = v_ref[j]
        now = value_buf[pl.ds(at, 8, stride=8), :]
        past = value_buf[pl.ds(at - 64, 8, stride=8), :]
        scale = scale_buf[pl.ds(s_ref[j], 8, stride=8), :]
        f = radial_buf[n_ref[j]]
        g = radial_buf[n_ref[j] + 1]
        h = harm_buf[h_ref[j]]
        body = now * (g_ref[j] * f + m_ref[j] * g) + (p_ref[j] * past) * (cos_t * g)
        return (h * scale) * body

    def group_body(group, _):
        first = group * GROUP
        orders = subf + first.astype(F32)
        squares = orders * orders
        orders_i = sub + first
        diag = logs_ref[pl.ds(pl.multiple_of(first, 8), 8), :]

        def put_values(slot, values):
            at = pl.multiple_of(slot * 64, 64)
            value_buf[pl.ds(at, 64), :] = jnp.concatenate(values, axis=0)

        def ratio_at(j):
            jf = j.astype(F32)
            return (jf * jf - squares) * inv_ref[j]

        seeds = []
        levels = []
        scales = []
        for c in range(PARTS):
            log_seed = diag + orders * logs[c]
            level = jnp.minimum(jnp.ceil(log_seed * (1.0 / LOG_BIG)), 0.0)
            seeds.append(jnp.exp(log_seed - level * LOG_BIG))
            levels.append(level)
            scales.append(jnp.where(level >= 0.0, 1.0, jnp.where(level >= -1.0, SMALL, 0.0)))
        scale_buf[pl.ds(0, 64), :] = jnp.concatenate(scales, axis=0)
        zero = jnp.zeros((8, 128), F32)
        one = [zero] * PARTS
        two = [zero] * PARTS
        put_values(0, one)
        total = jnp.ones((8, 128), F32)
        rho = ratio_at(jnp.maximum(first - 1, 0))
        for i in range(STEP):
            fresh = [twice[c] * one[c] - rho * two[c] for c in range(PARTS)]
            if i < GROUP:
                fresh = [jnp.where(sub == i, seeds[c], fresh[c]) for c in range(PARTS)]
            put_values(1 + i, fresh)
            one, two = fresh, one
            rho = ratio_at(first + i)
            total = total * jnp.where(orders_i < first + i, rho, 1.0)

        def block_body(block, carry):
            one, two, levels, total, rho = carry
            start = first + block * STEP
            sigma = lax.rsqrt(total)
            sigma_small = sigma * SMALL
            limit = 64.0 * total * sigma
            scales = []
            one, two, levels = list(one), list(two), list(levels)
            for c in range(PARTS):
                big = jnp.abs(one[c]) > limit
                factor = jnp.where(big, sigma_small, sigma)
                one[c] = one[c] * factor
                two[c] = two[c] * factor
                levels[c] = jnp.where(big, levels[c] + 1.0, levels[c])
                scales.append(
                    jnp.where(levels[c] >= 0.0, 1.0, jnp.where(levels[c] >= -1.0, SMALL, 0.0))
                )
            scale_buf[pl.ds(pl.multiple_of(block * 64, 64), 64), :] = jnp.concatenate(scales, axis=0)
            put_values(block * SLOT, one)
            total = jnp.ones((8, 128), F32)
            for i in range(STEP):
                fresh = [twice[c] * one[c] - rho * two[c] for c in range(PARTS)]
                put_values(block * SLOT + 1 + i, fresh)
                one, two = fresh, one
                rho = ratio_at(start + i)
                total = total * rho
            return tuple(one), tuple(two), tuple(levels), total, rho

        blocks = (NMAX + 1 - first + STEP - 1) // STEP
        lax.fori_loop(1, blocks, block_body, (tuple(one), tuple(two), tuple(levels), total, rho))

        def slab_rows(piece, _):
            for u in range(UNROLL):
                j = slab_starts_ref[group] + piece * UNROLL + u
                value = entry(sv_ref, ss_ref, sn_ref, sh_ref, sg_ref, sm_ref, sp_ref, j)
                slab_buf[pl.ds((j // 8) * 64 + j % 8, 8, stride=8), :] = value * weight
            return 0

        count = slab_starts_ref[group + 1] - slab_starts_ref[group]
        lax.fori_loop(0, (count + UNROLL - 1) // UNROLL, slab_rows, 0)

        def main_rows(piece, _):
            for u in range(UNROLL):
                j = starts_ref[group] + piece * UNROLL + u
                value = entry(rv_ref, rs_ref, rn_ref, rh_ref, rg_ref, rm_ref, rp_ref, j)
                design_buf[pl.ds(rd_ref[j], 8, stride=8), :] = value
            return 0

        count = starts_ref[group + 1] - starts_ref[group]
        lax.fori_loop(0, (count + UNROLL - 1) // UNROLL, main_rows, 0)
        return 0

    lax.fori_loop(0, GROUPS, group_body, 0)

    def clear(j, _):
        design_buf[pl.ds(rd_ref[j], 8, stride=8), :] = jnp.zeros((8, 128), F32)
        return 0

    lax.fori_loop(starts_ref[GROUPS], rows, clear, 0)

    slab_view = slab_buf.reshape(slab_buf.shape[0] // 64, 8, 8, 128)
    width = out_ref.shape[1]
    for c in range(PARTS):
        for half in range(width // 256):
            block = slab_view[pl.ds(half * 32, 32), c].reshape(256, 128).T
            hi = block.astype(BF16)
            slab_hi[pl.ds(c * 128, 128), pl.ds(half * 256, 256)] = hi
            slab_lo[pl.ds(c * 128, 128), pl.ds(half * 256, 256)] = (block - hi.astype(F32)).astype(BF16)

    view = design_buf.reshape(design_buf.shape[0] // 64, 8, 8, 128)

    own = right_ref.shape[1]
    total = jnp.zeros((own, 128), F32)
    at = col_ref[0] * (own // 8)
    for c in range(PARTS):
        total = total + view[pl.ds(at, own // 8), c].reshape(own, 128) * scaled[c : c + 1, :]
    summed = lax.dot_general(
        jnp.ones((8, 128), F32), total, (((1,), (1,)), ((), ())),
        precision=lax.Precision.HIGHEST, preferred_element_type=F32,
    )
    right_out_ref[...] = right_ref[...] + summed[0:1, :]

    def chunk_body(index, _):
        slot = lax.rem(index, 2)
        his = []
        los = []
        for c in range(PARTS):
            x = view[pl.ds(index * (CHUNK // 8), CHUNK // 8), c].reshape(CHUNK, 128)
            hi = x.astype(BF16)
            his.append(hi)
            los.append((x - hi.astype(F32)).astype(BF16))
        hi = jnp.concatenate(his, axis=1)
        lo = jnp.concatenate(los, axis=1)
        update = jnp.dot(hi, slab_hi[...], preferred_element_type=F32)
        update += jnp.dot(hi, slab_lo[...], preferred_element_type=F32)
        update += jnp.dot(lo, slab_hi[...], preferred_element_type=F32)
        fetch(index, slot).wait()

        @pl.when(index >= 2)
        def _():
            put(index - 2, slot).wait()

        out_buf[slot] = in_buf[slot] + update
        put(index, slot).start()

        @pl.when(index + 2 < chunks)
        def _():
            fetch(index + 2, slot).start()

        return 0

    lax.fori_loop(0, chunks, chunk_body, 0)
    put(chunks - 2, 0).wait()
    put(chunks - 1, 1).wait()


def local_update(params, col, unknowns, slab_map, normal_slab, right_side):
    rows, width = normal_slab.shape
    own = right_side.shape[0]
    degree, order, kind = unknowns[0], unknowns[1], unknowns[2]
    place = lax.broadcasted_iota(jnp.int32, (rows,), 0)
    unused = kind == 2
    key = (
        ((jnp.where(unused, SPARE, order) - BASE) << 23)
        | (degree << 14)
        | (jnp.where(unused, 0, kind) << 13)
        | place
    )
    key = lax.sort(key, is_stable=False)
    order = (key >> 23) + BASE
    starts = group_starts(order)
    unused = order > NMAX
    order = jnp.where(unused, 0, order)
    degree = (key >> 14) & 511
    kind = (key >> 13) & 1
    place = key & 8191
    target = (place // 8) * 64 + place % 8
    facts = row_facts(degree, order, kind)
    pad = UNROLL
    facts = tuple(jnp.concatenate([x, x[:1] + jnp.zeros((pad,), x.dtype)]) for x in facts)
    target = jnp.concatenate([target, (rows // 8) * 64 + jnp.arange(pad, dtype=jnp.int32)])
    slab_facts = row_facts(slab_map[0], slab_map[1], slab_map[2])
    slab_facts = tuple(jnp.concatenate([x, x[:1] + jnp.zeros((pad,), x.dtype)]) for x in slab_facts)
    slab_starts = group_starts(slab_map[1])

    smem = pl.BlockSpec(memory_space=pltpu.SMEM)
    vmem = pl.BlockSpec(memory_space=pltpu.VMEM)
    hbm = pl.BlockSpec(memory_space=pltpu.HBM)
    out, right = pl.pallas_call(
        kernel,
        out_shape=(
            jax.ShapeDtypeStruct((rows, width), F32),
            jax.ShapeDtypeStruct((1, own), F32),
        ),
        in_specs=[smem] * 19 + [vmem] * 3 + [hbm],
        out_specs=(hbm, vmem),
        scratch_shapes=[
            pltpu.VMEM((BLOCKS * SLOT * 64, 128), F32),
            pltpu.VMEM((BLOCKS * 64, 128), F32),
            pltpu.VMEM((TOP * 2, 8, 128), F32),
            pltpu.VMEM((TOP * 2, 8, 128), F32),
            pltpu.VMEM(((rows // 8 + 1) * 64, 128), F32),
            pltpu.VMEM(((width // 8 + 1) * 64, 128), F32),
            pltpu.VMEM((OBS, width), BF16),
            pltpu.VMEM((OBS, width), BF16),
            pltpu.VMEM((2, CHUNK, width), F32),
            pltpu.VMEM((2, CHUNK, width), F32),
            pltpu.SemaphoreType.DMA((2,)),
            pltpu.SemaphoreType.DMA((2,)),
        ],
        compiler_params=pltpu.CompilerParams(vmem_limit_bytes=60 * 1024 * 1024),
        name="normal_update",
    )(
        col, starts, slab_starts, jnp.asarray(inverse_squares()),
        *facts, target, *slab_facts,
        params, jnp.asarray(diagonal_logs()), right_side.reshape(1, own), normal_slab,
    )
    return out, right.reshape(own)


def on_device(
    colatitude, longitude, radius_ratio, component, obs_weight, observed,
    unknown_map, slab_map, normal_slab, right_side,
):
    zeros = jnp.zeros_like(colatitude)
    local = jnp.stack(
        [colatitude, longitude, radius_ratio, component.astype(F32), obs_weight, observed, zeros, zeros]
    )
    params = lax.all_gather(local, "row", axis=0)
    params = params.transpose(1, 0, 2).reshape(8, PARTS, 128)
    rows = normal_slab.shape[0]
    unknowns = lax.dynamic_slice_in_dim(unknown_map, lax.axis_index("row") * rows, rows, axis=1)
    col = lax.axis_index("col").astype(jnp.int32).reshape(1)
    return local_update(params, col, unknowns, slab_map, normal_slab, right_side)


def solution(mesh):
    return jax.shard_map(
        on_device,
        mesh=mesh,
        in_specs=(
            P("row"), P("row"), P("row"), P("row"), P("row"), P("row"),
            P(), P(None, "col"), P("row", "col"), P(("row", "col")),
        ),
        out_specs=(P("row", "col"), P(("row", "col"))),
        check_vma=False,
    )
```

```python
import jax
import jax.numpy as jnp
import numpy as np
from jax import lax
from jax.experimental import pallas as pl
from jax.experimental.pallas import tpu as pltpu
from jax.sharding import PartitionSpec as P

NMAX = 300
TOP = 304
GROUP = 8
GROUPS = TOP // GROUP
STEP = 16
SLOT = STEP + 1
PITCH = 9
WIDE = 8 * PITCH
RING = 8
BUFS = 4
OBS = 1024
PARTS = 8
CHUNK = 256
DRAIN = 8
LATE = 1 << 20
BIG = float(2.0**64)
SMALL = float(2.0**-64)
LOG_BIG = float(64.0 * np.log(2.0))
F32 = jnp.float32
BF16 = jnp.bfloat16
I32 = jnp.int32


def blocks_of(group):
    return (NMAX + STEP - group * GROUP) // STEP


def diagonal_logs():
    counter = np.arange(1, TOP, dtype=np.float64)
    steps = 0.5 * np.log((2.0 * counter + 1.0) / (2.0 * counter))
    logs = np.concatenate([[0.0], 0.5 * np.log(2.0) + np.cumsum(steps)])
    return np.broadcast_to(logs[:, None], (TOP, 128)).astype(np.float32)


def block_scales():
    table = []
    for group in range(GROUPS):
        order = (group * GROUP + np.arange(GROUP, dtype=np.float64))[:, None]
        for block in range(blocks_of(group)):
            sigma = np.ones((GROUP, 1))
            if block > 0:
                degree = order + STEP * (block - 1) + np.arange(STEP)[None, :]
                ratio = (degree**2 - order**2) / (degree**2 - 0.25)
                if block == 1:
                    ratio[:, 0] = 1.0
                sigma = 1.0 / np.sqrt(np.prod(ratio, axis=1, keepdims=True))
            table.append(np.broadcast_to(sigma, (GROUP, 128)))
    table.append(np.ones((GROUP, 128)))
    return np.concatenate(table, axis=0).astype(np.float32)


def inverse_squares():
    degree = np.arange(TOP + 2 * STEP, dtype=np.float64)[:, None] - 1.0
    return np.broadcast_to(1.0 / (degree * degree - 0.25), (TOP + 2 * STEP, 128)).astype(np.float32)


BLOCKS = sum(blocks_of(group) for group in range(GROUPS))


def list_keys(unknowns, slab_map):
    rows = unknowns.shape[1]
    width = slab_map.shape[1]
    total = -(-(rows + width + 64) // 1024) * 1024
    degree = jnp.concatenate([unknowns[0], slab_map[0], jnp.full((total - rows - width,), 2, I32)])
    order = jnp.concatenate([unknowns[1], slab_map[1], jnp.zeros((total - rows - width,), I32)])
    kind = jnp.concatenate([unknowns[2], slab_map[2], jnp.full((total - rows - width,), 2, I32)])
    place = lax.broadcasted_iota(I32, (total,), 0)
    beyond = degree - order
    key = (
        (((order >> 3) - 32) << 26)
        | ((beyond >> 4) << 21)
        | ((beyond & 15) << 17)
        | ((order & 7) << 14)
        | (kind << 13)
        | place
    )
    return jnp.where(kind == 2, (31 << 26) | place, key)


def list_facts(key, limit):
    group = (key >> 26) + 32
    used = group < GROUPS
    group = jnp.where(used, group, 0)
    block = jnp.where(used, (key >> 21) & 31, 0)
    step = jnp.where(used, (key >> 17) & 15, 2)
    lane = jnp.where(used, (key >> 14) & 7, 0)
    kind = jnp.where(used, (key >> 13) & 1, 0)
    place = jnp.minimum(key & 8191, limit)
    order = group * GROUP + lane
    degree = order + block * STEP + step
    number = 19 * group - (((group - 1) * (group - 1)) >> 2) + block
    ring = number & (RING - 1)
    number = jnp.where(used, number, LATE)
    at_value = (ring * SLOT + 1 + step) * WIDE + lane
    at_scale = ring * WIDE + lane
    target = place * PITCH
    m = order.astype(F32)
    first = degree - step
    product = jnp.ones_like(m)
    for q in range(STEP):
        j = first + q
        jf = j.astype(F32)
        ratio = (jf * jf - m * m) / (jf * jf - 0.25)
        product = jnp.where((j > order) & (j <= degree), product * ratio, product)
    return number, at_value, at_scale, degree, order * 2 + kind, target, lax.rsqrt(product)


def gather_kernel(theta_ref, lon_ref, ratio_ref, comp_ref, weight_ref, seen_ref, key_ref, *rest):
    outs = rest[:7]
    params_ref, local, everyone, send_sem, recv_sem = rest[7:]
    me = lax.axis_index("row")
    count = everyone.shape[0]
    half = theta_ref.shape[0]
    barrier = pltpu.get_barrier_semaphore()
    for d in range(1, count):
        pl.semaphore_signal(
            barrier, inc=1, device_id={"row": lax.rem(me + d, count)}, device_id_type=pl.DeviceIdType.MESH
        )
    local[...] = jnp.zeros_like(local)
    for k, ref in enumerate((theta_ref, lon_ref, ratio_ref, comp_ref, weight_ref, seen_ref)):
        local[pl.ds(k, 1), pl.ds(0, half)] = ref[...].astype(F32).reshape(1, half)
    pl.semaphore_wait(barrier, count - 1)

    def send(d):
        return pltpu.make_async_remote_copy(
            src_ref=local, dst_ref=everyone.at[me], send_sem=send_sem.at[d], recv_sem=recv_sem.at[d],
            device_id={"row": lax.rem(me + d, count)}, device_id_type=pl.DeviceIdType.MESH,
        )

    def receive(d):
        return pltpu.make_async_remote_copy(
            src_ref=local, dst_ref=everyone.at[lax.rem(me + count - d, count)],
            send_sem=send_sem.at[d], recv_sem=recv_sem.at[d],
            device_id={"row": lax.rem(me + d, count)}, device_id_type=pl.DeviceIdType.MESH,
        )

    for d in range(1, count):
        send(d).start()
    everyone[me] = local[...]
    for ref, value in zip(outs, list_facts(key_ref[...], LIMIT)):
        ref[...] = value
    for d in range(1, count):
        receive(d).wait_recv()
    left = lax.broadcasted_iota(I32, (8, 128), 1) < half
    for c in range(PARTS):
        merged = jnp.where(left, everyone[2 * c], pltpu.roll(everyone[2 * c + 1], half, 1))
        params_ref[pl.ds(c, 8, stride=8), :] = merged
    for d in range(1, count):
        send(d).wait_send()


LIMIT = 6656


def kernel(
    col_ref, number_hbm, value_hbm, scale_hbm, radial_hbm, harm_hbm, target_hbm, grow_hbm,
    params_ref, table_hbm, inv_ref, logs_ref, right_ref, normal_ref,
    out_ref, right_out_ref,
    number_ref, value_ref, scale_ref, radial_ref, harm_ref, target_ref, grow_ref,
    value_buf, scale_buf, harm_buf, radial_buf, design_buf, seed_buf, level_buf, table_ref,
    slab_hi, slab_lo, in_buf, out_buf, list_sem, in_sem, out_sem,
):
    rows, width = normal_ref.shape
    chunks = rows // CHUNK

    lists = [
        pltpu.make_async_copy(src, dst, list_sem.at[k])
        for k, (src, dst) in enumerate(
            (
                (table_hbm, table_ref),
                (number_hbm, number_ref),
                (value_hbm, value_ref),
                (scale_hbm, scale_ref),
                (radial_hbm, radial_ref),
                (harm_hbm, harm_ref),
                (target_hbm, target_ref),
                (grow_hbm, grow_ref),
            )
        )
    ]
    for copy in lists:
        copy.start()

    def fetch(index, slot):
        return pltpu.make_async_copy(
            normal_ref.at[pl.ds(pl.multiple_of(index * CHUNK, CHUNK), CHUNK)], in_buf.at[slot], in_sem.at[slot]
        )

    def put(index, slot):
        return pltpu.make_async_copy(
            out_buf.at[slot], out_ref.at[pl.ds(pl.multiple_of(index * CHUNK, CHUNK), CHUNK)], out_sem.at[slot]
        )

    for k in range(BUFS):
        fetch(k, k).start()

    def param(k):
        return params_ref[pl.ds(8 * k, 8), :]

    theta = param(0)
    lon = param(1)
    cos_t = jnp.cos(theta)
    sin_t = jnp.sin(theta)
    log_s = jnp.log(sin_t)
    comp = param(3)
    weight = param(4)
    scaled = weight * param(5)
    part0 = jnp.where(comp == 2.0, 1.0, jnp.where(comp == 1.0, 0.0, -1.0))
    part1 = jnp.where(comp == 2.0, 0.0, jnp.where(comp == 1.0, 1.0, -1.0))
    part1q = part1 / (sin_t * sin_t)
    inv_r = 1.0 / param(2)

    def spread(values, c):
        return jnp.broadcast_to(values[c : c + 1, :], (8, 128))

    twice = [spread(2.0 * cos_t, c) for c in range(PARTS)]
    logs = [spread(log_s, c) for c in range(PARTS)]
    subf = lax.broadcasted_iota(I32, (8, 128), 0).astype(F32)

    c1 = jnp.cos(lon)
    s1 = jnp.sin(lon)
    cs = [jnp.ones_like(c1)]
    sn = [jnp.zeros_like(c1)]
    for _ in range(8):
        cs.append(cs[-1] * c1 - sn[-1] * s1)
        sn.append(sn[-1] * c1 + cs[-2] * s1)
    c8, s8 = cs[8], sn[8]
    powers = [inv_r * inv_r * inv_r]
    step_r = inv_r
    for _ in range(7):
        powers.append(powers[-1] * inv_r)
    for _ in range(3):
        step_r = step_r * step_r

    def fill(block, carry):
        cc, ss, pw = carry
        base = block * 8
        for j in range(8):
            nf = (base + j).astype(F32)
            square = nf * nf
            harm_buf[(base + j) * 4] = cc[j]
            harm_buf[(base + j) * 4 + 1] = cc[j] * square
            harm_buf[(base + j) * 4 + 2] = ss[j]
            harm_buf[(base + j) * 4 + 3] = ss[j] * square
            inv_d = 1.0 / ((nf + 1.0) * (nf + 2.0))
            g = pw[j] * part1q * inv_d
            u = (cos_t * g) * (2.0 / (2.0 * nf - 1.0))
            radial_buf[(base + j) * 4] = pw[j] * (part0 - part1 * ((2.0 * nf + 1.0) * inv_d)) + nf * g
            radial_buf[(base + j) * 4 + 1] = g
            radial_buf[(base + j) * 4 + 2] = u * square
            radial_buf[(base + j) * 4 + 3] = u
        orders = subf + base.astype(F32)
        diag = logs_ref[pl.ds(pl.multiple_of(base, 8), 8), :]
        before = -1.0 / (1.0 - (orders * orders - 0.25) * inv_ref[pl.ds(pl.multiple_of(base, 8), 8), :])
        for c in range(PARTS):
            log_seed = diag + orders * logs[c]
            level = jnp.minimum(jnp.ceil(log_seed * (1.0 / LOG_BIG)), 0.0)
            at = pl.multiple_of(block * 64, 64) + c * 8
            seed_buf[pl.ds(at, 8), :] = jnp.exp(log_seed - level * LOG_BIG) * before
            level_buf[pl.ds(at, 8), :] = level * 64.0
        return (
            tuple(cc[j] * c8 - ss[j] * s8 for j in range(8)),
            tuple(ss[j] * c8 + cc[j] * s8 for j in range(8)),
            tuple(pw[j] * step_r for j in range(8)),
        )

    lax.fori_loop(0, GROUPS, fill, (tuple(cs[:8]), tuple(sn[:8]), tuple(powers)))

    for copy in lists:
        copy.wait()

    def make_row(j):
        at = value_ref[j]
        now = value_buf[pl.ds(at, 8, stride=PITCH), :]
        past = value_buf[pl.ds(at - WIDE, 8, stride=PITCH), :]
        scale = scale_buf[pl.ds(scale_ref[j], 8, stride=PITCH), :]
        n = radial_ref[j] * 4
        h = harm_ref[j] * 2
        body = harm_buf[h] * (now * radial_buf[n] - past * radial_buf[n + 2]) - harm_buf[h + 1] * (
            now * radial_buf[n + 1] - past * radial_buf[n + 3]
        )
        design_buf[pl.ds(target_ref[j], 8), :] = body * (scale * grow_ref[j])

    def drain(cursor, number):
        def more(at):
            return number_ref[at] <= number

        def piece(at):
            for u in range(DRAIN):
                make_row(at + u)
            kept = at + 0
            for u in range(DRAIN):
                kept = kept + (number_ref[at + u] <= number).astype(I32)
            return kept

        return lax.while_loop(more, piece, cursor)

    def group_body(group, carry):
        cursor, number = carry
        zero = jnp.zeros((8, 128), F32)
        orders = subf + (group * GROUP).astype(F32)
        squares = orders * orders - 0.25
        at = pl.multiple_of(group * 64, 64)
        one = tuple(zero for _ in range(PARTS))
        two = tuple(seed_buf[pl.ds(at + c * 8, 8), :] for c in range(PARTS))
        levels = tuple(level_buf[pl.ds(at + c * 8, 8), :] for c in range(PARTS))

        def factors(number):
            sigma = table_ref[pl.ds(pl.multiple_of(number * 8, 8), 8), :]
            return sigma, sigma * SMALL, 64.0 / sigma

        def block_body(block, carry):
            one, two, levels, (sigma, sigma_small, limit), cursor, number = carry
            one, two, levels = list(one), list(two), list(levels)
            cursor = drain(cursor, number - RING)
            ring = number & (RING - 1)
            first = pl.multiple_of(group * GROUP + block * STEP, 8)
            at_scale = ring * WIDE
            at_value = ring * (SLOT * WIDE)
            for c in range(PARTS):
                big = jnp.abs(one[c]) > limit
                factor = jnp.where(big, sigma_small, sigma)
                one[c] = one[c] * factor
                two[c] = two[c] * factor
                levels[c] = levels[c] + jnp.where(big, 64.0, 0.0)
                scale_buf[pl.ds(at_scale + c * PITCH, 8), :] = jnp.exp2(levels[c])
                value_buf[pl.ds(at_value + c * PITCH, 8), :] = one[c]
            for i in range(STEP):
                make_row(cursor + i)
                rho = 1.0 - squares * inv_ref[pl.ds(first + i, 8), :]
                fresh = [twice[c] * one[c] - rho * two[c] for c in range(PARTS)]
                for c in range(PARTS):
                    value_buf[pl.ds(at_value + (1 + i) * WIDE + c * PITCH, 8), :] = fresh[c]
                one, two = fresh, one
            done = jnp.int32(0)
            for half in (8, 4, 2, 1):
                done = done + jnp.where(number_ref[cursor + done + (half - 1)] < number, half, 0)
            done = done + (number_ref[cursor + done] < number).astype(I32)
            cursor = cursor + jnp.minimum(done, STEP)
            return tuple(one), tuple(two), tuple(levels), factors(number + 1), cursor, number + 1

        blocks = (NMAX + STEP - group * GROUP) // STEP
        out = lax.fori_loop(0, blocks, block_body, (one, two, levels, factors(number), cursor, number))
        return out[4], out[5]

    cursor, _ = lax.fori_loop(0, GROUPS, group_body, (jnp.int32(0), jnp.int32(0)))
    cursor = drain(cursor, BLOCKS)

    def clear(j, _):
        design_buf[pl.ds(target_ref[j], 8), :] = jnp.zeros((8, 128), F32)
        return 0

    lax.fori_loop(cursor, rows + width, clear, 0)

    def entries(first, count, c):
        return design_buf[pl.ds(first * PITCH + c, count, stride=PITCH), :]

    for c in range(PARTS):
        for half in range(width // 256):
            block = entries(rows + half * 256, 256, c)
            block = (block * weight[c : c + 1, :]).T
            hi = block.astype(BF16)
            slab_hi[pl.ds(c * 128, 128), pl.ds(half * 256, 256)] = hi
            slab_lo[pl.ds(c * 128, 128), pl.ds(half * 256, 256)] = (block - hi.astype(F32)).astype(BF16)

    own = right_ref.shape[0]
    total = jnp.zeros((own, 128), F32)
    at = col_ref[0] * own
    for c in range(PARTS):
        total = total + entries(at, own, c) * scaled[c : c + 1, :]
    summed = lax.dot_general(
        jnp.ones((8, 128), F32), total, (((1,), (1,)), ((), ())),
        precision=lax.Precision.HIGHEST, preferred_element_type=F32,
    )
    right_out_ref[...] = right_ref[...] + summed[0:1, :].reshape(own)

    def chunk_body(index, _):
        slot = lax.rem(index, BUFS)
        his = []
        los = []
        for c in range(PARTS):
            x = entries(index * CHUNK, CHUNK, c)
            hi = x.astype(BF16)
            his.append(hi)
            los.append((x - hi.astype(F32)).astype(BF16))
        hi = jnp.concatenate(his, axis=1)
        lo = jnp.concatenate(los, axis=1)
        update = jnp.dot(hi, slab_hi[...], preferred_element_type=F32)
        update += jnp.dot(hi, slab_lo[...], preferred_element_type=F32)
        update += jnp.dot(lo, slab_hi[...], preferred_element_type=F32)
        fetch(index, slot).wait()

        @pl.when(index >= BUFS)
        def _():
            put(index - BUFS, slot).wait()

        out_buf[slot] = in_buf[slot] + update
        put(index, slot).start()

        @pl.when(index + BUFS < chunks)
        def _():
            fetch(index + BUFS, slot).start()

        return 0

    lax.fori_loop(0, chunks, chunk_body, 0)
    for k in range(BUFS):
        put(chunks - BUFS + k, k).wait()


def local_update(params, col, facts, normal_slab, right_side):
    rows, width = normal_slab.shape
    own = right_side.shape[0]
    entries = facts[0].shape[0]
    smem = pl.BlockSpec(memory_space=pltpu.SMEM)
    vmem = pl.BlockSpec(memory_space=pltpu.VMEM)
    hbm = pl.BlockSpec(memory_space=pltpu.HBM)
    return pl.pallas_call(
        kernel,
        out_shape=(
            jax.ShapeDtypeStruct((rows, width), F32),
            jax.ShapeDtypeStruct((own,), F32),
        ),
        in_specs=[smem] + [hbm] * 7 + [vmem, hbm, vmem, vmem, vmem, hbm],
        out_specs=(hbm, vmem),
        scratch_shapes=[pltpu.SMEM((entries,), I32)] * 6
        + [pltpu.SMEM((entries,), F32)]
        + [
            pltpu.VMEM((RING * SLOT * WIDE, 128), F32),
            pltpu.VMEM((RING * WIDE, 128), F32),
            pltpu.VMEM((TOP * 4, 8, 128), F32),
            pltpu.VMEM((TOP * 4, 8, 128), F32),
            pltpu.VMEM(((rows + width + 1) * PITCH, 128), F32),
            pltpu.VMEM((GROUPS * 64, 128), F32),
            pltpu.VMEM((GROUPS * 64, 128), F32),
            pltpu.VMEM((BLOCKS * 8 + 8, 128), F32),
            pltpu.VMEM((OBS, width), BF16),
            pltpu.VMEM((OBS, width), BF16),
            pltpu.VMEM((BUFS, CHUNK, width), F32),
            pltpu.VMEM((BUFS, CHUNK, width), F32),
            pltpu.SemaphoreType.DMA((8,)),
            pltpu.SemaphoreType.DMA((BUFS,)),
            pltpu.SemaphoreType.DMA((BUFS,)),
        ],
        compiler_params=pltpu.CompilerParams(vmem_limit_bytes=62 * 1024 * 1024),
        name="normal_update",
    )(
        col, *facts, params, jnp.asarray(block_scales()), jnp.asarray(inverse_squares()),
        jnp.asarray(diagonal_logs()), right_side, normal_slab,
    )


def on_device(
    colatitude, longitude, radius_ratio, component, obs_weight, observed,
    unknown_map, slab_map, normal_slab, right_side,
):
    rows, width = normal_slab.shape
    unknowns = lax.dynamic_slice_in_dim(unknown_map, lax.axis_index("row") * rows, rows, axis=1)
    col = lax.axis_index("col").astype(I32).reshape(1)
    key = lax.sort(list_keys(unknowns, slab_map), is_stable=False)
    entries = key.shape[0]
    shape = (entries // 128, 128)
    count = lax.axis_size("row")
    vmem = pl.BlockSpec(memory_space=pltpu.VMEM)
    outs = pl.pallas_call(
        gather_kernel,
        out_shape=tuple(jax.ShapeDtypeStruct(shape, I32) for _ in range(6))
        + (jax.ShapeDtypeStruct(shape, F32), jax.ShapeDtypeStruct((64, 128), F32)),
        in_specs=[vmem] * 7,
        out_specs=(vmem,) * 8,
        scratch_shapes=[
            pltpu.VMEM((8, 128), F32),
            pltpu.VMEM((count, 8, 128), F32),
            pltpu.SemaphoreType.DMA((count,)),
            pltpu.SemaphoreType.DMA((count,)),
        ],
        compiler_params=pltpu.CompilerParams(collective_id=0, has_side_effects=True),
        name="gather_observations",
    )(colatitude, longitude, radius_ratio, component, obs_weight, observed, key.reshape(shape))
    facts = tuple(x.reshape(entries) for x in outs[:7])
    return local_update(outs[7], col, facts, normal_slab, right_side)


def solution(mesh):
    return jax.shard_map(
        on_device,
        mesh=mesh,
        in_specs=(
            P("row"), P("row"), P("row"), P("row"), P("row"), P("row"),
            P(), P(None, "col"), P("row", "col"), P(("row", "col")),
        ),
        out_specs=(P("row", "col"), P(("row", "col"))),
        check_vma=False,
    )
```

```python
import jax
import jax.numpy as jnp
import numpy as np
from jax import lax
from jax.experimental import pallas as pl
from jax.experimental.pallas import tpu as pltpu
from jax.sharding import PartitionSpec as P

NMAX = 300
TOP = 304
GROUP = 8
GROUPS = TOP // GROUP
STEP = 16
SLOT = STEP + 1
PITCH = 9
WIDE = 8 * PITCH
RING = 8
BUFS = 2
OBS = 1024
PARTS = 8
CHUNK = 512
PACE = 16
DRAIN = 8
LATE = 1 << 20
BIG = float(2.0**64)
SMALL = float(2.0**-64)
LOG_BIG = float(64.0 * np.log(2.0))
F32 = jnp.float32
BF16 = jnp.bfloat16
I32 = jnp.int32


def blocks_of(group):
    return (NMAX + STEP - group * GROUP) // STEP


def diagonal_logs():
    counter = np.arange(1, TOP, dtype=np.float64)
    steps = 0.5 * np.log((2.0 * counter + 1.0) / (2.0 * counter))
    logs = np.concatenate([[0.0], 0.5 * np.log(2.0) + np.cumsum(steps)])
    return np.broadcast_to(logs[:, None], (TOP, 128)).astype(np.float32)


def block_scales():
    table = []
    for group in range(GROUPS):
        order = (group * GROUP + np.arange(GROUP, dtype=np.float64))[:, None]
        for block in range(blocks_of(group)):
            sigma = np.ones((GROUP, 1))
            if block > 0:
                degree = order + STEP * (block - 1) + np.arange(STEP)[None, :]
                ratio = (degree**2 - order**2) / (degree**2 - 0.25)
                if block == 1:
                    ratio[:, 0] = 1.0
                sigma = 1.0 / np.sqrt(np.prod(ratio, axis=1, keepdims=True))
            table.append(np.broadcast_to(sigma, (GROUP, 128)))
    table.append(np.ones((GROUP, 128)))
    return np.concatenate(table, axis=0).astype(np.float32)


def inverse_squares():
    degree = np.arange(TOP + 2 * STEP, dtype=np.float64)[:, None] - 1.0
    return np.broadcast_to(1.0 / (degree * degree - 0.25), (TOP + 2 * STEP, 128)).astype(np.float32)


BLOCKS = sum(blocks_of(group) for group in range(GROUPS))


def row_key(degree, order, kind, place):
    beyond = degree - order
    key = (
        (((order >> 3) - 32) << 26)
        | ((beyond >> 4) << 21)
        | ((beyond & 15) << 17)
        | ((order & 7) << 14)
        | (kind << 13)
        | place
    )
    return jnp.where(kind == 2, (31 << 26) | place, key)


def sort_keys(key):
    height = key.shape[0]
    total = height * 128
    row = lax.broadcasted_iota(I32, key.shape, 0)
    lane = lax.broadcasted_iota(I32, key.shape, 1)
    index = row * 128 + lane
    size = 2
    while size <= total:
        rising = (index & size) == 0
        stride = size // 2
        while stride >= 1:
            low = (index & stride) == 0
            if stride < 128:
                ahead, behind = pltpu.roll(key, 128 - stride, 1), pltpu.roll(key, stride, 1)
            else:
                ahead, behind = pltpu.roll(key, height - stride // 128, 0), pltpu.roll(key, stride // 128, 0)
            other = jnp.where(low, ahead, behind)
            key = jnp.where(low == rising, jnp.minimum(key, other), jnp.maximum(key, other))
            stride //= 2
        size *= 2
    return key


def list_facts(key, limit):
    group = (key >> 26) + 32
    used = group < GROUPS
    group = jnp.where(used, group, 0)
    block = jnp.where(used, (key >> 21) & 31, 0)
    step = jnp.where(used, (key >> 17) & 15, 2)
    lane = jnp.where(used, (key >> 14) & 7, 0)
    kind = jnp.where(used, (key >> 13) & 1, 0)
    place = jnp.minimum(key & 8191, limit)
    order = group * GROUP + lane
    degree = order + block * STEP + step
    number = 19 * group - (((group - 1) * (group - 1)) >> 2) + block
    ring = number & (RING - 1)
    number = jnp.where(used, number, LATE)
    at_value = (ring * SLOT + 1 + step) * WIDE + lane
    at_scale = ring * WIDE + lane
    target = place * PITCH
    m = order.astype(F32)
    first = degree - step
    product = jnp.ones_like(m)
    for q in range(STEP):
        j = first + q
        jf = j.astype(F32)
        ratio = (jf * jf - m * m) / (jf * jf - 0.25)
        product = jnp.where((j > order) & (j <= degree), product * ratio, product)
    places = (at_value << 16) | target
    factors = (degree << 18) | ((order * 2 + kind) * 2)
    return number, at_scale, places, factors, lax.rsqrt(product)


def gather_kernel(
    theta_ref, lon_ref, ratio_ref, comp_ref, weight_ref, seen_ref, unknown_ref, slab_ref,
    number_ref, scale_ref, places_ref, factors_ref, grow_ref, params_ref,
    local, everyone, map_buf, key_buf, send_sem, recv_sem, map_sem,
):
    me = lax.axis_index("row")
    count = everyone.shape[0]
    half = theta_ref.shape[0]
    rows = map_buf.shape[1]
    width = slab_ref.shape[1]
    read_map = pltpu.make_async_copy(
        unknown_ref.at[:, pl.ds(pl.multiple_of(me * rows, 128), rows)], map_buf, map_sem.at[0]
    )
    read_map.start()
    barrier = pltpu.get_barrier_semaphore()
    for d in range(1, count):
        pl.semaphore_signal(
            barrier, inc=1, device_id={"row": lax.rem(me + d, count)}, device_id_type=pl.DeviceIdType.MESH
        )
    local[...] = jnp.zeros_like(local)
    for k, ref in enumerate((theta_ref, lon_ref, ratio_ref, comp_ref, weight_ref, seen_ref)):
        local[pl.ds(k, 1), pl.ds(0, half)] = ref[...].astype(F32).reshape(1, half)
    pl.semaphore_wait(barrier, count - 1)

    def send(d):
        return pltpu.make_async_remote_copy(
            src_ref=local, dst_ref=everyone.at[me], send_sem=send_sem.at[d], recv_sem=recv_sem.at[d],
            device_id={"row": lax.rem(me + d, count)}, device_id_type=pl.DeviceIdType.MESH,
        )

    def receive(d):
        return pltpu.make_async_remote_copy(
            src_ref=local, dst_ref=everyone.at[lax.rem(me + count - d, count)],
            send_sem=send_sem.at[d], recv_sem=recv_sem.at[d],
            device_id={"row": lax.rem(me + d, count)}, device_id_type=pl.DeviceIdType.MESH,
        )

    for d in range(1, count):
        send(d).start()
    everyone[me] = local[...]
    read_map.wait()
    lanes = lax.broadcasted_iota(I32, (1, 128), 1)
    for t in range((rows + width) // 128):
        ref, at = (map_buf, t * 128) if t * 128 < rows else (slab_ref, t * 128 - rows)
        part = [ref[pl.ds(k, 1), pl.ds(at, 128)] for k in range(3)]
        key_buf[pl.ds(t, 1), :] = row_key(part[0], part[1], part[2], lanes + t * 128)
    place = lax.broadcasted_iota(I32, key_buf.shape, 0) * 128 + lax.broadcasted_iota(I32, key_buf.shape, 1)
    key = sort_keys(jnp.where(place < rows + width, key_buf[...], (31 << 26) | place))
    facts = list_facts(key[: number_ref.shape[0]], rows + width)
    for ref, value in zip((number_ref, scale_ref, places_ref, factors_ref, grow_ref), facts):
        ref[...] = value
    for d in range(1, count):
        receive(d).wait_recv()
    left = lax.broadcasted_iota(I32, (8, 128), 1) < half
    for c in range(PARTS):
        merged = jnp.where(left, everyone[2 * c], pltpu.roll(everyone[2 * c + 1], half, 1))
        params_ref[pl.ds(c, 8, stride=8), :] = merged
    for d in range(1, count):
        send(d).wait_send()


def kernel(
    col_ref, number_hbm, scale_hbm, places_hbm, factors_hbm, grow_hbm,
    params_ref, table_hbm, inv_ref, logs_ref, right_ref, normal_ref,
    out_ref, right_out_ref,
    number_ref, scale_ref, places_ref, factors_ref, grow_ref,
    value_buf, scale_buf, harm_buf, radial_buf, design_buf, seed_buf, level_buf, table_ref,
    slab_hi, slab_lo, in_buf, out_buf, list_sem, in_sem, out_sem,
):
    rows, width = normal_ref.shape
    chunks = rows // CHUNK

    lists = [
        pltpu.make_async_copy(src, dst, list_sem.at[k])
        for k, (src, dst) in enumerate(
            (
                (table_hbm, table_ref),
                (number_hbm, number_ref),
                (scale_hbm, scale_ref),
                (places_hbm, places_ref),
                (factors_hbm, factors_ref),
                (grow_hbm, grow_ref),
            )
        )
    ]
    for copy in lists:
        copy.start()

    def fetch(index, slot):
        return pltpu.make_async_copy(
            normal_ref.at[pl.ds(pl.multiple_of(index * CHUNK, CHUNK), CHUNK)], in_buf.at[slot], in_sem.at[slot]
        )

    def put(index, slot):
        return pltpu.make_async_copy(
            out_buf.at[slot], out_ref.at[pl.ds(pl.multiple_of(index * CHUNK, CHUNK), CHUNK)], out_sem.at[slot]
        )

    for k in range(BUFS):
        fetch(k, k).start()

    def param(k):
        return params_ref[pl.ds(8 * k, 8), :]

    theta = param(0)
    lon = param(1)
    cos_t = jnp.cos(theta)
    sin_t = jnp.sin(theta)
    log_s = jnp.log(sin_t)
    comp = param(3)
    weight = param(4)
    scaled = weight * param(5)
    part0 = jnp.where(comp == 2.0, 1.0, jnp.where(comp == 1.0, 0.0, -1.0))
    part1 = jnp.where(comp == 2.0, 0.0, jnp.where(comp == 1.0, 1.0, -1.0))
    part1q = part1 / (sin_t * sin_t)
    inv_r = 1.0 / param(2)

    def spread(values, c):
        return jnp.broadcast_to(values[c : c + 1, :], (8, 128))

    twice = [spread(2.0 * cos_t, c) for c in range(PARTS)]
    logs = [spread(log_s, c) for c in range(PARTS)]
    subf = lax.broadcasted_iota(I32, (8, 128), 0).astype(F32)

    c1 = jnp.cos(lon)
    s1 = jnp.sin(lon)
    cs = [jnp.ones_like(c1)]
    sn = [jnp.zeros_like(c1)]
    for _ in range(8):
        cs.append(cs[-1] * c1 - sn[-1] * s1)
        sn.append(sn[-1] * c1 + cs[-2] * s1)
    c8, s8 = cs[8], sn[8]
    powers = [inv_r * inv_r * inv_r]
    step_r = inv_r
    for _ in range(7):
        powers.append(powers[-1] * inv_r)
    for _ in range(3):
        step_r = step_r * step_r

    def fill(block, carry):
        cc, ss, pw = carry
        base = block * 8
        for j in range(8):
            nf = (base + j).astype(F32)
            square = nf * nf
            harm_buf[(base + j) * 4] = cc[j]
            harm_buf[(base + j) * 4 + 1] = cc[j] * square
            harm_buf[(base + j) * 4 + 2] = ss[j]
            harm_buf[(base + j) * 4 + 3] = ss[j] * square
            inv_d = 1.0 / ((nf + 1.0) * (nf + 2.0))
            g = pw[j] * part1q * inv_d
            u = (cos_t * g) * (2.0 / (2.0 * nf - 1.0))
            radial_buf[(base + j) * 4] = pw[j] * (part0 - part1 * ((2.0 * nf + 1.0) * inv_d)) + nf * g
            radial_buf[(base + j) * 4 + 1] = g
            radial_buf[(base + j) * 4 + 2] = u * square
            radial_buf[(base + j) * 4 + 3] = u
        orders = subf + base.astype(F32)
        diag = logs_ref[pl.ds(pl.multiple_of(base, 8), 8), :]
        before = -1.0 / (1.0 - (orders * orders - 0.25) * inv_ref[pl.ds(pl.multiple_of(base, 8), 8), :])
        for c in range(PARTS):
            log_seed = diag + orders * logs[c]
            level = jnp.minimum(jnp.ceil(log_seed * (1.0 / LOG_BIG)), 0.0)
            at = pl.multiple_of(block * 64, 64) + c * 8
            seed_buf[pl.ds(at, 8), :] = jnp.exp(log_seed - level * LOG_BIG) * before
            level_buf[pl.ds(at, 8), :] = level * 64.0
        return (
            tuple(cc[j] * c8 - ss[j] * s8 for j in range(8)),
            tuple(ss[j] * c8 + cc[j] * s8 for j in range(8)),
            tuple(pw[j] * step_r for j in range(8)),
        )

    lax.fori_loop(0, GROUPS, fill, (tuple(cs[:8]), tuple(sn[:8]), tuple(powers)))

    for copy in lists:
        copy.wait()

    def make_row(j):
        places = places_ref[j]
        factors = factors_ref[j]
        at = places >> 16
        now = value_buf[pl.ds(at, 8, stride=PITCH), :]
        past = value_buf[pl.ds(at - WIDE, 8, stride=PITCH), :]
        scale = scale_buf[pl.ds(scale_ref[j], 8, stride=PITCH), :]
        n = factors >> 16
        h = factors & 65535
        body = harm_buf[h] * (now * radial_buf[n] - past * radial_buf[n + 2]) - harm_buf[h + 1] * (
            now * radial_buf[n + 1] - past * radial_buf[n + 3]
        )
        design_buf[pl.ds(places & 65535, 8), :] = body * (scale * grow_ref[j])

    def drain(cursor, number):
        def more(at):
            return number_ref[at] <= number

        def piece(at):
            for u in range(DRAIN):
                make_row(at + u)
            kept = at + 0
            for u in range(DRAIN):
                kept = kept + (number_ref[at + u] <= number).astype(I32)
            return kept

        return lax.while_loop(more, piece, cursor)

    def group_body(group, carry):
        cursor, number = carry
        zero = jnp.zeros((8, 128), F32)
        orders = subf + (group * GROUP).astype(F32)
        squares = orders * orders - 0.25
        at = pl.multiple_of(group * 64, 64)
        one = tuple(zero for _ in range(PARTS))
        two = tuple(seed_buf[pl.ds(at + c * 8, 8), :] for c in range(PARTS))
        levels = tuple(level_buf[pl.ds(at + c * 8, 8), :] for c in range(PARTS))

        def factors(number):
            sigma = table_ref[pl.ds(pl.multiple_of(number * 8, 8), 8), :]
            return sigma, sigma * SMALL, 64.0 / sigma

        def block_body(block, carry):
            one, two, levels, (sigma, sigma_small, limit), cursor, number = carry
            one, two, levels = list(one), list(two), list(levels)
            cursor = drain(cursor, number - RING)
            ring = number & (RING - 1)
            first = pl.multiple_of(group * GROUP + block * STEP, 8)
            at_scale = ring * WIDE
            at_value = ring * (SLOT * WIDE)
            for c in range(PARTS):
                big = jnp.abs(one[c]) > limit
                factor = jnp.where(big, sigma_small, sigma)
                one[c] = one[c] * factor
                two[c] = two[c] * factor
                levels[c] = levels[c] + jnp.where(big, 64.0, 0.0)
                scale_buf[pl.ds(at_scale + c * PITCH, 8), :] = jnp.exp2(levels[c])
                value_buf[pl.ds(at_value + c * PITCH, 8), :] = one[c]
            for i in range(STEP):
                for k in range(i * PACE // STEP, (i + 1) * PACE // STEP):
                    make_row(cursor + k)
                rho = 1.0 - squares * inv_ref[pl.ds(first + i, 8), :]
                fresh = [twice[c] * one[c] - rho * two[c] for c in range(PARTS)]
                for c in range(PARTS):
                    value_buf[pl.ds(at_value + (1 + i) * WIDE + c * PITCH, 8), :] = fresh[c]
                one, two = fresh, one
            done = jnp.int32(0)
            for half in (8, 4, 2, 1, 1):
                done = done + jnp.where(number_ref[cursor + done + (half - 1)] < number, half, 0)
            cursor = cursor + jnp.minimum(done, PACE)
            return tuple(one), tuple(two), tuple(levels), factors(number + 1), cursor, number + 1

        blocks = (NMAX + STEP - group * GROUP) // STEP
        out = lax.fori_loop(0, blocks, block_body, (one, two, levels, factors(number), cursor, number))
        return out[4], out[5]

    cursor, _ = lax.fori_loop(0, GROUPS, group_body, (jnp.int32(0), jnp.int32(0)))
    cursor = drain(cursor, BLOCKS)

    def clear(j, _):
        design_buf[pl.ds(places_ref[j] & 65535, 8), :] = jnp.zeros((8, 128), F32)
        return 0

    lax.fori_loop(cursor, rows + width, clear, 0)

    def entries(first, count, c):
        return design_buf[pl.ds(first * PITCH + c, count, stride=PITCH), :]

    for c in range(PARTS):
        for half in range(width // 256):
            block = entries(rows + half * 256, 256, c)
            block = (block * weight[c : c + 1, :]).T
            hi = block.astype(BF16)
            slab_hi[pl.ds(c * 128, 128), pl.ds(half * 256, 256)] = hi
            slab_lo[pl.ds(c * 128, 128), pl.ds(half * 256, 256)] = (block - hi.astype(F32)).astype(BF16)

    own = right_ref.shape[0]
    total = jnp.zeros((own, 128), F32)
    at = col_ref[0] * own
    for c in range(PARTS):
        total = total + entries(at, own, c) * scaled[c : c + 1, :]
    summed = lax.dot_general(
        jnp.ones((8, 128), F32), total, (((1,), (1,)), ((), ())),
        precision=lax.Precision.HIGHEST, preferred_element_type=F32,
    )
    right_out_ref[...] = right_ref[...] + summed[0:1, :].reshape(own)

    def chunk_body(index, _):
        slot = lax.rem(index, BUFS)
        his = []
        los = []
        for c in range(PARTS):
            x = entries(index * CHUNK, CHUNK, c)
            hi = x.astype(BF16)
            his.append(hi)
            los.append((x - hi.astype(F32)).astype(BF16))
        hi = jnp.concatenate(his, axis=1)
        lo = jnp.concatenate(los, axis=1)
        update = jnp.dot(hi, slab_hi[...], preferred_element_type=F32)
        update += jnp.dot(hi, slab_lo[...], preferred_element_type=F32)
        update += jnp.dot(lo, slab_hi[...], preferred_element_type=F32)
        fetch(index, slot).wait()

        @pl.when(index >= BUFS)
        def _():
            put(index - BUFS, slot).wait()

        out_buf[slot] = in_buf[slot] + update
        put(index, slot).start()

        @pl.when(index + BUFS < chunks)
        def _():
            fetch(index + BUFS, slot).start()

        return 0

    lax.fori_loop(0, chunks, chunk_body, 0)
    for k in range(BUFS):
        put(chunks - BUFS + k, k).wait()


def local_update(params, col, facts, normal_slab, right_side):
    rows, width = normal_slab.shape
    own = right_side.shape[0]
    entries = facts[0].shape[0]
    smem = pl.BlockSpec(memory_space=pltpu.SMEM)
    vmem = pl.BlockSpec(memory_space=pltpu.VMEM)
    hbm = pl.BlockSpec(memory_space=pltpu.HBM)
    return pl.pallas_call(
        kernel,
        out_shape=(
            jax.ShapeDtypeStruct((rows, width), F32),
            jax.ShapeDtypeStruct((own,), F32),
        ),
        in_specs=[smem] + [hbm] * 5 + [vmem, hbm, vmem, vmem, vmem, hbm],
        out_specs=(hbm, vmem),
        scratch_shapes=[pltpu.SMEM((entries,), I32)] * 4
        + [pltpu.SMEM((entries,), F32)]
        + [
            pltpu.VMEM((RING * SLOT * WIDE, 128), F32),
            pltpu.VMEM((RING * WIDE, 128), F32),
            pltpu.VMEM((TOP * 4, 8, 128), F32),
            pltpu.VMEM((TOP * 4, 8, 128), F32),
            pltpu.VMEM(((rows + width + 1) * PITCH, 128), F32),
            pltpu.VMEM((GROUPS * 64, 128), F32),
            pltpu.VMEM((GROUPS * 64, 128), F32),
            pltpu.VMEM((BLOCKS * 8 + 8, 128), F32),
            pltpu.VMEM((OBS, width), BF16),
            pltpu.VMEM((OBS, width), BF16),
            pltpu.VMEM((BUFS, CHUNK, width), F32),
            pltpu.VMEM((BUFS, CHUNK, width), F32),
            pltpu.SemaphoreType.DMA((6,)),
            pltpu.SemaphoreType.DMA((BUFS,)),
            pltpu.SemaphoreType.DMA((BUFS,)),
        ],
        compiler_params=pltpu.CompilerParams(vmem_limit_bytes=62 * 1024 * 1024),
        name="normal_update",
    )(
        col, *facts, params, jnp.asarray(block_scales()), jnp.asarray(inverse_squares()),
        jnp.asarray(diagonal_logs()), right_side, normal_slab,
    )


def on_device(
    colatitude, longitude, radius_ratio, component, obs_weight, observed,
    unknown_map, slab_map, normal_slab, right_side,
):
    rows, width = normal_slab.shape
    col = lax.axis_index("col").astype(I32).reshape(1)
    entries = -(-(rows + width + 2 * PACE) // 1024) * 1024
    total = 1 << (rows + width - 1).bit_length()
    shape = (entries // 128, 128)
    count = lax.axis_size("row")
    vmem = pl.BlockSpec(memory_space=pltpu.VMEM)
    outs = pl.pallas_call(
        gather_kernel,
        out_shape=tuple(jax.ShapeDtypeStruct(shape, I32) for _ in range(4))
        + (jax.ShapeDtypeStruct(shape, F32), jax.ShapeDtypeStruct((64, 128), F32)),
        in_specs=[vmem] * 6 + [pl.BlockSpec(memory_space=pltpu.HBM), vmem],
        out_specs=(vmem,) * 6,
        scratch_shapes=[
            pltpu.VMEM((8, 128), F32),
            pltpu.VMEM((count, 8, 128), F32),
            pltpu.VMEM((3, rows), I32),
            pltpu.VMEM((total // 128, 128), I32),
            pltpu.SemaphoreType.DMA((count,)),
            pltpu.SemaphoreType.DMA((count,)),
            pltpu.SemaphoreType.DMA((1,)),
        ],
        compiler_params=pltpu.CompilerParams(collective_id=0, has_side_effects=True),
        name="gather_observations",
    )(colatitude, longitude, radius_ratio, component, obs_weight, observed, unknown_map, slab_map)
    facts = tuple(x.reshape(entries) for x in outs[:5])
    return local_update(outs[5], col, facts, normal_slab, right_side)


def solution(mesh):
    return jax.shard_map(
        on_device,
        mesh=mesh,
        in_specs=(
            P("row"), P("row"), P("row"), P("row"), P("row"), P("row"),
            P(), P(None, "col"), P("row", "col"), P(("row", "col")),
        ),
        out_specs=(P("row", "col"), P(("row", "col"))),
        check_vma=False,
    )
```

```python
import jax
import jax.numpy as jnp
import numpy as np
from jax import lax
from jax.experimental import pallas as pl
from jax.experimental.pallas import tpu as pltpu
from jax.sharding import PartitionSpec as P

NMAX = 300
TOP = 304
GROUP = 8
GROUPS = TOP // GROUP
STEP = 16
SLOT = STEP + 1
PITCH = 9
WIDE = 8 * PITCH
RING = 8
BUFS = 2
OBS = 1024
PARTS = 8
CHUNK = 768
PACE = 16
BATCH = 2
DRAIN = 16
LATE = 1 << 20
BIG = float(2.0**64)
SMALL = float(2.0**-64)
LOG_BIG = float(64.0 * np.log(2.0))
F32 = jnp.float32
BF16 = jnp.bfloat16
F8 = jnp.float8_e4m3fn
I32 = jnp.int32


def blocks_of(group):
    return (NMAX + STEP - group * GROUP) // STEP


def diagonal_logs():
    counter = np.arange(1, TOP, dtype=np.float64)
    steps = 0.5 * np.log((2.0 * counter + 1.0) / (2.0 * counter))
    logs = np.concatenate([[0.0], 0.5 * np.log(2.0) + np.cumsum(steps)])
    return np.broadcast_to(logs[:, None], (TOP, 128)).astype(np.float32)


def block_scales():
    table = []
    for group in range(GROUPS):
        order = (group * GROUP + np.arange(GROUP, dtype=np.float64))[:, None]
        for block in range(blocks_of(group)):
            sigma = np.ones((GROUP, 1))
            if block > 0:
                degree = order + STEP * (block - 1) + np.arange(STEP)[None, :]
                ratio = (degree**2 - order**2) / (degree**2 - 0.25)
                if block == 1:
                    ratio[:, 0] = 1.0
                sigma = 1.0 / np.sqrt(np.prod(ratio, axis=1, keepdims=True))
            table.append(np.broadcast_to(sigma, (GROUP, 128)))
    table.append(np.ones((GROUP, 128)))
    return np.concatenate(table, axis=0).astype(np.float32)


def inverse_squares():
    degree = np.arange(TOP + 2 * STEP, dtype=np.float64)[:, None] - 1.0
    return np.broadcast_to(1.0 / (degree * degree - 0.25), (TOP + 2 * STEP, 128)).astype(np.float32)


BLOCKS = sum(blocks_of(group) for group in range(GROUPS))


def row_key(degree, order, kind, place):
    beyond = degree - order
    key = (
        (((order >> 3) - 32) << 26)
        | ((beyond >> 4) << 21)
        | ((beyond & 15) << 17)
        | ((order & 7) << 14)
        | (kind << 13)
        | place
    )
    return jnp.where(kind == 2, (31 << 26) | place, key)


def sort_keys(key):
    height = key.shape[0]
    total = height * 128
    row = lax.broadcasted_iota(I32, key.shape, 0)
    lane = lax.broadcasted_iota(I32, key.shape, 1)
    index = row * 128 + lane
    size = 2
    while size <= total:
        rising = (index & size) == 0
        stride = size // 2
        while stride >= 1:
            low = (index & stride) == 0
            if stride < 128:
                ahead, behind = pltpu.roll(key, 128 - stride, 1), pltpu.roll(key, stride, 1)
            else:
                ahead, behind = pltpu.roll(key, height - stride // 128, 0), pltpu.roll(key, stride // 128, 0)
            other = jnp.where(low, ahead, behind)
            key = jnp.where(low == rising, jnp.minimum(key, other), jnp.maximum(key, other))
            stride //= 2
        size *= 2
    return key


def list_facts(key, limit):
    group = (key >> 26) + 32
    used = group < GROUPS
    group = jnp.where(used, group, 0)
    block = jnp.where(used, (key >> 21) & 31, 0)
    step = jnp.where(used, (key >> 17) & 15, 2)
    lane = jnp.where(used, (key >> 14) & 7, 0)
    kind = jnp.where(used, (key >> 13) & 1, 0)
    place = jnp.minimum(key & 8191, limit)
    order = group * GROUP + lane
    degree = order + block * STEP + step
    number = 19 * group - (((group - 1) * (group - 1)) >> 2) + block
    ring = number & (RING - 1)
    number = jnp.where(used, number, LATE)
    at_value = (ring * SLOT + 1 + step) * WIDE + lane
    at_scale = ring * WIDE + lane
    target = place * PITCH
    m = order.astype(F32)
    first = degree - step
    product = jnp.ones_like(m)
    for q in range(STEP):
        j = first + q
        jf = j.astype(F32)
        ratio = (jf * jf - m * m) / (jf * jf - 0.25)
        product = jnp.where((j > order) & (j <= degree), product * ratio, product)
    at_harm = (order * 2 + kind) * 16
    return number, at_value, at_scale, degree * 32, at_harm, target, lax.rsqrt(product)


def gather_kernel(
    theta_ref, lon_ref, ratio_ref, comp_ref, weight_ref, seen_ref, unknown_ref, slab_ref,
    number_ref, value_ref, scale_ref, radial_ref, harm_ref, target_ref, grow_ref, params_ref,
    local, everyone, map_buf, key_buf, send_sem, recv_sem, map_sem,
):
    me = lax.axis_index("row")
    count = everyone.shape[0]
    half = theta_ref.shape[0]
    rows = map_buf.shape[1]
    width = slab_ref.shape[1]
    read_map = pltpu.make_async_copy(
        unknown_ref.at[:, pl.ds(pl.multiple_of(me * rows, 128), rows)], map_buf, map_sem.at[0]
    )
    read_map.start()
    barrier = pltpu.get_barrier_semaphore()
    for d in range(1, count):
        pl.semaphore_signal(
            barrier, inc=1, device_id={"row": lax.rem(me + d, count)}, device_id_type=pl.DeviceIdType.MESH
        )
    local[...] = jnp.zeros_like(local)
    for k, ref in enumerate((theta_ref, lon_ref, ratio_ref, comp_ref, weight_ref, seen_ref)):
        local[pl.ds(k, 1), pl.ds(0, half)] = ref[...].astype(F32).reshape(1, half)
    pl.semaphore_wait(barrier, count - 1)

    def send(d):
        return pltpu.make_async_remote_copy(
            src_ref=local, dst_ref=everyone.at[me], send_sem=send_sem.at[d], recv_sem=recv_sem.at[d],
            device_id={"row": lax.rem(me + d, count)}, device_id_type=pl.DeviceIdType.MESH,
        )

    def receive(d):
        return pltpu.make_async_remote_copy(
            src_ref=local, dst_ref=everyone.at[lax.rem(me + count - d, count)],
            send_sem=send_sem.at[d], recv_sem=recv_sem.at[d],
            device_id={"row": lax.rem(me + d, count)}, device_id_type=pl.DeviceIdType.MESH,
        )

    for d in range(1, count):
        send(d).start()
    everyone[me] = local[...]
    read_map.wait()
    lanes = lax.broadcasted_iota(I32, (1, 128), 1)
    for t in range((rows + width) // 128):
        ref, at = (map_buf, t * 128) if t * 128 < rows else (slab_ref, t * 128 - rows)
        part = [ref[pl.ds(k, 1), pl.ds(at, 128)] for k in range(3)]
        key_buf[pl.ds(t, 1), :] = row_key(part[0], part[1], part[2], lanes + t * 128)
    place = lax.broadcasted_iota(I32, key_buf.shape, 0) * 128 + lax.broadcasted_iota(I32, key_buf.shape, 1)
    key = sort_keys(jnp.where(place < rows + width, key_buf[...], (31 << 26) | place))
    facts = list_facts(key[: number_ref.shape[0]], rows + width)
    outs = (number_ref, value_ref, scale_ref, radial_ref, harm_ref, target_ref, grow_ref)
    for ref, value in zip(outs, facts):
        ref[...] = value
    for d in range(1, count):
        receive(d).wait_recv()
    left = lax.broadcasted_iota(I32, (8, 128), 1) < half
    for c in range(PARTS):
        merged = jnp.where(left, everyone[2 * c], pltpu.roll(everyone[2 * c + 1], half, 1))
        params_ref[pl.ds(c, 8, stride=8), :] = merged
    for d in range(1, count):
        send(d).wait_send()


def kernel(
    col_ref, number_hbm, value_hbm, scale_hbm, radial_hbm, harm_hbm, target_hbm, grow_hbm,
    params_ref, table_hbm, inv_ref, logs_ref, right_ref, normal_ref,
    out_ref, right_out_ref,
    number_ref, value_ref, scale_ref, radial_ref, harm_ref, target_ref, grow_ref,
    value_buf, scale_buf, harm_buf, radial_buf, design_buf, seed_buf, level_buf, table_ref,
    slab_hi, slab_lo, in_buf, out_buf, list_sem, in_sem, out_sem,
):
    rows, width = normal_ref.shape
    chunks = rows // CHUNK

    lists = [
        pltpu.make_async_copy(src, dst, list_sem.at[k])
        for k, (src, dst) in enumerate(
            (
                (table_hbm, table_ref),
                (number_hbm, number_ref),
                (value_hbm, value_ref),
                (scale_hbm, scale_ref),
                (radial_hbm, radial_ref),
                (harm_hbm, harm_ref),
                (target_hbm, target_ref),
                (grow_hbm, grow_ref),
            )
        )
    ]
    for copy in lists:
        copy.start()

    def fetch(index, slot):
        return pltpu.make_async_copy(
            normal_ref.at[pl.ds(pl.multiple_of(index * CHUNK, CHUNK), CHUNK)], in_buf.at[slot], in_sem.at[slot]
        )

    def put(index, slot):
        return pltpu.make_async_copy(
            out_buf.at[slot], out_ref.at[pl.ds(pl.multiple_of(index * CHUNK, CHUNK), CHUNK)], out_sem.at[slot]
        )

    for k in range(BUFS):
        fetch(k, k).start()

    def param(k):
        return params_ref[pl.ds(8 * k, 8), :]

    theta = param(0)
    lon = param(1)
    cos_t = jnp.cos(theta)
    sin_t = jnp.sin(theta)
    log_s = jnp.log(sin_t)
    comp = param(3)
    weight = param(4)
    scaled = weight * param(5)
    part0 = jnp.where(comp == 2.0, 1.0, jnp.where(comp == 1.0, 0.0, -1.0))
    part1 = jnp.where(comp == 2.0, 0.0, jnp.where(comp == 1.0, 1.0, -1.0))
    part1q = part1 / (sin_t * sin_t)
    inv_r = 1.0 / param(2)

    def spread(values, c):
        return jnp.broadcast_to(values[c : c + 1, :], (8, 128))

    twice = [spread(2.0 * cos_t, c) for c in range(PARTS)]
    logs = [spread(log_s, c) for c in range(PARTS)]
    subf = lax.broadcasted_iota(I32, (8, 128), 0).astype(F32)

    c1 = jnp.cos(lon)
    s1 = jnp.sin(lon)
    cs = [jnp.ones_like(c1)]
    sn = [jnp.zeros_like(c1)]
    for _ in range(8):
        cs.append(cs[-1] * c1 - sn[-1] * s1)
        sn.append(sn[-1] * c1 + cs[-2] * s1)
    c8, s8 = cs[8], sn[8]
    powers = [inv_r * inv_r * inv_r]
    step_r = inv_r
    for _ in range(7):
        powers.append(powers[-1] * inv_r)
    for _ in range(3):
        step_r = step_r * step_r

    def fill(block, carry):
        cc, ss, pw = carry
        base = block * 8
        for j in range(8):
            nf = (base + j).astype(F32)
            square = nf * nf
            harm_buf[pl.ds(pl.multiple_of(base * 32, 32) + j * 32, 8), :] = cc[j]
            harm_buf[pl.ds(pl.multiple_of(base * 32, 32) + j * 32 + 8, 8), :] = cc[j] * square
            harm_buf[pl.ds(pl.multiple_of(base * 32, 32) + j * 32 + 16, 8), :] = ss[j]
            harm_buf[pl.ds(pl.multiple_of(base * 32, 32) + j * 32 + 24, 8), :] = ss[j] * square
            inv_d = 1.0 / ((nf + 1.0) * (nf + 2.0))
            g = pw[j] * part1q * inv_d
            u = (cos_t * g) * (2.0 / (2.0 * nf - 1.0))
            radial_buf[pl.ds(pl.multiple_of(base * 32, 32) + j * 32, 8), :] = pw[j] * (part0 - part1 * ((2.0 * nf + 1.0) * inv_d)) + nf * g
            radial_buf[pl.ds(pl.multiple_of(base * 32, 32) + j * 32 + 8, 8), :] = g
            radial_buf[pl.ds(pl.multiple_of(base * 32, 32) + j * 32 + 16, 8), :] = u * square
            radial_buf[pl.ds(pl.multiple_of(base * 32, 32) + j * 32 + 24, 8), :] = u
        orders = subf + base.astype(F32)
        diag = logs_ref[pl.ds(pl.multiple_of(base, 8), 8), :]
        before = -1.0 / (1.0 - (orders * orders - 0.25) * inv_ref[pl.ds(pl.multiple_of(base, 8), 8), :])
        for c in range(PARTS):
            log_seed = diag + orders * logs[c]
            level = jnp.minimum(jnp.ceil(log_seed * (1.0 / LOG_BIG)), 0.0)
            at = pl.multiple_of(block * 64, 64) + c * 8
            seed_buf[pl.ds(at, 8), :] = jnp.exp(log_seed - level * LOG_BIG) * before
            level_buf[pl.ds(at, 8), :] = level * 64.0
        return (
            tuple(cc[j] * c8 - ss[j] * s8 for j in range(8)),
            tuple(ss[j] * c8 + cc[j] * s8 for j in range(8)),
            tuple(pw[j] * step_r for j in range(8)),
        )

    lax.fori_loop(0, GROUPS, fill, (tuple(cs[:8]), tuple(sn[:8]), tuple(powers)))

    for copy in lists:
        copy.wait()

    def make_row(j):
        at = value_ref[j]
        now = value_buf[pl.ds(at, 8, stride=PITCH), :]
        past = value_buf[pl.ds(at - WIDE, 8, stride=PITCH), :]
        scale = scale_buf[pl.ds(scale_ref[j], 8, stride=PITCH), :]
        n = pl.multiple_of(radial_ref[j], 32)
        h = pl.multiple_of(harm_ref[j], 16)
        kept = now * radial_buf[pl.ds(n, 8), :] - past * radial_buf[pl.ds(n + 16, 8), :]
        spun = now * radial_buf[pl.ds(n + 8, 8), :] - past * radial_buf[pl.ds(n + 24, 8), :]
        body = harm_buf[pl.ds(h, 8), :] * kept - harm_buf[pl.ds(h + 8, 8), :] * spun
        design_buf[pl.ds(target_ref[j], 8), :] = body * (scale * grow_ref[j])

    def drain(cursor, number):
        def more(at):
            return number_ref[at] <= number

        def piece(at):
            for u in range(DRAIN):
                make_row(at + u)
            kept = at + 0
            for u in range(DRAIN):
                kept = kept + (number_ref[at + u] <= number).astype(I32)
            return kept

        return lax.while_loop(more, piece, cursor)

    def group_body(group, carry):
        cursor, number = carry
        zero = jnp.zeros((8, 128), F32)
        orders = subf + (group * GROUP).astype(F32)
        squares = orders * orders - 0.25
        at = pl.multiple_of(group * 64, 64)
        one = tuple(zero for _ in range(PARTS))
        two = tuple(seed_buf[pl.ds(at + c * 8, 8), :] for c in range(PARTS))
        levels = tuple(level_buf[pl.ds(at + c * 8, 8), :] for c in range(PARTS))

        def factors(number):
            sigma = table_ref[pl.ds(pl.multiple_of(number * 8, 8), 8), :]
            return sigma, sigma * SMALL, 64.0 / sigma

        def block_body(block, carry):
            one, two, levels, (sigma, sigma_small, limit), cursor, number = carry
            one, two, levels = list(one), list(two), list(levels)
            cursor = drain(cursor, number - RING)
            ring = number & (RING - 1)
            first = pl.multiple_of(group * GROUP + block * STEP, 8)
            at_scale = ring * WIDE
            at_value = ring * (SLOT * WIDE)
            for c in range(PARTS):
                big = jnp.abs(one[c]) > limit
                factor = jnp.where(big, sigma_small, sigma)
                one[c] = one[c] * factor
                two[c] = two[c] * factor
                levels[c] = levels[c] + jnp.where(big, 64.0, 0.0)
                value_buf[pl.ds(at_value + c * PITCH, 8), :] = one[c]
            for i in range(STEP):
                if i % BATCH == 0:
                    for k in range(i * PACE // STEP, (i + BATCH) * PACE // STEP):
                        make_row(cursor + k)
                rho = 1.0 - squares * inv_ref[pl.ds(first + i, 8), :]
                fresh = [twice[c] * one[c] - rho * two[c] for c in range(PARTS)]
                for c in range(PARTS):
                    value_buf[pl.ds(at_value + (1 + i) * WIDE + c * PITCH, 8), :] = fresh[c]
                one, two = fresh, one
            for c in range(PARTS):
                scale_buf[pl.ds(at_scale + c * PITCH, 8), :] = jnp.exp2(levels[c])
            done = jnp.int32(0)
            for half in (8, 4, 2, 1, 1):
                done = done + jnp.where(number_ref[cursor + done + (half - 1)] < number, half, 0)
            cursor = cursor + jnp.minimum(done, PACE)
            return tuple(one), tuple(two), tuple(levels), factors(number + 1), cursor, number + 1

        blocks = (NMAX + STEP - group * GROUP) // STEP
        out = lax.fori_loop(0, blocks, block_body, (one, two, levels, factors(number), cursor, number))
        return out[4], out[5]

    cursor, _ = lax.fori_loop(0, GROUPS, group_body, (jnp.int32(0), jnp.int32(0)))
    cursor = drain(cursor, BLOCKS)

    def clear(piece, _):
        for u in range(DRAIN):
            design_buf[pl.ds(target_ref[cursor + piece * DRAIN + u], 8), :] = zero
        return 0

    zero = jnp.zeros((8, 128), F32)
    lax.fori_loop(0, (rows + width - cursor + DRAIN - 1) // DRAIN, clear, 0)

    def entries(first, count, c):
        return design_buf[pl.ds(first * PITCH + c, count, stride=PITCH), :]

    peak = jnp.full((8, 128), 1e-30, F32)
    for c in range(PARTS):
        block = jnp.abs(entries(rows, width, c) * weight[c : c + 1, :])
        peak = jnp.maximum(peak, jnp.max(block.reshape(width // 8, 8, 128), axis=0))
    peak = jnp.max(peak, axis=(0, 1), keepdims=True)
    shrink = jnp.exp2(jnp.ceil(jnp.log2(jnp.broadcast_to(peak, (8, 128)))) - 7.0)[0:1, :]
    grow = 1.0 / shrink
    for c in range(PARTS):
        for half in range(width // 256):
            block = entries(rows + half * 256, 256, c)
            block = (block * weight[c : c + 1, :]).T
            hi = block.astype(BF16)
            lo = block - hi.astype(F32)
            cols = pl.ds(half * 256, 256)
            factor = jnp.concatenate([grow, grow], axis=1)
            slab_hi[pl.ds(c * 128, 128), cols] = hi
            slab_lo[pl.ds(c * 128, 128), cols] = (block * factor).astype(F8)
            slab_lo[pl.ds(OBS + c * 128, 128), cols] = (lo * (factor * 512.0)).astype(F8)
    shrink = jnp.concatenate([shrink] * (width // 128), axis=1) * (1.0 / 512.0)

    own = right_ref.shape[0]
    total = jnp.zeros((own, 128), F32)
    at = col_ref[0] * own
    for c in range(PARTS):
        total = total + entries(at, own, c) * scaled[c : c + 1, :]
    summed = lax.dot_general(
        jnp.ones((8, 128), F32), total, (((1,), (1,)), ((), ())),
        precision=lax.Precision.HIGHEST, preferred_element_type=F32,
    )
    right_out_ref[...] = right_ref[...] + summed[0:1, :].reshape(own)

    def chunk_body(index, _):
        slot = lax.rem(index, BUFS)
        his = []
        los = []
        tops = []
        for c in range(PARTS):
            x = entries(index * CHUNK, CHUNK, c)
            hi = x.astype(BF16)
            his.append(hi)
            los.append(((x - hi.astype(F32)) * 512.0).astype(F8))
            tops.append(x.astype(F8))
        update = jnp.dot(jnp.concatenate(los + tops, axis=1), slab_lo[...], preferred_element_type=F32) * shrink
        update += jnp.dot(jnp.concatenate(his, axis=1), slab_hi[...], preferred_element_type=F32)
        fetch(index, slot).wait()

        @pl.when(index >= BUFS)
        def _():
            put(index - BUFS, slot).wait()

        out_buf[slot] = in_buf[slot] + update
        put(index, slot).start()

        @pl.when(index + BUFS < chunks)
        def _():
            fetch(index + BUFS, slot).start()

        return 0

    lax.fori_loop(0, chunks, chunk_body, 0)
    for k in range(BUFS):
        put(chunks - BUFS + k, k).wait()


def local_update(params, col, facts, normal_slab, right_side):
    rows, width = normal_slab.shape
    own = right_side.shape[0]
    entries = facts[0].shape[0]
    smem = pl.BlockSpec(memory_space=pltpu.SMEM)
    vmem = pl.BlockSpec(memory_space=pltpu.VMEM)
    hbm = pl.BlockSpec(memory_space=pltpu.HBM)
    return pl.pallas_call(
        kernel,
        out_shape=(
            jax.ShapeDtypeStruct((rows, width), F32),
            jax.ShapeDtypeStruct((own,), F32),
        ),
        in_specs=[smem] + [hbm] * 7 + [vmem, hbm, vmem, vmem, vmem, hbm],
        out_specs=(hbm, vmem),
        scratch_shapes=[pltpu.SMEM((entries,), I32)] * 6
        + [pltpu.SMEM((entries,), F32)]
        + [
            pltpu.VMEM((RING * SLOT * WIDE, 128), F32),
            pltpu.VMEM((RING * WIDE, 128), F32),
            pltpu.VMEM((TOP * 32, 128), F32),
            pltpu.VMEM((TOP * 32, 128), F32),
            pltpu.VMEM(((rows + width + 1) * PITCH, 128), F32),
            pltpu.VMEM((GROUPS * 64, 128), F32),
            pltpu.VMEM((GROUPS * 64, 128), F32),
            pltpu.VMEM((BLOCKS * 8 + 8, 128), F32),
            pltpu.VMEM((OBS, width), BF16),
            pltpu.VMEM((2 * OBS, width), F8),
            pltpu.VMEM((BUFS, CHUNK, width), F32),
            pltpu.VMEM((BUFS, CHUNK, width), F32),
            pltpu.SemaphoreType.DMA((8,)),
            pltpu.SemaphoreType.DMA((BUFS,)),
            pltpu.SemaphoreType.DMA((BUFS,)),
        ],
        compiler_params=pltpu.CompilerParams(vmem_limit_bytes=62 * 1024 * 1024),
        name="normal_update",
    )(
        col, *facts, params, jnp.asarray(block_scales()), jnp.asarray(inverse_squares()),
        jnp.asarray(diagonal_logs()), right_side, normal_slab,
    )


def on_device(
    colatitude, longitude, radius_ratio, component, obs_weight, observed,
    unknown_map, slab_map, normal_slab, right_side,
):
    rows, width = normal_slab.shape
    col = lax.axis_index("col").astype(I32).reshape(1)
    entries = -(-(rows + width + 2 * PACE) // 1024) * 1024
    total = 1 << (rows + width - 1).bit_length()
    shape = (entries // 128, 128)
    count = lax.axis_size("row")
    vmem = pl.BlockSpec(memory_space=pltpu.VMEM)
    outs = pl.pallas_call(
        gather_kernel,
        out_shape=tuple(jax.ShapeDtypeStruct(shape, I32) for _ in range(6))
        + (jax.ShapeDtypeStruct(shape, F32), jax.ShapeDtypeStruct((64, 128), F32)),
        in_specs=[vmem] * 6 + [pl.BlockSpec(memory_space=pltpu.HBM), vmem],
        out_specs=(vmem,) * 8,
        scratch_shapes=[
            pltpu.VMEM((8, 128), F32),
            pltpu.VMEM((count, 8, 128), F32),
            pltpu.VMEM((3, rows), I32),
            pltpu.VMEM((total // 128, 128), I32),
            pltpu.SemaphoreType.DMA((count,)),
            pltpu.SemaphoreType.DMA((count,)),
            pltpu.SemaphoreType.DMA((1,)),
        ],
        compiler_params=pltpu.CompilerParams(collective_id=0, has_side_effects=True),
        name="gather_observations",
    )(colatitude, longitude, radius_ratio, component, obs_weight, observed, unknown_map, slab_map)
    facts = tuple(x.reshape(entries) for x in outs[:7])
    return local_update(outs[7], col, facts, normal_slab, right_side)


def solution(mesh):
    return jax.shard_map(
        on_device,
        mesh=mesh,
        in_specs=(
            P("row"), P("row"), P("row"), P("row"), P("row"), P("row"),
            P(), P(None, "col"), P("row", "col"), P(("row", "col")),
        ),
        out_specs=(P("row", "col"), P(("row", "col"))),
        check_vma=False,
    )
```

```python
import jax
import jax.numpy as jnp
import numpy as np
from jax import lax
from jax.experimental import pallas as pl
from jax.experimental.pallas import tpu as pltpu
from jax.sharding import PartitionSpec as P

NMAX = 300
TOP = 304
GROUP = 8
GROUPS = TOP // GROUP
STEP = 16
SLOT = STEP + 1
PITCH = 9
WIDE = 8 * PITCH
RING = 8
BUFS = 2
OBS = 1024
PARTS = 8
CHUNK = 768
PACE = 16
BATCH = 2
DRAIN = 16
BODY = 4
LATE = 1 << 20
BIG = float(2.0**64)
SMALL = float(2.0**-64)
LOG_BIG = float(64.0 * np.log(2.0))
F32 = jnp.float32
BF16 = jnp.bfloat16
F8 = jnp.float8_e4m3fn
I32 = jnp.int32


def blocks_of(group):
    return (NMAX + STEP - group * GROUP) // STEP


def diagonal_logs():
    counter = np.arange(1, TOP, dtype=np.float64)
    steps = 0.5 * np.log((2.0 * counter + 1.0) / (2.0 * counter))
    logs = np.concatenate([[0.0], 0.5 * np.log(2.0) + np.cumsum(steps)])
    return np.broadcast_to(logs[:, None], (TOP, 128)).astype(np.float32)


def block_scales():
    table = []
    for group in range(GROUPS):
        order = (group * GROUP + np.arange(GROUP, dtype=np.float64))[:, None]
        for block in range(blocks_of(group)):
            sigma = np.zeros((GROUP, 1))
            if block > 0:
                degree = order + STEP * (block - 1) + np.arange(STEP)[None, :]
                ratio = (degree**2 - order**2) / (degree**2 - 0.25)
                if block == 1:
                    ratio[:, 0] = 1.0
                sigma = 1.0 / np.sqrt(np.prod(ratio, axis=1, keepdims=True))
            table.append(np.broadcast_to(sigma, (GROUP, 128)))
    table += [np.zeros((GROUP, 128))] * (STEPS - len(table))
    return np.concatenate(table, axis=0).astype(np.float32)


def inverse_squares():
    degree = np.arange(TOP + 2 * STEP, dtype=np.float64)[:, None] - 1.0
    return np.broadcast_to(1.0 / (degree * degree - 0.25), (TOP + 2 * STEP, 128)).astype(np.float32)


BLOCKS = sum(blocks_of(group) for group in range(GROUPS))
STEPS = -(-BLOCKS // BODY) * BODY


def block_lists():
    lists = np.zeros((2, STEPS), np.int32)
    at = 0
    for group in range(GROUPS):
        for block in range(blocks_of(group)):
            lists[:, at] = group * GROUP, group * GROUP + block * STEP
            at += 1
    return lists.reshape(-1)


def row_key(degree, order, kind, place):
    beyond = degree - order
    key = (
        (((order >> 3) - 32) << 26)
        | ((beyond >> 4) << 21)
        | ((beyond & 15) << 17)
        | ((order & 7) << 14)
        | (kind << 13)
        | place
    )
    return jnp.where(kind == 2, (31 << 26) | place, key)


def sort_keys(key):
    height = key.shape[0]
    total = height * 128
    row = lax.broadcasted_iota(I32, key.shape, 0)
    lane = lax.broadcasted_iota(I32, key.shape, 1)
    index = row * 128 + lane
    size = 2
    while size <= total:
        rising = (index & size) == 0
        stride = size // 2
        while stride >= 1:
            low = (index & stride) == 0
            if stride < 128:
                ahead, behind = pltpu.roll(key, 128 - stride, 1), pltpu.roll(key, stride, 1)
            else:
                ahead, behind = pltpu.roll(key, height - stride // 128, 0), pltpu.roll(key, stride // 128, 0)
            other = jnp.where(low, ahead, behind)
            key = jnp.where(low == rising, jnp.minimum(key, other), jnp.maximum(key, other))
            stride //= 2
        size *= 2
    return key


def list_facts(key, limit):
    group = (key >> 26) + 32
    used = group < GROUPS
    group = jnp.where(used, group, 0)
    block = jnp.where(used, (key >> 21) & 31, 0)
    step = jnp.where(used, (key >> 17) & 15, 2)
    lane = jnp.where(used, (key >> 14) & 7, 0)
    kind = jnp.where(used, (key >> 13) & 1, 0)
    place = jnp.minimum(key & 8191, limit)
    order = group * GROUP + lane
    degree = order + block * STEP + step
    number = 19 * group - (((group - 1) * (group - 1)) >> 2) + block
    ring = number & (RING - 1)
    number = jnp.where(used, number, LATE)
    at_value = (ring * SLOT + 1 + step) * WIDE + lane
    at_scale = ring * WIDE + lane
    target = place * PITCH
    m = order.astype(F32)
    first = degree - step
    product = jnp.ones_like(m)
    for q in range(STEP):
        j = first + q
        jf = j.astype(F32)
        ratio = (jf * jf - m * m) / (jf * jf - 0.25)
        product = jnp.where((j > order) & (j <= degree), product * ratio, product)
    at_harm = (order * 2 + kind) * 16
    return number, at_value, at_scale, degree * 32, at_harm, target, lax.rsqrt(product)


def gather_kernel(
    theta_ref, lon_ref, ratio_ref, comp_ref, weight_ref, seen_ref, unknown_ref, slab_ref,
    number_ref, value_ref, scale_ref, radial_ref, harm_ref, target_ref, grow_ref, params_ref,
    local, everyone, map_buf, key_buf, send_sem, recv_sem, map_sem,
):
    me = lax.axis_index("row")
    count = everyone.shape[0]
    half = theta_ref.shape[0]
    rows = map_buf.shape[1]
    width = slab_ref.shape[1]
    read_map = pltpu.make_async_copy(
        unknown_ref.at[:, pl.ds(pl.multiple_of(me * rows, 128), rows)], map_buf, map_sem.at[0]
    )
    read_map.start()
    barrier = pltpu.get_barrier_semaphore()
    for d in range(1, count):
        pl.semaphore_signal(
            barrier, inc=1, device_id={"row": lax.rem(me + d, count)}, device_id_type=pl.DeviceIdType.MESH
        )
    local[...] = jnp.zeros_like(local)
    for k, ref in enumerate((theta_ref, lon_ref, ratio_ref, comp_ref, weight_ref, seen_ref)):
        local[pl.ds(k, 1), pl.ds(0, half)] = ref[...].astype(F32).reshape(1, half)
    pl.semaphore_wait(barrier, count - 1)

    def send(d):
        return pltpu.make_async_remote_copy(
            src_ref=local, dst_ref=everyone.at[me], send_sem=send_sem.at[d], recv_sem=recv_sem.at[d],
            device_id={"row": lax.rem(me + d, count)}, device_id_type=pl.DeviceIdType.MESH,
        )

    def receive(d):
        return pltpu.make_async_remote_copy(
            src_ref=local, dst_ref=everyone.at[lax.rem(me + count - d, count)],
            send_sem=send_sem.at[d], recv_sem=recv_sem.at[d],
            device_id={"row": lax.rem(me + d, count)}, device_id_type=pl.DeviceIdType.MESH,
        )

    for d in range(1, count):
        send(d).start()
    everyone[me] = local[...]
    read_map.wait()
    lanes = lax.broadcasted_iota(I32, (1, 128), 1)
    for t in range((rows + width) // 128):
        ref, at = (map_buf, t * 128) if t * 128 < rows else (slab_ref, t * 128 - rows)
        part = [ref[pl.ds(k, 1), pl.ds(at, 128)] for k in range(3)]
        key_buf[pl.ds(t, 1), :] = row_key(part[0], part[1], part[2], lanes + t * 128)
    place = lax.broadcasted_iota(I32, key_buf.shape, 0) * 128 + lax.broadcasted_iota(I32, key_buf.shape, 1)
    key = sort_keys(jnp.where(place < rows + width, key_buf[...], (31 << 26) | place))
    facts = list_facts(key[: number_ref.shape[0]], rows + width)
    outs = (number_ref, value_ref, scale_ref, radial_ref, harm_ref, target_ref, grow_ref)
    for ref, value in zip(outs, facts):
        ref[...] = value
    for d in range(1, count):
        receive(d).wait_recv()
    left = lax.broadcasted_iota(I32, (8, 128), 1) < half
    for c in range(PARTS):
        merged = jnp.where(left, everyone[2 * c], pltpu.roll(everyone[2 * c + 1], half, 1))
        params_ref[pl.ds(c, 8, stride=8), :] = merged
    for d in range(1, count):
        send(d).wait_send()


def kernel(
    col_ref, blocks_ref, number_hbm, value_hbm, scale_hbm, radial_hbm, harm_hbm, target_hbm, grow_hbm,
    params_ref, table_hbm, inv_ref, logs_ref, right_ref, normal_ref,
    out_ref, right_out_ref,
    number_ref, value_ref, scale_ref, radial_ref, harm_ref, target_ref, grow_ref,
    value_buf, scale_buf, harm_buf, radial_buf, design_buf, seed_buf, level_buf, square_buf, table_ref,
    slab_hi, slab_lo, in_buf, out_buf, list_sem, in_sem, out_sem,
):
    rows, width = normal_ref.shape
    chunks = rows // CHUNK

    lists = [
        pltpu.make_async_copy(src, dst, list_sem.at[k])
        for k, (src, dst) in enumerate(
            (
                (table_hbm, table_ref),
                (number_hbm, number_ref),
                (value_hbm, value_ref),
                (scale_hbm, scale_ref),
                (radial_hbm, radial_ref),
                (harm_hbm, harm_ref),
                (target_hbm, target_ref),
                (grow_hbm, grow_ref),
            )
        )
    ]
    for copy in lists:
        copy.start()

    def fetch(index, slot):
        return pltpu.make_async_copy(
            normal_ref.at[pl.ds(pl.multiple_of(index * CHUNK, CHUNK), CHUNK)], in_buf.at[slot], in_sem.at[slot]
        )

    def put(index, slot):
        return pltpu.make_async_copy(
            out_buf.at[slot], out_ref.at[pl.ds(pl.multiple_of(index * CHUNK, CHUNK), CHUNK)], out_sem.at[slot]
        )

    for k in range(BUFS):
        fetch(k, k).start()

    def param(k):
        return params_ref[pl.ds(8 * k, 8), :]

    theta = param(0)
    lon = param(1)
    cos_t = jnp.cos(theta)
    sin_t = jnp.sin(theta)
    log_s = jnp.log(sin_t)
    comp = param(3)
    weight = param(4)
    scaled = weight * param(5)
    part0 = jnp.where(comp == 2.0, 1.0, jnp.where(comp == 1.0, 0.0, -1.0))
    part1 = jnp.where(comp == 2.0, 0.0, jnp.where(comp == 1.0, 1.0, -1.0))
    part1q = part1 / (sin_t * sin_t)
    inv_r = 1.0 / param(2)

    def spread(values, c):
        return jnp.broadcast_to(values[c : c + 1, :], (8, 128))

    twice = [spread(2.0 * cos_t, c) for c in range(PARTS)]
    logs = [spread(log_s, c) for c in range(PARTS)]
    subf = lax.broadcasted_iota(I32, (8, 128), 0).astype(F32)

    c1 = jnp.cos(lon)
    s1 = jnp.sin(lon)
    cs = [jnp.ones_like(c1)]
    sn = [jnp.zeros_like(c1)]
    for _ in range(8):
        cs.append(cs[-1] * c1 - sn[-1] * s1)
        sn.append(sn[-1] * c1 + cs[-2] * s1)
    c8, s8 = cs[8], sn[8]
    powers = [inv_r * inv_r * inv_r]
    step_r = inv_r
    for _ in range(7):
        powers.append(powers[-1] * inv_r)
    for _ in range(3):
        step_r = step_r * step_r

    def fill(block, carry):
        cc, ss, pw = carry
        base = block * 8
        for j in range(8):
            nf = (base + j).astype(F32)
            square = nf * nf
            harm_buf[pl.ds(pl.multiple_of(base * 32, 32) + j * 32, 8), :] = cc[j]
            harm_buf[pl.ds(pl.multiple_of(base * 32, 32) + j * 32 + 8, 8), :] = cc[j] * square
            harm_buf[pl.ds(pl.multiple_of(base * 32, 32) + j * 32 + 16, 8), :] = ss[j]
            harm_buf[pl.ds(pl.multiple_of(base * 32, 32) + j * 32 + 24, 8), :] = ss[j] * square
            inv_d = 1.0 / ((nf + 1.0) * (nf + 2.0))
            g = pw[j] * part1q * inv_d
            u = (cos_t * g) * (2.0 / (2.0 * nf - 1.0))
            radial_buf[pl.ds(pl.multiple_of(base * 32, 32) + j * 32, 8), :] = pw[j] * (part0 - part1 * ((2.0 * nf + 1.0) * inv_d)) + nf * g
            radial_buf[pl.ds(pl.multiple_of(base * 32, 32) + j * 32 + 8, 8), :] = g
            radial_buf[pl.ds(pl.multiple_of(base * 32, 32) + j * 32 + 16, 8), :] = u * square
            radial_buf[pl.ds(pl.multiple_of(base * 32, 32) + j * 32 + 24, 8), :] = u
        orders = subf + base.astype(F32)
        diag = logs_ref[pl.ds(pl.multiple_of(base, 8), 8), :]
        square = orders * orders - 0.25
        square_buf[pl.ds(pl.multiple_of(base, 8), 8), :] = square
        before = -1.0 / (1.0 - square * inv_ref[pl.ds(pl.multiple_of(base, 8), 8), :])
        for c in range(PARTS):
            log_seed = diag + orders * logs[c]
            level = jnp.minimum(jnp.ceil(log_seed * (1.0 / LOG_BIG)), 0.0)
            at = pl.multiple_of(block * 64, 64) + c * 8
            seed_buf[pl.ds(at, 8), :] = jnp.exp(log_seed - level * LOG_BIG) * before
            level_buf[pl.ds(at, 8), :] = level * 64.0
        return (
            tuple(cc[j] * c8 - ss[j] * s8 for j in range(8)),
            tuple(ss[j] * c8 + cc[j] * s8 for j in range(8)),
            tuple(pw[j] * step_r for j in range(8)),
        )

    lax.fori_loop(0, GROUPS, fill, (tuple(cs[:8]), tuple(sn[:8]), tuple(powers)))

    for copy in lists:
        copy.wait()

    def make_row(j):
        at = value_ref[j]
        now = value_buf[pl.ds(at, 8, stride=PITCH), :]
        past = value_buf[pl.ds(at - WIDE, 8, stride=PITCH), :]
        scale = scale_buf[pl.ds(scale_ref[j], 8, stride=PITCH), :]
        n = pl.multiple_of(radial_ref[j], 32)
        h = pl.multiple_of(harm_ref[j], 16)
        kept = now * radial_buf[pl.ds(n, 8), :] - past * radial_buf[pl.ds(n + 16, 8), :]
        spun = now * radial_buf[pl.ds(n + 8, 8), :] - past * radial_buf[pl.ds(n + 24, 8), :]
        body = harm_buf[pl.ds(h, 8), :] * kept - harm_buf[pl.ds(h + 8, 8), :] * spun
        design_buf[pl.ds(target_ref[j], 8), :] = body * (scale * grow_ref[j])

    def drain(cursor, number):
        def more(at):
            return number_ref[at] <= number

        def piece(at):
            for u in range(DRAIN):
                make_row(at + u)
            return at + passed(at, number + 1)

        return lax.while_loop(more, piece, cursor)

    def passed(at, number):
        done = jnp.int32(0)
        for half in (8, 4, 2, 1, 1):
            done = done + jnp.where(number_ref[at + done + (half - 1)] < number, half, 0)
        return done

    zero = jnp.zeros((8, 128), F32)

    def block_step(number, state, cursor):
        one, two, levels = [list(x) for x in state]
        order = blocks_ref[number]
        first = blocks_ref[STEPS + number]
        ring = number & (RING - 1)
        at_scale = ring * WIDE
        at_value = ring * (SLOT * WIDE)
        at_seed = pl.multiple_of(order * 8, 64)
        opens = jnp.broadcast_to(order == first, (8, 128))
        sigma = table_ref[pl.ds(pl.multiple_of(number * 8, 8), 8), :]
        sigma_small = sigma * SMALL
        limit = 64.0 / sigma
        squares = square_buf[pl.ds(pl.multiple_of(order, 8), 8), :]
        for c in range(PARTS):
            big = jnp.abs(one[c]) > limit
            factor = jnp.where(big, sigma_small, sigma)
            one[c] = one[c] * factor
            two[c] = jnp.where(opens, seed_buf[pl.ds(at_seed + c * 8, 8), :], two[c] * factor)
            level = levels[c] + jnp.where(big, 64.0, 0.0)
            levels[c] = jnp.where(opens, level_buf[pl.ds(at_seed + c * 8, 8), :], level)
            value_buf[pl.ds(at_value + c * PITCH, 8), :] = one[c]
        for i in range(STEP):
            if i % BATCH == 0:
                for k in range(i * PACE // STEP, (i + BATCH) * PACE // STEP):
                    make_row(cursor + k)
            rho = 1.0 - squares * inv_ref[pl.ds(first + i, 8), :]
            fresh = [twice[c] * one[c] - rho * two[c] for c in range(PARTS)]
            for c in range(PARTS):
                value_buf[pl.ds(at_value + (1 + i) * WIDE + c * PITCH, 8), :] = fresh[c]
            one, two = fresh, one
        for c in range(PARTS):
            scale_buf[pl.ds(at_scale + c * PITCH, 8), :] = jnp.exp2(levels[c])
        return tuple(one), tuple(two), tuple(levels)

    def body(index, carry):
        state, cursor = carry
        number = index * BODY
        cursor = drain(cursor, number + BODY - 1 - RING)
        for k in range(BODY):
            state = block_step(number + k, state, cursor)
            cursor = cursor + passed(cursor, number + k)
        return state, cursor

    still = tuple((zero,) * PARTS for _ in range(3))
    _, cursor = lax.fori_loop(0, STEPS // BODY, body, (still, jnp.int32(0)))
    cursor = drain(cursor, BLOCKS)

    def clear(piece, _):
        for u in range(DRAIN):
            design_buf[pl.ds(target_ref[cursor + piece * DRAIN + u], 8), :] = zero
        return 0

    lax.fori_loop(0, (rows + width - cursor + DRAIN - 1) // DRAIN, clear, 0)

    def entries(first, count, c):
        return design_buf[pl.ds(first * PITCH + c, count, stride=PITCH), :]

    peak = jnp.full((8, 128), 1e-30, F32)
    for c in range(PARTS):
        block = jnp.abs(entries(rows, width, c) * weight[c : c + 1, :])
        peak = jnp.maximum(peak, jnp.max(block.reshape(width // 8, 8, 128), axis=0))
    peak = jnp.max(peak, axis=(0, 1), keepdims=True)
    shrink = jnp.exp2(jnp.ceil(jnp.log2(jnp.broadcast_to(peak, (8, 128)))) - 7.0)[0:1, :]
    grow = 1.0 / shrink
    for c in range(PARTS):
        for half in range(width // 256):
            block = entries(rows + half * 256, 256, c)
            block = (block * weight[c : c + 1, :]).T
            hi = block.astype(BF16)
            lo = block - hi.astype(F32)
            cols = pl.ds(half * 256, 256)
            factor = jnp.concatenate([grow, grow], axis=1)
            slab_hi[pl.ds(c * 128, 128), cols] = hi
            slab_lo[pl.ds(c * 128, 128), cols] = (block * factor).astype(F8)
            slab_lo[pl.ds(OBS + c * 128, 128), cols] = (lo * (factor * 512.0)).astype(F8)
    shrink = jnp.concatenate([shrink] * (width // 128), axis=1) * (1.0 / 512.0)

    own = right_ref.shape[0]
    total = jnp.zeros((own, 128), F32)
    at = col_ref[0] * own
    for c in range(PARTS):
        total = total + entries(at, own, c) * scaled[c : c + 1, :]
    summed = lax.dot_general(
        jnp.ones((8, 128), F32), total, (((1,), (1,)), ((), ())),
        precision=lax.Precision.HIGHEST, preferred_element_type=F32,
    )
    right_out_ref[...] = right_ref[...] + summed[0:1, :].reshape(own)

    def chunk_body(index, _):
        slot = lax.rem(index, BUFS)
        his = []
        los = []
        tops = []
        for c in range(PARTS):
            x = entries(index * CHUNK, CHUNK, c)
            hi = x.astype(BF16)
            his.append(hi)
            los.append(((x - hi.astype(F32)) * 512.0).astype(F8))
            tops.append(x.astype(F8))
        update = jnp.dot(jnp.concatenate(los + tops, axis=1), slab_lo[...], preferred_element_type=F32) * shrink
        update += jnp.dot(jnp.concatenate(his, axis=1), slab_hi[...], preferred_element_type=F32)
        fetch(index, slot).wait()

        @pl.when(index >= BUFS)
        def _():
            put(index - BUFS, slot).wait()

        out_buf[slot] = in_buf[slot] + update
        put(index, slot).start()

        @pl.when(index + BUFS < chunks)
        def _():
            fetch(index + BUFS, slot).start()

        return 0

    lax.fori_loop(0, chunks, chunk_body, 0)
    for k in range(BUFS):
        put(chunks - BUFS + k, k).wait()


def local_update(params, col, facts, normal_slab, right_side):
    rows, width = normal_slab.shape
    own = right_side.shape[0]
    entries = facts[0].shape[0]
    smem = pl.BlockSpec(memory_space=pltpu.SMEM)
    vmem = pl.BlockSpec(memory_space=pltpu.VMEM)
    hbm = pl.BlockSpec(memory_space=pltpu.HBM)
    return pl.pallas_call(
        kernel,
        out_shape=(
            jax.ShapeDtypeStruct((rows, width), F32),
            jax.ShapeDtypeStruct((own,), F32),
        ),
        in_specs=[smem] * 2 + [hbm] * 7 + [vmem, hbm, vmem, vmem, vmem, hbm],
        out_specs=(hbm, vmem),
        scratch_shapes=[pltpu.SMEM((entries,), I32)] * 6
        + [pltpu.SMEM((entries,), F32)]
        + [
            pltpu.VMEM((RING * SLOT * WIDE, 128), F32),
            pltpu.VMEM((RING * WIDE, 128), F32),
            pltpu.VMEM((TOP * 32, 128), F32),
            pltpu.VMEM((TOP * 32, 128), F32),
            pltpu.VMEM(((rows + width + 1) * PITCH, 128), F32),
            pltpu.VMEM((GROUPS * 64, 128), F32),
            pltpu.VMEM((GROUPS * 64, 128), F32),
            pltpu.VMEM((TOP, 128), F32),
            pltpu.VMEM((STEPS * 8, 128), F32),
            pltpu.VMEM((OBS, width), BF16),
            pltpu.VMEM((2 * OBS, width), F8),
            pltpu.VMEM((BUFS, CHUNK, width), F32),
            pltpu.VMEM((BUFS, CHUNK, width), F32),
            pltpu.SemaphoreType.DMA((8,)),
            pltpu.SemaphoreType.DMA((BUFS,)),
            pltpu.SemaphoreType.DMA((BUFS,)),
        ],
        compiler_params=pltpu.CompilerParams(vmem_limit_bytes=62 * 1024 * 1024),
        name="normal_update",
    )(
        col, jnp.asarray(block_lists()), *facts, params, jnp.asarray(block_scales()), jnp.asarray(inverse_squares()),
        jnp.asarray(diagonal_logs()), right_side, normal_slab,
    )


def on_device(
    colatitude, longitude, radius_ratio, component, obs_weight, observed,
    unknown_map, slab_map, normal_slab, right_side,
):
    rows, width = normal_slab.shape
    col = lax.axis_index("col").astype(I32).reshape(1)
    entries = -(-(rows + width + 2 * PACE) // 1024) * 1024
    total = 1 << (rows + width - 1).bit_length()
    shape = (entries // 128, 128)
    count = lax.axis_size("row")
    vmem = pl.BlockSpec(memory_space=pltpu.VMEM)
    outs = pl.pallas_call(
        gather_kernel,
        out_shape=tuple(jax.ShapeDtypeStruct(shape, I32) for _ in range(6))
        + (jax.ShapeDtypeStruct(shape, F32), jax.ShapeDtypeStruct((64, 128), F32)),
        in_specs=[vmem] * 6 + [pl.BlockSpec(memory_space=pltpu.HBM), vmem],
        out_specs=(vmem,) * 8,
        scratch_shapes=[
            pltpu.VMEM((8, 128), F32),
            pltpu.VMEM((count, 8, 128), F32),
            pltpu.VMEM((3, rows), I32),
            pltpu.VMEM((total // 128, 128), I32),
            pltpu.SemaphoreType.DMA((count,)),
            pltpu.SemaphoreType.DMA((count,)),
            pltpu.SemaphoreType.DMA((1,)),
        ],
        compiler_params=pltpu.CompilerParams(collective_id=0, has_side_effects=True),
        name="gather_observations",
    )(colatitude, longitude, radius_ratio, component, obs_weight, observed, unknown_map, slab_map)
    facts = tuple(x.reshape(entries) for x in outs[:7])
    return local_update(outs[7], col, facts, normal_slab, right_side)


def solution(mesh):
    return jax.shard_map(
        on_device,
        mesh=mesh,
        in_specs=(
            P("row"), P("row"), P("row"), P("row"), P("row"), P("row"),
            P(), P(None, "col"), P("row", "col"), P(("row", "col")),
        ),
        out_specs=(P("row", "col"), P(("row", "col"))),
        check_vma=False,
    )
```

```python
import jax
import jax.numpy as jnp
import numpy as np
from jax import lax
from jax.experimental import pallas as pl
from jax.experimental.pallas import tpu as pltpu
from jax.sharding import PartitionSpec as P

NMAX = 300
TOP = 304
GROUP = 8
GROUPS = TOP // GROUP
STEP = 16
SLOT = STEP + 1
PITCH = 9
WIDE = 8 * PITCH
RING = 8
BUFS = 2
OBS = 1024
PARTS = 8
CHUNK = 768
PACE = 16
BATCH = 2
DRAIN = 16
BODY = 5
LATE = 1 << 14
BIG = float(2.0**64)
SMALL = float(2.0**-64)
LOG_BIG = float(64.0 * np.log(2.0))
F32 = jnp.float32
BF16 = jnp.bfloat16
F8 = jnp.float8_e4m3fn
I32 = jnp.int32


def blocks_of(group):
    return (NMAX + STEP - group * GROUP) // STEP


def diagonal_logs():
    counter = np.arange(1, TOP, dtype=np.float64)
    steps = 0.5 * np.log((2.0 * counter + 1.0) / (2.0 * counter))
    logs = np.concatenate([[0.0], 0.5 * np.log(2.0) + np.cumsum(steps)])
    return np.broadcast_to(logs[:, None], (TOP, 128)).astype(np.float32)


def block_scales():
    table = []
    for group in range(GROUPS):
        order = (group * GROUP + np.arange(GROUP, dtype=np.float64))[:, None]
        for block in range(blocks_of(group)):
            sigma = np.zeros((GROUP, 1))
            if block > 0:
                degree = order + STEP * (block - 1) + np.arange(STEP)[None, :]
                ratio = (degree**2 - order**2) / (degree**2 - 0.25)
                if block == 1:
                    ratio[:, 0] = 1.0
                sigma = 1.0 / np.sqrt(np.prod(ratio, axis=1, keepdims=True))
            table.append(np.broadcast_to(sigma, (GROUP, 128)))
    table += [np.zeros((GROUP, 128))] * (STEPS - len(table))
    return np.concatenate(table, axis=0).astype(np.float32)


def inverse_squares():
    degree = np.arange(TOP + 2 * STEP, dtype=np.float64)[:, None] - 1.0
    return np.broadcast_to(1.0 / (degree * degree - 0.25), (TOP + 2 * STEP, 128)).astype(np.float32)


BLOCKS = sum(blocks_of(group) for group in range(GROUPS))
STEPS = -(-BLOCKS // BODY) * BODY


def block_lists():
    lists = np.zeros((2, STEPS), np.int32)
    at = 0
    for group in range(GROUPS):
        for block in range(blocks_of(group)):
            lists[:, at] = group * GROUP, group * GROUP + block * STEP
            at += 1
    return lists.reshape(-1)


def row_key(degree, order, kind, place):
    beyond = degree - order
    key = (
        (((order >> 3) - 32) << 26)
        | ((beyond >> 4) << 21)
        | ((beyond & 15) << 17)
        | ((order & 7) << 14)
        | (kind << 13)
        | place
    )
    return jnp.where(kind == 2, (31 << 26) | place, key)


def sort_keys(key):
    height = key.shape[0]
    total = height * 128
    row = lax.broadcasted_iota(I32, key.shape, 0)
    lane = lax.broadcasted_iota(I32, key.shape, 1)
    index = row * 128 + lane
    size = 2
    while size <= total:
        rising = (index & size) == 0
        stride = size // 2
        while stride >= 1:
            low = (index & stride) == 0
            if stride < 128:
                ahead, behind = pltpu.roll(key, 128 - stride, 1), pltpu.roll(key, stride, 1)
            else:
                ahead, behind = pltpu.roll(key, height - stride // 128, 0), pltpu.roll(key, stride // 128, 0)
            other = jnp.where(low, ahead, behind)
            key = jnp.where(low == rising, jnp.minimum(key, other), jnp.maximum(key, other))
            stride //= 2
        size *= 2
    return key


def list_facts(key, limit):
    group = (key >> 26) + 32
    used = group < GROUPS
    group = jnp.where(used, group, 0)
    block = jnp.where(used, (key >> 21) & 31, 0)
    step = jnp.where(used, (key >> 17) & 15, 2)
    lane = jnp.where(used, (key >> 14) & 7, 0)
    kind = jnp.where(used, (key >> 13) & 1, 0)
    place = jnp.minimum(key & 8191, limit)
    order = group * GROUP + lane
    degree = order + block * STEP + step
    number = 19 * group - (((group - 1) * (group - 1)) >> 2) + block
    ring = number & (RING - 1)
    number = jnp.where(used, number, LATE)
    at_value = (ring * SLOT + 1 + step) * WIDE + lane
    at_scale = ring * WIDE + lane
    target = place * PITCH
    m = order.astype(F32)
    first = degree - step
    product = jnp.ones_like(m)
    for q in range(STEP):
        j = first + q
        jf = j.astype(F32)
        ratio = (jf * jf - m * m) / (jf * jf - 0.25)
        product = jnp.where((j > order) & (j <= degree), product * ratio, product)
    at_harm = (order * 2 + kind) * 16
    return (number << 16) | at_scale, (at_value << 16) | at_harm, (degree << 21) | target, lax.rsqrt(product)


def gather_kernel(
    theta_hbm, lon_hbm, ratio_hbm, comp_hbm, weight_hbm, seen_hbm, unknown_ref, slab_hbm,
    number_ref, value_ref, target_ref, grow_ref, params_ref,
    theta_ref, lon_ref, ratio_ref, comp_ref, weight_ref, seen_ref, slab_ref,
    local, everyone, map_buf, key_buf, send_sem, recv_sem, map_sem, in_sem,
):
    me = lax.axis_index("row")
    count = everyone.shape[0]
    half = theta_ref.shape[0]
    rows = map_buf.shape[1]
    width = slab_ref.shape[1]
    read_map = pltpu.make_async_copy(
        unknown_ref.at[:, pl.ds(pl.multiple_of(me * rows, 128), rows)], map_buf, map_sem.at[0]
    )
    inputs = [
        pltpu.make_async_copy(src, dst, in_sem.at[k])
        for k, (src, dst) in enumerate(
            (
                (theta_hbm, theta_ref),
                (lon_hbm, lon_ref),
                (ratio_hbm, ratio_ref),
                (comp_hbm, comp_ref),
                (weight_hbm, weight_ref),
                (seen_hbm, seen_ref),
                (slab_hbm, slab_ref),
            )
        )
    ]
    barrier = pltpu.get_barrier_semaphore()
    for d in range(1, count):
        pl.semaphore_signal(
            barrier, inc=1, device_id={"row": lax.rem(me + d, count)}, device_id_type=pl.DeviceIdType.MESH
        )
    for copy in inputs:
        copy.start()
    read_map.start()
    local[...] = jnp.zeros_like(local)
    for copy in inputs:
        copy.wait()
    for k, ref in enumerate((theta_ref, lon_ref, ratio_ref, comp_ref, weight_ref, seen_ref)):
        local[pl.ds(k, 1), pl.ds(0, half)] = ref[...].astype(F32).reshape(1, half)
    pl.semaphore_wait(barrier, count - 1)

    def send(d):
        return pltpu.make_async_remote_copy(
            src_ref=local, dst_ref=everyone.at[me], send_sem=send_sem.at[d], recv_sem=recv_sem.at[d],
            device_id={"row": lax.rem(me + d, count)}, device_id_type=pl.DeviceIdType.MESH,
        )

    def receive(d):
        return pltpu.make_async_remote_copy(
            src_ref=local, dst_ref=everyone.at[lax.rem(me + count - d, count)],
            send_sem=send_sem.at[d], recv_sem=recv_sem.at[d],
            device_id={"row": lax.rem(me + d, count)}, device_id_type=pl.DeviceIdType.MESH,
        )

    for d in range(1, count):
        send(d).start()
    everyone[me] = local[...]
    read_map.wait()
    lanes = lax.broadcasted_iota(I32, (1, 128), 1)
    for t in range((rows + width) // 128):
        ref, at = (map_buf, t * 128) if t * 128 < rows else (slab_ref, t * 128 - rows)
        part = [ref[pl.ds(k, 1), pl.ds(at, 128)] for k in range(3)]
        key_buf[pl.ds(t, 1), :] = row_key(part[0], part[1], part[2], lanes + t * 128)
    place = lax.broadcasted_iota(I32, key_buf.shape, 0) * 128 + lax.broadcasted_iota(I32, key_buf.shape, 1)
    key = sort_keys(jnp.where(place < rows + width, key_buf[...], (31 << 26) | place))
    facts = list_facts(key[: number_ref.shape[0]], rows + width)
    outs = (number_ref, value_ref, target_ref, grow_ref)
    for ref, value in zip(outs, facts):
        ref[...] = value
    for d in range(1, count):
        receive(d).wait_recv()
    left = lax.broadcasted_iota(I32, (8, 128), 1) < half
    for c in range(PARTS):
        merged = jnp.where(left, everyone[2 * c], pltpu.roll(everyone[2 * c + 1], half, 1))
        params_ref[pl.ds(c, 8, stride=8), :] = merged
    for d in range(1, count):
        send(d).wait_send()


def kernel(
    col_ref, blocks_ref, number_hbm, value_hbm, target_hbm, grow_hbm,
    params_ref, table_hbm, inv_ref, logs_ref, right_ref, normal_ref,
    out_ref, right_out_ref,
    number_ref, value_ref, target_ref, grow_ref,
    value_buf, scale_buf, harm_buf, radial_buf, design_buf, seed_buf, level_buf, square_buf, table_ref,
    slab_hi, slab_lo, in_buf, out_buf, list_sem, in_sem, out_sem,
):
    rows, width = normal_ref.shape
    chunks = rows // CHUNK

    lists = [
        pltpu.make_async_copy(src, dst, list_sem.at[k])
        for k, (src, dst) in enumerate(
            (
                (number_hbm, number_ref),
                (value_hbm, value_ref),
                (target_hbm, target_ref),
                (grow_hbm, grow_ref),
                (table_hbm, table_ref),
            )
        )
    ]
    for copy in lists:
        copy.start()

    def fetch(index, slot):
        return pltpu.make_async_copy(
            normal_ref.at[pl.ds(pl.multiple_of(index * CHUNK, CHUNK), CHUNK)], in_buf.at[slot], in_sem.at[slot]
        )

    def put(index, slot):
        return pltpu.make_async_copy(
            out_buf.at[slot], out_ref.at[pl.ds(pl.multiple_of(index * CHUNK, CHUNK), CHUNK)], out_sem.at[slot]
        )


    def param(k):
        return params_ref[pl.ds(8 * k, 8), :]

    theta = param(0)
    lon = param(1)
    cos_t = jnp.cos(theta)
    sin_t = jnp.sin(theta)
    log_s = jnp.log(sin_t)
    comp = param(3)
    weight = param(4)
    scaled = weight * param(5)
    part0 = jnp.where(comp == 2.0, 1.0, jnp.where(comp == 1.0, 0.0, -1.0))
    part1 = jnp.where(comp == 2.0, 0.0, jnp.where(comp == 1.0, 1.0, -1.0))
    part1q = part1 / (sin_t * sin_t)
    inv_r = 1.0 / param(2)

    def spread(values, c):
        return jnp.broadcast_to(values[c : c + 1, :], (8, 128))

    twice = [spread(2.0 * cos_t, c) for c in range(PARTS)]
    logs = [spread(log_s, c) for c in range(PARTS)]
    subf = lax.broadcasted_iota(I32, (8, 128), 0).astype(F32)

    c1 = jnp.cos(lon)
    s1 = jnp.sin(lon)
    cs = [jnp.ones_like(c1)]
    sn = [jnp.zeros_like(c1)]
    for _ in range(8):
        cs.append(cs[-1] * c1 - sn[-1] * s1)
        sn.append(sn[-1] * c1 + cs[-2] * s1)
    c8, s8 = cs[8], sn[8]
    powers = [inv_r * inv_r * inv_r]
    step_r = inv_r
    for _ in range(7):
        powers.append(powers[-1] * inv_r)
    for _ in range(3):
        step_r = step_r * step_r

    def fill(block, carry):
        cc, ss, pw = carry
        base = block * 8
        for j in range(8):
            nf = (base + j).astype(F32)
            square = nf * nf
            harm_buf[pl.ds(pl.multiple_of(base * 32, 32) + j * 32, 8), :] = cc[j]
            harm_buf[pl.ds(pl.multiple_of(base * 32, 32) + j * 32 + 8, 8), :] = cc[j] * square
            harm_buf[pl.ds(pl.multiple_of(base * 32, 32) + j * 32 + 16, 8), :] = ss[j]
            harm_buf[pl.ds(pl.multiple_of(base * 32, 32) + j * 32 + 24, 8), :] = ss[j] * square
            inv_d = 1.0 / ((nf + 1.0) * (nf + 2.0))
            g = pw[j] * part1q * inv_d
            u = (cos_t * g) * (2.0 / (2.0 * nf - 1.0))
            radial_buf[pl.ds(pl.multiple_of(base * 32, 32) + j * 32, 8), :] = pw[j] * (part0 - part1 * ((2.0 * nf + 1.0) * inv_d)) + nf * g
            radial_buf[pl.ds(pl.multiple_of(base * 32, 32) + j * 32 + 8, 8), :] = g
            radial_buf[pl.ds(pl.multiple_of(base * 32, 32) + j * 32 + 16, 8), :] = u * square
            radial_buf[pl.ds(pl.multiple_of(base * 32, 32) + j * 32 + 24, 8), :] = u
        orders = subf + base.astype(F32)
        diag = logs_ref[pl.ds(pl.multiple_of(base, 8), 8), :]
        square = orders * orders - 0.25
        square_buf[pl.ds(pl.multiple_of(base, 8), 8), :] = square
        before = -1.0 / (1.0 - square * inv_ref[pl.ds(pl.multiple_of(base, 8), 8), :])
        for c in range(PARTS):
            log_seed = diag + orders * logs[c]
            level = jnp.minimum(jnp.ceil(log_seed * (1.0 / LOG_BIG)), 0.0)
            at = pl.multiple_of(block * 64, 64) + c * 8
            seed_buf[pl.ds(at, 8), :] = jnp.exp(log_seed - level * LOG_BIG) * before
            level_buf[pl.ds(at, 8), :] = level * 64.0
        return (
            tuple(cc[j] * c8 - ss[j] * s8 for j in range(8)),
            tuple(ss[j] * c8 + cc[j] * s8 for j in range(8)),
            tuple(pw[j] * step_r for j in range(8)),
        )

    lax.fori_loop(0, GROUPS, fill, (tuple(cs[:8]), tuple(sn[:8]), tuple(powers)))

    for copy in lists:
        copy.wait()
    for k in range(BUFS):
        fetch(k, k).start()

    def make_row(j):
        values = value_ref[j]
        targets = target_ref[j]
        at = values >> 16
        now = value_buf[pl.ds(at, 8, stride=PITCH), :]
        past = value_buf[pl.ds(at - WIDE, 8, stride=PITCH), :]
        scale = scale_buf[pl.ds(number_ref[j] & 65535, 8, stride=PITCH), :]
        n = pl.multiple_of(targets >> 16, 32)
        h = pl.multiple_of(values & 65535, 16)
        kept = now * radial_buf[pl.ds(n, 8), :] - past * radial_buf[pl.ds(n + 16, 8), :]
        spun = now * radial_buf[pl.ds(n + 8, 8), :] - past * radial_buf[pl.ds(n + 24, 8), :]
        body = harm_buf[pl.ds(h, 8), :] * kept - harm_buf[pl.ds(h + 8, 8), :] * spun
        design_buf[pl.ds(targets & 65535, 8), :] = body * (scale * grow_ref[j])

    def drain(cursor, number):
        def more(at):
            return number_ref[at] < ((number + 1) << 16)

        def piece(at):
            for u in range(DRAIN):
                make_row(at + u)
            return at + passed(at, number + 1)

        return lax.while_loop(more, piece, cursor)

    def passed(at, number):
        done = jnp.int32(0)
        for half in (8, 4, 2, 1, 1):
            done = done + jnp.where(number_ref[at + done + (half - 1)] < (number << 16), half, 0)
        return done

    zero = jnp.zeros((8, 128), F32)

    def block_step(number, state, cursor):
        one, two, levels = [list(x) for x in state]
        order = blocks_ref[number]
        first = blocks_ref[STEPS + number]
        ring = number & (RING - 1)
        at_scale = ring * WIDE
        at_value = ring * (SLOT * WIDE)
        at_seed = pl.multiple_of(order * 8, 64)
        opens = jnp.broadcast_to(order == first, (8, 128))
        sigma = table_ref[pl.ds(pl.multiple_of(number * 8, 8), 8), :]
        sigma_small = sigma * SMALL
        limit = 64.0 / sigma
        squares = square_buf[pl.ds(pl.multiple_of(order, 8), 8), :]
        for c in range(PARTS):
            big = jnp.abs(one[c]) > limit
            factor = jnp.where(big, sigma_small, sigma)
            one[c] = one[c] * factor
            two[c] = jnp.where(opens, seed_buf[pl.ds(at_seed + c * 8, 8), :], two[c] * factor)
            level = levels[c] + jnp.where(big, 64.0, 0.0)
            levels[c] = jnp.where(opens, level_buf[pl.ds(at_seed + c * 8, 8), :], level)
            value_buf[pl.ds(at_value + c * PITCH, 8), :] = one[c]
        for i in range(STEP):
            if i % BATCH == 0:
                for k in range(i * PACE // STEP, (i + BATCH) * PACE // STEP):
                    make_row(cursor + k)
            rho = 1.0 - squares * inv_ref[pl.ds(first + i, 8), :]
            fresh = [twice[c] * one[c] - rho * two[c] for c in range(PARTS)]
            for c in range(PARTS):
                value_buf[pl.ds(at_value + (1 + i) * WIDE + c * PITCH, 8), :] = fresh[c]
            one, two = fresh, one
        for c in range(PARTS):
            scale_buf[pl.ds(at_scale + c * PITCH, 8), :] = jnp.exp2(levels[c])
        return tuple(one), tuple(two), tuple(levels)

    def body(index, carry):
        state, cursor = carry
        number = index * BODY
        cursor = drain(cursor, number + BODY - 1 - RING)
        for k in range(BODY):
            state = block_step(number + k, state, cursor)
            cursor = cursor + passed(cursor, number + k)
        return state, cursor

    still = tuple((zero,) * PARTS for _ in range(3))
    _, cursor = lax.fori_loop(0, STEPS // BODY, body, (still, jnp.int32(0)))
    cursor = drain(cursor, BLOCKS)

    def clear(piece, _):
        for u in range(DRAIN):
            design_buf[pl.ds(target_ref[cursor + piece * DRAIN + u] & 65535, 8), :] = zero
        return 0

    lax.fori_loop(0, (rows + width - cursor + DRAIN - 1) // DRAIN, clear, 0)

    def entries(first, count, c):
        return design_buf[pl.ds(first * PITCH + c, count, stride=PITCH), :]

    peak = jnp.full((8, 128), 1e-30, F32)
    for c in range(PARTS):
        block = jnp.abs(entries(rows, width, c) * weight[c : c + 1, :])
        peak = jnp.maximum(peak, jnp.max(block.reshape(width // 8, 8, 128), axis=0))
    peak = jnp.max(peak, axis=(0, 1), keepdims=True)
    shrink = jnp.exp2(jnp.ceil(jnp.log2(jnp.broadcast_to(peak, (8, 128)))) - 7.0)[0:1, :]
    grow = 1.0 / shrink
    for c in range(PARTS):
        for half in range(width // 256):
            block = entries(rows + half * 256, 256, c)
            block = (block * weight[c : c + 1, :]).T
            hi = block.astype(BF16)
            lo = block - hi.astype(F32)
            cols = pl.ds(half * 256, 256)
            factor = jnp.concatenate([grow, grow], axis=1)
            slab_hi[pl.ds(c * 128, 128), cols] = hi
            slab_lo[pl.ds(c * 128, 128), cols] = (block * factor).astype(F8)
            slab_lo[pl.ds(OBS + c * 128, 128), cols] = (lo * (factor * 512.0)).astype(F8)
    shrink = jnp.concatenate([shrink] * (width // 128), axis=1) * (1.0 / 512.0)

    own = right_ref.shape[0]
    total = jnp.zeros((own, 128), F32)
    at = col_ref[0] * own
    for c in range(PARTS):
        total = total + entries(at, own, c) * scaled[c : c + 1, :]
    summed = lax.dot_general(
        jnp.ones((8, 128), F32), total, (((1,), (1,)), ((), ())),
        precision=lax.Precision.HIGHEST, preferred_element_type=F32,
    )
    right_out_ref[...] = right_ref[...] + summed[0:1, :].reshape(own)

    def chunk_body(index, _):
        slot = lax.rem(index, BUFS)
        his = []
        los = []
        tops = []
        for c in range(PARTS):
            x = entries(index * CHUNK, CHUNK, c)
            hi = x.astype(BF16)
            his.append(hi)
            los.append(((x - hi.astype(F32)) * 512.0).astype(F8))
            tops.append(x.astype(F8))
        update = jnp.dot(jnp.concatenate(los + tops, axis=1), slab_lo[...], preferred_element_type=F32) * shrink
        update += jnp.dot(jnp.concatenate(his, axis=1), slab_hi[...], preferred_element_type=F32)
        fetch(index, slot).wait()

        @pl.when(index >= BUFS)
        def _():
            put(index - BUFS, slot).wait()

        out_buf[slot] = in_buf[slot] + update
        put(index, slot).start()

        @pl.when(index + BUFS < chunks)
        def _():
            fetch(index + BUFS, slot).start()

        return 0

    lax.fori_loop(0, chunks, chunk_body, 0)
    for k in range(BUFS):
        put(chunks - BUFS + k, k).wait()


def local_update(params, col, facts, normal_slab, right_side):
    rows, width = normal_slab.shape
    own = right_side.shape[0]
    entries = facts[0].shape[0]
    smem = pl.BlockSpec(memory_space=pltpu.SMEM)
    vmem = pl.BlockSpec(memory_space=pltpu.VMEM)
    hbm = pl.BlockSpec(memory_space=pltpu.HBM)
    return pl.pallas_call(
        kernel,
        out_shape=(
            jax.ShapeDtypeStruct((rows, width), F32),
            jax.ShapeDtypeStruct((own,), F32),
        ),
        in_specs=[smem] * 2 + [hbm] * 4 + [vmem, hbm, vmem, vmem, vmem, hbm],
        out_specs=(hbm, vmem),
        scratch_shapes=[pltpu.SMEM((entries,), I32)] * 3
        + [pltpu.SMEM((entries,), F32)]
        + [
            pltpu.VMEM((RING * SLOT * WIDE, 128), F32),
            pltpu.VMEM((RING * WIDE, 128), F32),
            pltpu.VMEM((TOP * 32, 128), F32),
            pltpu.VMEM((TOP * 32, 128), F32),
            pltpu.VMEM(((rows + width + 1) * PITCH, 128), F32),
            pltpu.VMEM((GROUPS * 64, 128), F32),
            pltpu.VMEM((GROUPS * 64, 128), F32),
            pltpu.VMEM((TOP, 128), F32),
            pltpu.VMEM((STEPS * 8, 128), F32),
            pltpu.VMEM((OBS, width), BF16),
            pltpu.VMEM((2 * OBS, width), F8),
            pltpu.VMEM((BUFS, CHUNK, width), F32),
            pltpu.VMEM((BUFS, CHUNK, width), F32),
            pltpu.SemaphoreType.DMA((5,)),
            pltpu.SemaphoreType.DMA((BUFS,)),
            pltpu.SemaphoreType.DMA((BUFS,)),
        ],
        compiler_params=pltpu.CompilerParams(vmem_limit_bytes=62 * 1024 * 1024),
        name="normal_update",
    )(
        col, jnp.asarray(block_lists()), *facts, params, jnp.asarray(block_scales()), jnp.asarray(inverse_squares()),
        jnp.asarray(diagonal_logs()), right_side, normal_slab,
    )


def on_device(
    colatitude, longitude, radius_ratio, component, obs_weight, observed,
    unknown_map, slab_map, normal_slab, right_side,
):
    rows, width = normal_slab.shape
    col = lax.axis_index("col").astype(I32).reshape(1)
    entries = -(-(rows + width + 2 * PACE) // 1024) * 1024
    total = 1 << (rows + width - 1).bit_length()
    shape = (entries // 128, 128)
    count = lax.axis_size("row")
    vmem = pl.BlockSpec(memory_space=pltpu.VMEM)
    outs = pl.pallas_call(
        gather_kernel,
        out_shape=tuple(jax.ShapeDtypeStruct(shape, I32) for _ in range(3))
        + (jax.ShapeDtypeStruct(shape, F32), jax.ShapeDtypeStruct((64, 128), F32)),
        in_specs=[pl.BlockSpec(memory_space=pltpu.HBM)] * 8,
        out_specs=(vmem,) * 5,
        scratch_shapes=[
            pltpu.VMEM(colatitude.shape, F32),
            pltpu.VMEM(colatitude.shape, F32),
            pltpu.VMEM(colatitude.shape, F32),
            pltpu.VMEM(colatitude.shape, I32),
            pltpu.VMEM(colatitude.shape, F32),
            pltpu.VMEM(colatitude.shape, F32),
            pltpu.VMEM(slab_map.shape, I32),
            pltpu.VMEM((8, 128), F32),
            pltpu.VMEM((count, 8, 128), F32),
            pltpu.VMEM((3, rows), I32),
            pltpu.VMEM((total // 128, 128), I32),
            pltpu.SemaphoreType.DMA((count,)),
            pltpu.SemaphoreType.DMA((count,)),
            pltpu.SemaphoreType.DMA((1,)),
            pltpu.SemaphoreType.DMA((7,)),
        ],
        compiler_params=pltpu.CompilerParams(collective_id=0, has_side_effects=True),
        name="gather_observations",
    )(colatitude, longitude, radius_ratio, component, obs_weight, observed, unknown_map, slab_map)
    facts = tuple(x.reshape(entries) for x in outs[:4])
    return local_update(outs[4], col, facts, normal_slab, right_side)


def solution(mesh):
    return jax.shard_map(
        on_device,
        mesh=mesh,
        in_specs=(
            P("row"), P("row"), P("row"), P("row"), P("row"), P("row"),
            P(), P(None, "col"), P("row", "col"), P(("row", "col")),
        ),
        out_specs=(P("row", "col"), P(("row", "col"))),
        check_vma=False,
    )
```

```python
import jax
import jax.numpy as jnp
import numpy as np
from jax import lax
from jax.experimental import pallas as pl
from jax.experimental.pallas import tpu as pltpu
from jax.sharding import PartitionSpec as P

NMAX = 300
TOP = 304
GROUP = 8
GROUPS = TOP // GROUP
STEP = 16
SLOT = STEP + 1
PITCH = 9
WIDE = 8 * PITCH
RING = 8
BUFS = 2
OBS = 1024
PARTS = 8
CHUNK = 768
PACE = 16
BATCH = 2
DRAIN = 16
BODY = 5
LATE = 1 << 14
BIG = float(2.0**64)
SMALL = float(2.0**-64)
LOG_BIG = float(64.0 * np.log(2.0))
F32 = jnp.float32
BF16 = jnp.bfloat16
F8 = jnp.float8_e4m3fn
I32 = jnp.int32


def blocks_of(group):
    return (NMAX + STEP - group * GROUP) // STEP


def diagonal_logs():
    counter = np.arange(1, TOP, dtype=np.float64)
    steps = 0.5 * np.log((2.0 * counter + 1.0) / (2.0 * counter))
    logs = np.concatenate([[0.0], 0.5 * np.log(2.0) + np.cumsum(steps)])
    return np.broadcast_to(logs[:, None], (TOP, 128)).astype(np.float32)


def block_scales():
    table = []
    for group in range(GROUPS):
        order = (group * GROUP + np.arange(GROUP, dtype=np.float64))[:, None]
        for block in range(blocks_of(group)):
            sigma = np.zeros((GROUP, 1))
            if block > 0:
                degree = order + STEP * (block - 1) + np.arange(STEP)[None, :]
                ratio = (degree**2 - order**2) / (degree**2 - 0.25)
                if block == 1:
                    ratio[:, 0] = 1.0
                sigma = 1.0 / np.sqrt(np.prod(ratio, axis=1, keepdims=True))
            table.append(np.broadcast_to(sigma, (GROUP, 128)))
    table += [np.zeros((GROUP, 128))] * (STEPS - len(table))
    return np.concatenate(table, axis=0).astype(np.float32)


def inverse_squares():
    degree = np.arange(TOP + 2 * STEP, dtype=np.float64)[:, None] - 1.0
    return np.broadcast_to(1.0 / (degree * degree - 0.25), (TOP + 2 * STEP, 128)).astype(np.float32)


BLOCKS = sum(blocks_of(group) for group in range(GROUPS))
STEPS = -(-BLOCKS // BODY) * BODY


def block_lists():
    lists = np.zeros((2, STEPS), np.int32)
    at = 0
    for group in range(GROUPS):
        for block in range(blocks_of(group)):
            lists[:, at] = group * GROUP, group * GROUP + block * STEP
            at += 1
    return lists.reshape(-1)


def row_key(degree, order, kind, place):
    beyond = degree - order
    key = (
        (((order >> 3) - 32) << 26)
        | ((beyond >> 4) << 21)
        | ((beyond & 15) << 17)
        | ((order & 7) << 14)
        | (kind << 13)
        | place
    )
    return jnp.where(kind == 2, (31 << 26) | place, key)


def sort_keys(key, turn):
    height = key.shape[0]
    total = height * 128
    row = lax.broadcasted_iota(I32, key.shape, 0)
    lane = lax.broadcasted_iota(I32, key.shape, 1)
    index = lane * height + row
    size = 2
    while size <= total:
        rising = (index & size) == 0
        stride = size // 2
        while stride >= 1:
            low = (index & stride) == 0
            if stride < height:
                ahead, behind = pltpu.roll(key, height - stride, 0), pltpu.roll(key, stride, 0)
            else:
                ahead, behind = pltpu.roll(key, 128 - stride // height, 1), pltpu.roll(key, stride // height, 1)
            other = jnp.where(low, ahead, behind)
            key = jnp.where(low == rising, jnp.minimum(key, other), jnp.maximum(key, other))
            stride //= 2
        size *= 2
    columns = key.T
    turn[...] = jnp.concatenate([columns, columns], axis=1)
    return jnp.where(lane < height, turn[pl.ds(0, height, stride=2), :], turn[pl.ds(1, height, stride=2), :])


def list_facts(key, limit):
    group = (key >> 26) + 32
    used = group < GROUPS
    group = jnp.where(used, group, 0)
    block = jnp.where(used, (key >> 21) & 31, 0)
    step = jnp.where(used, (key >> 17) & 15, 2)
    lane = jnp.where(used, (key >> 14) & 7, 0)
    kind = jnp.where(used, (key >> 13) & 1, 0)
    place = jnp.minimum(key & 8191, limit)
    order = group * GROUP + lane
    degree = order + block * STEP + step
    number = 19 * group - (((group - 1) * (group - 1)) >> 2) + block
    ring = number & (RING - 1)
    number = jnp.where(used, number, LATE)
    at_value = (ring * SLOT + 1 + step) * WIDE + lane
    at_scale = ring * WIDE + lane
    target = place * PITCH
    m = order.astype(F32)
    first = degree - step
    product = jnp.ones_like(m)
    for q in range(STEP):
        j = first + q
        jf = j.astype(F32)
        ratio = (jf * jf - m * m) / (jf * jf - 0.25)
        product = jnp.where((j > order) & (j <= degree), product * ratio, product)
    at_harm = (order * 2 + kind) * 16
    return (number << 16) | at_scale, (at_value << 16) | at_harm, (degree << 21) | target, lax.rsqrt(product)


def gather_kernel(
    theta_hbm, lon_hbm, ratio_hbm, comp_hbm, weight_hbm, seen_hbm, unknown_ref, slab_hbm,
    number_ref, value_ref, target_ref, grow_ref, params_ref,
    theta_ref, lon_ref, ratio_ref, comp_ref, weight_ref, seen_ref, slab_ref,
    local, everyone, map_buf, key_buf, turn, send_sem, recv_sem, map_sem, in_sem,
):
    me = lax.axis_index("row")
    count = everyone.shape[0]
    half = theta_ref.shape[0]
    rows = map_buf.shape[1]
    width = slab_ref.shape[1]
    read_map = pltpu.make_async_copy(
        unknown_ref.at[:, pl.ds(pl.multiple_of(me * rows, 128), rows)], map_buf, map_sem.at[0]
    )
    inputs = [
        pltpu.make_async_copy(src, dst, in_sem.at[k])
        for k, (src, dst) in enumerate(
            (
                (theta_hbm, theta_ref),
                (lon_hbm, lon_ref),
                (ratio_hbm, ratio_ref),
                (comp_hbm, comp_ref),
                (weight_hbm, weight_ref),
                (seen_hbm, seen_ref),
                (slab_hbm, slab_ref),
            )
        )
    ]
    barrier = pltpu.get_barrier_semaphore()
    for d in range(1, count):
        pl.semaphore_signal(
            barrier, inc=1, device_id={"row": lax.rem(me + d, count)}, device_id_type=pl.DeviceIdType.MESH
        )
    for copy in inputs:
        copy.start()
    read_map.start()
    local[...] = jnp.zeros_like(local)
    for copy in inputs:
        copy.wait()
    for k, ref in enumerate((theta_ref, lon_ref, ratio_ref, comp_ref, weight_ref, seen_ref)):
        local[pl.ds(k, 1), pl.ds(0, half)] = ref[...].astype(F32).reshape(1, half)
    pl.semaphore_wait(barrier, count - 1)

    def send(d):
        return pltpu.make_async_remote_copy(
            src_ref=local, dst_ref=everyone.at[me], send_sem=send_sem.at[d], recv_sem=recv_sem.at[d],
            device_id={"row": lax.rem(me + d, count)}, device_id_type=pl.DeviceIdType.MESH,
        )

    def receive(d):
        return pltpu.make_async_remote_copy(
            src_ref=local, dst_ref=everyone.at[lax.rem(me + count - d, count)],
            send_sem=send_sem.at[d], recv_sem=recv_sem.at[d],
            device_id={"row": lax.rem(me + d, count)}, device_id_type=pl.DeviceIdType.MESH,
        )

    for d in range(1, count):
        send(d).start()
    everyone[me] = local[...]
    read_map.wait()
    lanes = lax.broadcasted_iota(I32, (1, 128), 1)
    for t in range((rows + width) // 128):
        ref, at = (map_buf, t * 128) if t * 128 < rows else (slab_ref, t * 128 - rows)
        part = [ref[pl.ds(k, 1), pl.ds(at, 128)] for k in range(3)]
        key_buf[pl.ds(t, 1), :] = row_key(part[0], part[1], part[2], lanes + t * 128)
    place = lax.broadcasted_iota(I32, key_buf.shape, 0) * 128 + lax.broadcasted_iota(I32, key_buf.shape, 1)
    key = sort_keys(jnp.where(place < rows + width, key_buf[...], (31 << 26) | place), turn)
    facts = list_facts(key[: number_ref.shape[0]], rows + width)
    outs = (number_ref, value_ref, target_ref, grow_ref)
    for ref, value in zip(outs, facts):
        ref[...] = value
    for d in range(1, count):
        receive(d).wait_recv()
    left = lax.broadcasted_iota(I32, (8, 128), 1) < half
    for c in range(PARTS):
        merged = jnp.where(left, everyone[2 * c], pltpu.roll(everyone[2 * c + 1], half, 1))
        params_ref[pl.ds(c, 8, stride=8), :] = merged
    for d in range(1, count):
        send(d).wait_send()


def kernel(
    col_ref, blocks_ref, number_hbm, value_hbm, target_hbm, grow_hbm,
    params_ref, table_hbm, inv_ref, logs_ref, right_ref, normal_ref,
    out_ref, right_out_ref,
    number_ref, value_ref, target_ref, grow_ref,
    value_buf, scale_buf, harm_buf, radial_buf, design_buf, seed_buf, level_buf, square_buf, table_ref,
    slab_hi, slab_lo, in_buf, out_buf, list_sem, in_sem, out_sem,
):
    rows, width = normal_ref.shape
    chunks = rows // CHUNK

    lists = [
        pltpu.make_async_copy(src, dst, list_sem.at[k])
        for k, (src, dst) in enumerate(
            (
                (number_hbm, number_ref),
                (value_hbm, value_ref),
                (target_hbm, target_ref),
                (grow_hbm, grow_ref),
                (table_hbm, table_ref),
            )
        )
    ]
    for copy in lists:
        copy.start()

    def fetch(index, slot):
        return pltpu.make_async_copy(
            normal_ref.at[pl.ds(pl.multiple_of(index * CHUNK, CHUNK), CHUNK)], in_buf.at[slot], in_sem.at[slot]
        )

    def put(index, slot):
        return pltpu.make_async_copy(
            out_buf.at[slot], out_ref.at[pl.ds(pl.multiple_of(index * CHUNK, CHUNK), CHUNK)], out_sem.at[slot]
        )


    def param(k):
        return params_ref[pl.ds(8 * k, 8), :]

    theta = param(0)
    lon = param(1)
    cos_t = jnp.cos(theta)
    sin_t = jnp.sin(theta)
    log_s = jnp.log(sin_t)
    comp = param(3)
    weight = param(4)
    scaled = weight * param(5)
    part0 = jnp.where(comp == 2.0, 1.0, jnp.where(comp == 1.0, 0.0, -1.0))
    part1 = jnp.where(comp == 2.0, 0.0, jnp.where(comp == 1.0, 1.0, -1.0))
    part1q = part1 / (sin_t * sin_t)
    inv_r = 1.0 / param(2)

    def spread(values, c):
        return jnp.broadcast_to(values[c : c + 1, :], (8, 128))

    twice = [spread(2.0 * cos_t, c) for c in range(PARTS)]
    logs = [spread(log_s, c) for c in range(PARTS)]
    subf = lax.broadcasted_iota(I32, (8, 128), 0).astype(F32)

    c1 = jnp.cos(lon)
    s1 = jnp.sin(lon)
    cs = [jnp.ones_like(c1)]
    sn = [jnp.zeros_like(c1)]
    for _ in range(8):
        cs.append(cs[-1] * c1 - sn[-1] * s1)
        sn.append(sn[-1] * c1 + cs[-2] * s1)
    c8, s8 = cs[8], sn[8]
    powers = [inv_r * inv_r * inv_r]
    step_r = inv_r
    for _ in range(7):
        powers.append(powers[-1] * inv_r)
    for _ in range(3):
        step_r = step_r * step_r

    def fill(block, carry):
        cc, ss, pw = carry
        base = block * 8
        for j in range(8):
            nf = (base + j).astype(F32)
            square = nf * nf
            harm_buf[pl.ds(pl.multiple_of(base * 32, 32) + j * 32, 8), :] = cc[j]
            harm_buf[pl.ds(pl.multiple_of(base * 32, 32) + j * 32 + 8, 8), :] = cc[j] * square
            harm_buf[pl.ds(pl.multiple_of(base * 32, 32) + j * 32 + 16, 8), :] = ss[j]
            harm_buf[pl.ds(pl.multiple_of(base * 32, 32) + j * 32 + 24, 8), :] = ss[j] * square
            inv_d = 1.0 / ((nf + 1.0) * (nf + 2.0))
            g = pw[j] * part1q * inv_d
            u = (cos_t * g) * (2.0 / (2.0 * nf - 1.0))
            radial_buf[pl.ds(pl.multiple_of(base * 32, 32) + j * 32, 8), :] = pw[j] * (part0 - part1 * ((2.0 * nf + 1.0) * inv_d)) + nf * g
            radial_buf[pl.ds(pl.multiple_of(base * 32, 32) + j * 32 + 8, 8), :] = g
            radial_buf[pl.ds(pl.multiple_of(base * 32, 32) + j * 32 + 16, 8), :] = u * square
            radial_buf[pl.ds(pl.multiple_of(base * 32, 32) + j * 32 + 24, 8), :] = u
        orders = subf + base.astype(F32)
        diag = logs_ref[pl.ds(pl.multiple_of(base, 8), 8), :]
        square = orders * orders - 0.25
        square_buf[pl.ds(pl.multiple_of(base, 8), 8), :] = square
        before = -1.0 / (1.0 - square * inv_ref[pl.ds(pl.multiple_of(base, 8), 8), :])
        for c in range(PARTS):
            log_seed = diag + orders * logs[c]
            level = jnp.minimum(jnp.ceil(log_seed * (1.0 / LOG_BIG)), 0.0)
            at = pl.multiple_of(block * 64, 64) + c * 8
            seed_buf[pl.ds(at, 8), :] = jnp.exp(log_seed - level * LOG_BIG) * before
            level_buf[pl.ds(at, 8), :] = level * 64.0
        return (
            tuple(cc[j] * c8 - ss[j] * s8 for j in range(8)),
            tuple(ss[j] * c8 + cc[j] * s8 for j in range(8)),
            tuple(pw[j] * step_r for j in range(8)),
        )

    lax.fori_loop(0, GROUPS, fill, (tuple(cs[:8]), tuple(sn[:8]), tuple(powers)))

    for copy in lists:
        copy.wait()
    for k in range(BUFS):
        fetch(k, k).start()

    def make_row(j):
        values = value_ref[j]
        targets = target_ref[j]
        at = values >> 16
        now = value_buf[pl.ds(at, 8, stride=PITCH), :]
        past = value_buf[pl.ds(at - WIDE, 8, stride=PITCH), :]
        scale = scale_buf[pl.ds(number_ref[j] & 65535, 8, stride=PITCH), :]
        n = pl.multiple_of(targets >> 16, 32)
        h = pl.multiple_of(values & 65535, 16)
        kept = now * radial_buf[pl.ds(n, 8), :] - past * radial_buf[pl.ds(n + 16, 8), :]
        spun = now * radial_buf[pl.ds(n + 8, 8), :] - past * radial_buf[pl.ds(n + 24, 8), :]
        body = harm_buf[pl.ds(h, 8), :] * kept - harm_buf[pl.ds(h + 8, 8), :] * spun
        design_buf[pl.ds(targets & 65535, 8), :] = body * (scale * grow_ref[j])

    def drain(cursor, number):
        def more(at):
            return number_ref[at] < ((number + 1) << 16)

        def piece(at):
            for u in range(DRAIN):
                make_row(at + u)
            return at + passed(at, number + 1)

        return lax.while_loop(more, piece, cursor)

    def passed(at, number):
        done = jnp.int32(0)
        for half in (8, 4, 2, 1, 1):
            done = done + jnp.where(number_ref[at + done + (half - 1)] < (number << 16), half, 0)
        return done

    zero = jnp.zeros((8, 128), F32)

    def block_step(number, state, cursor):
        one, two, levels = [list(x) for x in state]
        order = blocks_ref[number]
        first = blocks_ref[STEPS + number]
        ring = number & (RING - 1)
        at_scale = ring * WIDE
        at_value = ring * (SLOT * WIDE)
        at_seed = pl.multiple_of(order * 8, 64)
        opens = jnp.broadcast_to(order == first, (8, 128))
        sigma = table_ref[pl.ds(pl.multiple_of(number * 8, 8), 8), :]
        sigma_small = sigma * SMALL
        limit = 64.0 / sigma
        squares = square_buf[pl.ds(pl.multiple_of(order, 8), 8), :]
        for c in range(PARTS):
            big = jnp.abs(one[c]) > limit
            factor = jnp.where(big, sigma_small, sigma)
            one[c] = one[c] * factor
            two[c] = jnp.where(opens, seed_buf[pl.ds(at_seed + c * 8, 8), :], two[c] * factor)
            level = levels[c] + jnp.where(big, 64.0, 0.0)
            levels[c] = jnp.where(opens, level_buf[pl.ds(at_seed + c * 8, 8), :], level)
            value_buf[pl.ds(at_value + c * PITCH, 8), :] = one[c]
        for i in range(STEP):
            if i % BATCH == 0:
                for k in range(i * PACE // STEP, (i + BATCH) * PACE // STEP):
                    make_row(cursor + k)
            rho = 1.0 - squares * inv_ref[pl.ds(first + i, 8), :]
            fresh = [twice[c] * one[c] - rho * two[c] for c in range(PARTS)]
            for c in range(PARTS):
                value_buf[pl.ds(at_value + (1 + i) * WIDE + c * PITCH, 8), :] = fresh[c]
            one, two = fresh, one
        for c in range(PARTS):
            scale_buf[pl.ds(at_scale + c * PITCH, 8), :] = jnp.exp2(levels[c])
        return tuple(one), tuple(two), tuple(levels)

    def body(index, carry):
        state, cursor = carry
        number = index * BODY
        cursor = drain(cursor, number + BODY - 1 - RING)
        for k in range(BODY):
            state = block_step(number + k, state, cursor)
            cursor = cursor + passed(cursor, number + k)
        return state, cursor

    still = tuple((zero,) * PARTS for _ in range(3))
    _, cursor = lax.fori_loop(0, STEPS // BODY, body, (still, jnp.int32(0)))
    cursor = drain(cursor, BLOCKS)

    def clear(piece, _):
        for u in range(DRAIN):
            design_buf[pl.ds(target_ref[cursor + piece * DRAIN + u] & 65535, 8), :] = zero
        return 0

    lax.fori_loop(0, (rows + width - cursor + DRAIN - 1) // DRAIN, clear, 0)

    def entries(first, count, c):
        return design_buf[pl.ds(first * PITCH + c, count, stride=PITCH), :]

    peak = jnp.full((8, 128), 1e-30, F32)
    for c in range(PARTS):
        block = jnp.abs(entries(rows, width, c) * weight[c : c + 1, :])
        peak = jnp.maximum(peak, jnp.max(block.reshape(width // 8, 8, 128), axis=0))
    peak = jnp.max(peak, axis=(0, 1), keepdims=True)
    shrink = jnp.exp2(jnp.ceil(jnp.log2(jnp.broadcast_to(peak, (8, 128)))) - 7.0)[0:1, :]
    grow = 1.0 / shrink
    for c in range(PARTS):
        for half in range(width // 256):
            block = entries(rows + half * 256, 256, c)
            block = (block * weight[c : c + 1, :]).T
            hi = block.astype(BF16)
            lo = block - hi.astype(F32)
            cols = pl.ds(half * 256, 256)
            factor = jnp.concatenate([grow, grow], axis=1)
            slab_hi[pl.ds(c * 128, 128), cols] = hi
            slab_lo[pl.ds(c * 128, 128), cols] = (block * factor).astype(F8)
            slab_lo[pl.ds(OBS + c * 128, 128), cols] = (lo * (factor * 512.0)).astype(F8)
    shrink = jnp.concatenate([shrink] * (width // 128), axis=1) * (1.0 / 512.0)

    own = right_ref.shape[0]
    total = jnp.zeros((own, 128), F32)
    at = col_ref[0] * own
    for c in range(PARTS):
        total = total + entries(at, own, c) * scaled[c : c + 1, :]
    summed = lax.dot_general(
        jnp.ones((8, 128), F32), total, (((1,), (1,)), ((), ())),
        precision=lax.Precision.HIGHEST, preferred_element_type=F32,
    )
    right_out_ref[...] = right_ref[...] + summed[0:1, :].reshape(own)

    def chunk_body(index, _):
        slot = lax.rem(index, BUFS)
        his = []
        los = []
        tops = []
        for c in range(PARTS):
            x = entries(index * CHUNK, CHUNK, c)
            hi = x.astype(BF16)
            his.append(hi)
            los.append(((x - hi.astype(F32)) * 512.0).astype(F8))
            tops.append(x.astype(F8))
        update = jnp.dot(jnp.concatenate(los + tops, axis=1), slab_lo[...], preferred_element_type=F32) * shrink
        update += jnp.dot(jnp.concatenate(his, axis=1), slab_hi[...], preferred_element_type=F32)
        fetch(index, slot).wait()

        @pl.when(index >= BUFS)
        def _():
            put(index - BUFS, slot).wait()

        out_buf[slot] = in_buf[slot] + update
        put(index, slot).start()

        @pl.when(index + BUFS < chunks)
        def _():
            fetch(index + BUFS, slot).start()

        return 0

    lax.fori_loop(0, chunks, chunk_body, 0)
    for k in range(BUFS):
        put(chunks - BUFS + k, k).wait()


def local_update(params, col, facts, normal_slab, right_side):
    rows, width = normal_slab.shape
    own = right_side.shape[0]
    entries = facts[0].shape[0]
    smem = pl.BlockSpec(memory_space=pltpu.SMEM)
    vmem = pl.BlockSpec(memory_space=pltpu.VMEM)
    hbm = pl.BlockSpec(memory_space=pltpu.HBM)
    return pl.pallas_call(
        kernel,
        out_shape=(
            jax.ShapeDtypeStruct((rows, width), F32),
            jax.ShapeDtypeStruct((own,), F32),
        ),
        in_specs=[smem] * 2 + [hbm] * 4 + [vmem, hbm, vmem, vmem, vmem, hbm],
        out_specs=(hbm, vmem),
        scratch_shapes=[pltpu.SMEM((entries,), I32)] * 3
        + [pltpu.SMEM((entries,), F32)]
        + [
            pltpu.VMEM((RING * SLOT * WIDE, 128), F32),
            pltpu.VMEM((RING * WIDE, 128), F32),
            pltpu.VMEM((TOP * 32, 128), F32),
            pltpu.VMEM((TOP * 32, 128), F32),
            pltpu.VMEM(((rows + width + 1) * PITCH, 128), F32),
            pltpu.VMEM((GROUPS * 64, 128), F32),
            pltpu.VMEM((GROUPS * 64, 128), F32),
            pltpu.VMEM((TOP, 128), F32),
            pltpu.VMEM((STEPS * 8, 128), F32),
            pltpu.VMEM((OBS, width), BF16),
            pltpu.VMEM((2 * OBS, width), F8),
            pltpu.VMEM((BUFS, CHUNK, width), F32),
            pltpu.VMEM((BUFS, CHUNK, width), F32),
            pltpu.SemaphoreType.DMA((5,)),
            pltpu.SemaphoreType.DMA((BUFS,)),
            pltpu.SemaphoreType.DMA((BUFS,)),
        ],
        compiler_params=pltpu.CompilerParams(vmem_limit_bytes=62 * 1024 * 1024),
        name="normal_update",
    )(
        col, jnp.asarray(block_lists()), *facts, params, jnp.asarray(block_scales()), jnp.asarray(inverse_squares()),
        jnp.asarray(diagonal_logs()), right_side, normal_slab,
    )


def on_device(
    colatitude, longitude, radius_ratio, component, obs_weight, observed,
    unknown_map, slab_map, normal_slab, right_side,
):
    rows, width = normal_slab.shape
    col = lax.axis_index("col").astype(I32).reshape(1)
    entries = -(-(rows + width + 2 * PACE) // 1024) * 1024
    total = 1 << (rows + width - 1).bit_length()
    shape = (entries // 128, 128)
    count = lax.axis_size("row")
    vmem = pl.BlockSpec(memory_space=pltpu.VMEM)
    outs = pl.pallas_call(
        gather_kernel,
        out_shape=tuple(jax.ShapeDtypeStruct(shape, I32) for _ in range(3))
        + (jax.ShapeDtypeStruct(shape, F32), jax.ShapeDtypeStruct((64, 128), F32)),
        in_specs=[pl.BlockSpec(memory_space=pltpu.HBM)] * 8,
        out_specs=(vmem,) * 5,
        scratch_shapes=[
            pltpu.VMEM(colatitude.shape, F32),
            pltpu.VMEM(colatitude.shape, F32),
            pltpu.VMEM(colatitude.shape, F32),
            pltpu.VMEM(colatitude.shape, I32),
            pltpu.VMEM(colatitude.shape, F32),
            pltpu.VMEM(colatitude.shape, F32),
            pltpu.VMEM(slab_map.shape, I32),
            pltpu.VMEM((8, 128), F32),
            pltpu.VMEM((count, 8, 128), F32),
            pltpu.VMEM((3, rows), I32),
            pltpu.VMEM((total // 128, 128), I32),
            pltpu.VMEM((128, 128), I32),
            pltpu.SemaphoreType.DMA((count,)),
            pltpu.SemaphoreType.DMA((count,)),
            pltpu.SemaphoreType.DMA((1,)),
            pltpu.SemaphoreType.DMA((7,)),
        ],
        compiler_params=pltpu.CompilerParams(collective_id=0, has_side_effects=True),
        name="gather_observations",
    )(colatitude, longitude, radius_ratio, component, obs_weight, observed, unknown_map, slab_map)
    facts = tuple(x.reshape(entries) for x in outs[:4])
    return local_update(outs[4], col, facts, normal_slab, right_side)


def solution(mesh):
    return jax.shard_map(
        on_device,
        mesh=mesh,
        in_specs=(
            P("row"), P("row"), P("row"), P("row"), P("row"), P("row"),
            P(), P(None, "col"), P("row", "col"), P(("row", "col")),
        ),
        out_specs=(P("row", "col"), P(("row", "col"))),
        check_vma=False,
    )
```

```python
import jax
import jax.numpy as jnp
import numpy as np
from jax import lax
from jax.experimental import pallas as pl
from jax.experimental.pallas import tpu as pltpu
from jax.sharding import PartitionSpec as P

NMAX = 300
TOP = 304
GROUP = 8
GROUPS = TOP // GROUP
STEP = 16
SLOT = STEP + 1
PITCH = 9
WIDE = 8 * PITCH
RING = 8
BUFS = 2
OBS = 1024
PARTS = 8
CHUNK = 768
PACE = 16
BATCH = 2
DRAIN = 16
BODY = 5
LATE = 1 << 14
BIG = float(2.0**64)
SMALL = float(2.0**-64)
LOG_BIG = float(64.0 * np.log(2.0))
F32 = jnp.float32
BF16 = jnp.bfloat16
F8 = jnp.float8_e4m3fn
I32 = jnp.int32


def blocks_of(group):
    return (NMAX + STEP - group * GROUP) // STEP


def diagonal_logs():
    counter = np.arange(1, TOP, dtype=np.float64)
    steps = 0.5 * np.log((2.0 * counter + 1.0) / (2.0 * counter))
    logs = np.concatenate([[0.0], 0.5 * np.log(2.0) + np.cumsum(steps)])
    return np.broadcast_to(logs[:, None], (TOP, 128)).astype(np.float32)


def block_scales():
    table = []
    for group in range(GROUPS):
        order = (group * GROUP + np.arange(GROUP, dtype=np.float64))[:, None]
        for block in range(blocks_of(group)):
            sigma = np.zeros((GROUP, 1))
            if block > 0:
                degree = order + STEP * (block - 1) + np.arange(STEP)[None, :]
                ratio = (degree**2 - order**2) / (degree**2 - 0.25)
                if block == 1:
                    ratio[:, 0] = 1.0
                sigma = 1.0 / np.sqrt(np.prod(ratio, axis=1, keepdims=True))
            table.append(np.broadcast_to(sigma, (GROUP, 128)))
    table += [np.zeros((GROUP, 128))] * (STEPS - len(table))
    return np.concatenate(table, axis=0).astype(np.float32)


def inverse_squares():
    degree = np.arange(TOP + 2 * STEP, dtype=np.float64)[:, None] - 1.0
    return np.broadcast_to(1.0 / (degree * degree - 0.25), (TOP + 2 * STEP, 128)).astype(np.float32)


BLOCKS = sum(blocks_of(group) for group in range(GROUPS))
STEPS = -(-BLOCKS // BODY) * BODY


def block_lists():
    lists = np.zeros((2, STEPS), np.int32)
    at = 0
    for group in range(GROUPS):
        for block in range(blocks_of(group)):
            lists[:, at] = group * GROUP, group * GROUP + block * STEP
            at += 1
    return lists.reshape(-1)


def row_key(degree, order, kind, place):
    beyond = degree - order
    key = (
        (((order >> 3) - 32) << 26)
        | ((beyond >> 4) << 21)
        | ((beyond & 15) << 17)
        | ((order & 7) << 14)
        | (kind << 13)
        | place
    )
    return jnp.where(kind == 2, (31 << 26) | place, key)


def sort_keys(key, turn):
    height = key.shape[0]
    total = height * 128
    row = lax.broadcasted_iota(I32, key.shape, 0)
    lane = lax.broadcasted_iota(I32, key.shape, 1)
    index = lane * height + row
    size = 2
    while size <= total:
        rising = (index & size) == 0
        stride = size // 2
        while stride >= 1:
            low = (index & stride) == 0
            if stride < height:
                ahead, behind = pltpu.roll(key, height - stride, 0), pltpu.roll(key, stride, 0)
            else:
                ahead, behind = pltpu.roll(key, 128 - stride // height, 1), pltpu.roll(key, stride // height, 1)
            other = jnp.where(low, ahead, behind)
            key = jnp.where(low == rising, jnp.minimum(key, other), jnp.maximum(key, other))
            stride //= 2
        size *= 2
    columns = key.T
    turn[...] = jnp.concatenate([columns, columns], axis=1)
    return jnp.where(lane < height, turn[pl.ds(0, height, stride=2), :], turn[pl.ds(1, height, stride=2), :])


def list_facts(key, limit):
    group = (key >> 26) + 32
    used = group < GROUPS
    group = jnp.where(used, group, 0)
    block = jnp.where(used, (key >> 21) & 31, 0)
    step = jnp.where(used, (key >> 17) & 15, 2)
    lane = jnp.where(used, (key >> 14) & 7, 0)
    kind = jnp.where(used, (key >> 13) & 1, 0)
    place = jnp.minimum(key & 8191, limit)
    order = group * GROUP + lane
    degree = order + block * STEP + step
    number = 19 * group - (((group - 1) * (group - 1)) >> 2) + block
    ring = number & (RING - 1)
    number = jnp.where(used, number, LATE)
    at_value = (ring * SLOT + 1 + step) * WIDE + lane
    at_scale = ring * WIDE + lane
    target = place * PITCH
    m = order.astype(F32)
    first = degree - step
    product = jnp.ones_like(m)
    for q in range(STEP):
        j = first + q
        jf = j.astype(F32)
        ratio = (jf * jf - m * m) / (jf * jf - 0.25)
        product = jnp.where((j > order) & (j <= degree), product * ratio, product)
    at_harm = (order * 2 + kind) * 16
    return (number << 16) | at_scale, (at_value << 16) | at_harm, (degree << 21) | target, lax.rsqrt(product)


def gather_kernel(
    theta_hbm, lon_hbm, ratio_hbm, comp_hbm, weight_hbm, seen_hbm, unknown_ref, slab_hbm,
    number_ref, value_ref, target_ref, grow_ref, params_ref,
    theta_ref, lon_ref, ratio_ref, comp_ref, weight_ref, seen_ref, slab_ref,
    local, everyone, map_buf, key_buf, turn, send_sem, recv_sem, map_sem, in_sem,
):
    me = lax.axis_index("row")
    count = everyone.shape[0]
    half = theta_ref.shape[0]
    rows = map_buf.shape[1]
    width = slab_ref.shape[1]
    read_map = pltpu.make_async_copy(
        unknown_ref.at[:, pl.ds(pl.multiple_of(me * rows, 128), rows)], map_buf, map_sem.at[0]
    )
    inputs = [
        pltpu.make_async_copy(src, dst, in_sem.at[k])
        for k, (src, dst) in enumerate(
            (
                (theta_hbm, theta_ref),
                (lon_hbm, lon_ref),
                (ratio_hbm, ratio_ref),
                (comp_hbm, comp_ref),
                (weight_hbm, weight_ref),
                (seen_hbm, seen_ref),
                (slab_hbm, slab_ref),
            )
        )
    ]
    barrier = pltpu.get_barrier_semaphore()
    for d in range(1, count):
        pl.semaphore_signal(
            barrier, inc=1, device_id={"row": lax.rem(me + d, count)}, device_id_type=pl.DeviceIdType.MESH
        )
    for copy in inputs:
        copy.start()
    read_map.start()
    local[...] = jnp.zeros_like(local)
    for copy in inputs:
        copy.wait()
    for k, ref in enumerate((theta_ref, lon_ref, ratio_ref, comp_ref, weight_ref, seen_ref)):
        local[pl.ds(k, 1), pl.ds(0, half)] = ref[...].astype(F32).reshape(1, half)
    pl.semaphore_wait(barrier, count - 1)

    def send(d):
        return pltpu.make_async_remote_copy(
            src_ref=local, dst_ref=everyone.at[me], send_sem=send_sem.at[d], recv_sem=recv_sem.at[d],
            device_id={"row": lax.rem(me + d, count)}, device_id_type=pl.DeviceIdType.MESH,
        )

    def receive(d):
        return pltpu.make_async_remote_copy(
            src_ref=local, dst_ref=everyone.at[lax.rem(me + count - d, count)],
            send_sem=send_sem.at[d], recv_sem=recv_sem.at[d],
            device_id={"row": lax.rem(me + d, count)}, device_id_type=pl.DeviceIdType.MESH,
        )

    for d in sorted(range(1, count), key=lambda d: abs(2 * d - count)):
        send(d).start()
    everyone[me] = local[...]
    read_map.wait()
    lanes = lax.broadcasted_iota(I32, (1, 128), 1)
    for t in range((rows + width) // 128):
        ref, at = (map_buf, t * 128) if t * 128 < rows else (slab_ref, t * 128 - rows)
        part = [ref[pl.ds(k, 1), pl.ds(at, 128)] for k in range(3)]
        key_buf[pl.ds(t, 1), :] = row_key(part[0], part[1], part[2], lanes + t * 128)
    place = lax.broadcasted_iota(I32, key_buf.shape, 0) * 128 + lax.broadcasted_iota(I32, key_buf.shape, 1)
    key = sort_keys(jnp.where(place < rows + width, key_buf[...], (31 << 26) | place), turn)
    facts = list_facts(key[: number_ref.shape[0]], rows + width)
    outs = (number_ref, value_ref, target_ref, grow_ref)
    for ref, value in zip(outs, facts):
        ref[...] = value
    for d in range(1, count):
        receive(d).wait_recv()
    left = lax.broadcasted_iota(I32, (8, 128), 1) < half
    for c in range(PARTS):
        merged = jnp.where(left, everyone[2 * c], pltpu.roll(everyone[2 * c + 1], half, 1))
        params_ref[pl.ds(c, 8, stride=8), :] = merged
    for d in range(1, count):
        send(d).wait_send()


def kernel(
    col_ref, blocks_ref, number_hbm, value_hbm, target_hbm, grow_hbm,
    params_ref, table_hbm, inv_ref, logs_ref, right_ref, normal_ref,
    out_ref, right_out_ref,
    number_ref, value_ref, target_ref, grow_ref,
    value_buf, scale_buf, harm_buf, radial_buf, design_buf, seed_buf, level_buf, square_buf, table_ref,
    slab_hi, slab_lo, in_buf, out_buf, list_sem, in_sem, out_sem,
):
    rows, width = normal_ref.shape
    chunks = rows // CHUNK

    lists = [
        pltpu.make_async_copy(src, dst, list_sem.at[k])
        for k, (src, dst) in enumerate(
            (
                (number_hbm, number_ref),
                (value_hbm, value_ref),
                (target_hbm, target_ref),
                (grow_hbm, grow_ref),
                (table_hbm, table_ref),
            )
        )
    ]
    for copy in lists:
        copy.start()

    def fetch(index, slot):
        return pltpu.make_async_copy(
            normal_ref.at[pl.ds(pl.multiple_of(index * CHUNK, CHUNK), CHUNK)], in_buf.at[slot], in_sem.at[slot]
        )

    def put(index, slot):
        return pltpu.make_async_copy(
            out_buf.at[slot], out_ref.at[pl.ds(pl.multiple_of(index * CHUNK, CHUNK), CHUNK)], out_sem.at[slot]
        )


    def param(k):
        return params_ref[pl.ds(8 * k, 8), :]

    theta = param(0)
    lon = param(1)
    cos_t = jnp.cos(theta)
    sin_t = jnp.sin(theta)
    log_s = jnp.log(sin_t)
    comp = param(3)
    weight = param(4)
    scaled = weight * param(5)
    part0 = jnp.where(comp == 2.0, 1.0, jnp.where(comp == 1.0, 0.0, -1.0))
    part1 = jnp.where(comp == 2.0, 0.0, jnp.where(comp == 1.0, 1.0, -1.0))
    part1q = part1 / (sin_t * sin_t)
    inv_r = 1.0 / param(2)

    def spread(values, c):
        return jnp.broadcast_to(values[c : c + 1, :], (8, 128))

    twice = [spread(2.0 * cos_t, c) for c in range(PARTS)]
    logs = [spread(log_s, c) for c in range(PARTS)]
    subf = lax.broadcasted_iota(I32, (8, 128), 0).astype(F32)

    c1 = jnp.cos(lon)
    s1 = jnp.sin(lon)
    cs = [jnp.ones_like(c1)]
    sn = [jnp.zeros_like(c1)]
    for _ in range(8):
        cs.append(cs[-1] * c1 - sn[-1] * s1)
        sn.append(sn[-1] * c1 + cs[-2] * s1)
    c8, s8 = cs[8], sn[8]
    powers = [inv_r * inv_r * inv_r]
    step_r = inv_r
    for _ in range(7):
        powers.append(powers[-1] * inv_r)
    for _ in range(3):
        step_r = step_r * step_r

    def fill(block, carry):
        cc, ss, pw = carry
        base = block * 8
        for j in range(8):
            nf = (base + j).astype(F32)
            square = nf * nf
            harm_buf[pl.ds(pl.multiple_of(base * 32, 32) + j * 32, 8), :] = cc[j]
            harm_buf[pl.ds(pl.multiple_of(base * 32, 32) + j * 32 + 8, 8), :] = cc[j] * square
            harm_buf[pl.ds(pl.multiple_of(base * 32, 32) + j * 32 + 16, 8), :] = ss[j]
            harm_buf[pl.ds(pl.multiple_of(base * 32, 32) + j * 32 + 24, 8), :] = ss[j] * square
            inv_d = 1.0 / ((nf + 1.0) * (nf + 2.0))
            g = pw[j] * part1q * inv_d
            u = (cos_t * g) * (2.0 / (2.0 * nf - 1.0))
            radial_buf[pl.ds(pl.multiple_of(base * 32, 32) + j * 32, 8), :] = pw[j] * (part0 - part1 * ((2.0 * nf + 1.0) * inv_d)) + nf * g
            radial_buf[pl.ds(pl.multiple_of(base * 32, 32) + j * 32 + 8, 8), :] = g
            radial_buf[pl.ds(pl.multiple_of(base * 32, 32) + j * 32 + 16, 8), :] = u * square
            radial_buf[pl.ds(pl.multiple_of(base * 32, 32) + j * 32 + 24, 8), :] = u
        orders = subf + base.astype(F32)
        diag = logs_ref[pl.ds(pl.multiple_of(base, 8), 8), :]
        square = orders * orders - 0.25
        square_buf[pl.ds(pl.multiple_of(base, 8), 8), :] = square
        before = -1.0 / (1.0 - square * inv_ref[pl.ds(pl.multiple_of(base, 8), 8), :])
        for c in range(PARTS):
            log_seed = diag + orders * logs[c]
            level = jnp.minimum(jnp.ceil(log_seed * (1.0 / LOG_BIG)), 0.0)
            at = pl.multiple_of(block * 64, 64) + c * 8
            seed_buf[pl.ds(at, 8), :] = jnp.exp(log_seed - level * LOG_BIG) * before
            level_buf[pl.ds(at, 8), :] = level * 64.0
        return (
            tuple(cc[j] * c8 - ss[j] * s8 for j in range(8)),
            tuple(ss[j] * c8 + cc[j] * s8 for j in range(8)),
            tuple(pw[j] * step_r for j in range(8)),
        )

    lax.fori_loop(0, GROUPS, fill, (tuple(cs[:8]), tuple(sn[:8]), tuple(powers)))

    for copy in lists:
        copy.wait()
    for k in range(BUFS):
        fetch(k, k).start()

    def make_row(j):
        values = value_ref[j]
        targets = target_ref[j]
        at = values >> 16
        now = value_buf[pl.ds(at, 8, stride=PITCH), :]
        past = value_buf[pl.ds(at - WIDE, 8, stride=PITCH), :]
        scale = scale_buf[pl.ds(number_ref[j] & 65535, 8, stride=PITCH), :]
        n = pl.multiple_of(targets >> 16, 32)
        h = pl.multiple_of(values & 65535, 16)
        kept = now * radial_buf[pl.ds(n, 8), :] - past * radial_buf[pl.ds(n + 16, 8), :]
        spun = now * radial_buf[pl.ds(n + 8, 8), :] - past * radial_buf[pl.ds(n + 24, 8), :]
        body = harm_buf[pl.ds(h, 8), :] * kept - harm_buf[pl.ds(h + 8, 8), :] * spun
        design_buf[pl.ds(targets & 65535, 8), :] = body * (scale * grow_ref[j])

    def drain(cursor, number):
        def more(at):
            return number_ref[at] < ((number + 1) << 16)

        def piece(at):
            for u in range(DRAIN):
                make_row(at + u)
            return at + passed(at, number + 1)

        return lax.while_loop(more, piece, cursor)

    def passed(at, number):
        done = jnp.int32(0)
        for half in (8, 4, 2, 1, 1):
            done = done + jnp.where(number_ref[at + done + (half - 1)] < (number << 16), half, 0)
        return done

    zero = jnp.zeros((8, 128), F32)

    def block_step(number, state, cursor):
        one, two, levels = [list(x) for x in state]
        order = blocks_ref[number]
        first = blocks_ref[STEPS + number]
        ring = number & (RING - 1)
        at_scale = ring * WIDE
        at_value = ring * (SLOT * WIDE)
        at_seed = pl.multiple_of(order * 8, 64)
        opens = jnp.broadcast_to(order == first, (8, 128))
        sigma = table_ref[pl.ds(pl.multiple_of(number * 8, 8), 8), :]
        sigma_small = sigma * SMALL
        limit = 64.0 / sigma
        squares = square_buf[pl.ds(pl.multiple_of(order, 8), 8), :]
        for c in range(PARTS):
            big = jnp.abs(one[c]) > limit
            factor = jnp.where(big, sigma_small, sigma)
            one[c] = one[c] * factor
            two[c] = jnp.where(opens, seed_buf[pl.ds(at_seed + c * 8, 8), :], two[c] * factor)
            level = levels[c] + jnp.where(big, 64.0, 0.0)
            levels[c] = jnp.where(opens, level_buf[pl.ds(at_seed + c * 8, 8), :], level)
            value_buf[pl.ds(at_value + c * PITCH, 8), :] = one[c]
        for i in range(STEP):
            if i % BATCH == 0:
                for k in range(i * PACE // STEP, (i + BATCH) * PACE // STEP):
                    make_row(cursor + k)
            rho = 1.0 - squares * inv_ref[pl.ds(first + i, 8), :]
            fresh = [twice[c] * one[c] - rho * two[c] for c in range(PARTS)]
            for c in range(PARTS):
                value_buf[pl.ds(at_value + (1 + i) * WIDE + c * PITCH, 8), :] = fresh[c]
            one, two = fresh, one
        for c in range(PARTS):
            scale_buf[pl.ds(at_scale + c * PITCH, 8), :] = jnp.exp2(levels[c])
        return tuple(one), tuple(two), tuple(levels)

    def body(index, carry):
        state, cursor = carry
        number = index * BODY
        cursor = drain(cursor, number + BODY - 1 - RING)
        for k in range(BODY):
            state = block_step(number + k, state, cursor)
            cursor = cursor + passed(cursor, number + k)
        return state, cursor

    still = tuple((zero,) * PARTS for _ in range(3))
    _, cursor = lax.fori_loop(0, STEPS // BODY, body, (still, jnp.int32(0)))
    cursor = drain(cursor, BLOCKS)

    def clear(piece, _):
        for u in range(DRAIN):
            design_buf[pl.ds(target_ref[cursor + piece * DRAIN + u] & 65535, 8), :] = zero
        return 0

    lax.fori_loop(0, (rows + width - cursor + DRAIN - 1) // DRAIN, clear, 0)

    def entries(first, count, c):
        return design_buf[pl.ds(first * PITCH + c, count, stride=PITCH), :]

    peak = jnp.full((8, 128), 1e-30, F32)
    for c in range(PARTS):
        block = jnp.abs(entries(rows, width, c) * weight[c : c + 1, :])
        peak = jnp.maximum(peak, jnp.max(block.reshape(width // 8, 8, 128), axis=0))
    peak = jnp.max(peak, axis=(0, 1), keepdims=True)
    shrink = jnp.exp2(jnp.ceil(jnp.log2(jnp.broadcast_to(peak, (8, 128)))) - 7.0)[0:1, :]
    grow = 1.0 / shrink
    for c in range(PARTS):
        for half in range(width // 256):
            block = entries(rows + half * 256, 256, c)
            block = (block * weight[c : c + 1, :]).T
            hi = block.astype(BF16)
            lo = block - hi.astype(F32)
            cols = pl.ds(half * 256, 256)
            factor = jnp.concatenate([grow, grow], axis=1)
            slab_hi[pl.ds(c * 128, 128), cols] = hi
            slab_lo[pl.ds(c * 128, 128), cols] = (block * factor).astype(F8)
            slab_lo[pl.ds(OBS + c * 128, 128), cols] = (lo * (factor * 512.0)).astype(F8)
    shrink = jnp.concatenate([shrink] * (width // 128), axis=1) * (1.0 / 512.0)

    own = right_ref.shape[0]
    total = jnp.zeros((own, 128), F32)
    at = col_ref[0] * own
    for c in range(PARTS):
        total = total + entries(at, own, c) * scaled[c : c + 1, :]
    summed = lax.dot_general(
        jnp.ones((8, 128), F32), total, (((1,), (1,)), ((), ())),
        precision=lax.Precision.HIGHEST, preferred_element_type=F32,
    )
    right_out_ref[...] = right_ref[...] + summed[0:1, :].reshape(own)

    def chunk_body(index, _):
        slot = lax.rem(index, BUFS)
        his = []
        los = []
        tops = []
        for c in range(PARTS):
            x = entries(index * CHUNK, CHUNK, c)
            hi = x.astype(BF16)
            his.append(hi)
            los.append(((x - hi.astype(F32)) * 512.0).astype(F8))
            tops.append(x.astype(F8))
        update = jnp.dot(jnp.concatenate(los + tops, axis=1), slab_lo[...], preferred_element_type=F32) * shrink
        update += jnp.dot(jnp.concatenate(his, axis=1), slab_hi[...], preferred_element_type=F32)
        fetch(index, slot).wait()

        @pl.when(index >= BUFS)
        def _():
            put(index - BUFS, slot).wait()

        out_buf[slot] = in_buf[slot] + update
        put(index, slot).start()

        @pl.when(index + BUFS < chunks)
        def _():
            fetch(index + BUFS, slot).start()

        return 0

    lax.fori_loop(0, chunks, chunk_body, 0)
    for k in range(BUFS):
        put(chunks - BUFS + k, k).wait()


def local_update(params, col, facts, normal_slab, right_side):
    rows, width = normal_slab.shape
    own = right_side.shape[0]
    entries = facts[0].shape[0]
    smem = pl.BlockSpec(memory_space=pltpu.SMEM)
    vmem = pl.BlockSpec(memory_space=pltpu.VMEM)
    hbm = pl.BlockSpec(memory_space=pltpu.HBM)
    return pl.pallas_call(
        kernel,
        out_shape=(
            jax.ShapeDtypeStruct((rows, width), F32),
            jax.ShapeDtypeStruct((own,), F32),
        ),
        in_specs=[smem] * 2 + [hbm] * 4 + [vmem, hbm, vmem, vmem, vmem, hbm],
        out_specs=(hbm, vmem),
        scratch_shapes=[pltpu.SMEM((entries,), I32)] * 3
        + [pltpu.SMEM((entries,), F32)]
        + [
            pltpu.VMEM((RING * SLOT * WIDE, 128), F32),
            pltpu.VMEM((RING * WIDE, 128), F32),
            pltpu.VMEM((TOP * 32, 128), F32),
            pltpu.VMEM((TOP * 32, 128), F32),
            pltpu.VMEM(((rows + width + 1) * PITCH, 128), F32),
            pltpu.VMEM((GROUPS * 64, 128), F32),
            pltpu.VMEM((GROUPS * 64, 128), F32),
            pltpu.VMEM((TOP, 128), F32),
            pltpu.VMEM((STEPS * 8, 128), F32),
            pltpu.VMEM((OBS, width), BF16),
            pltpu.VMEM((2 * OBS, width), F8),
            pltpu.VMEM((BUFS, CHUNK, width), F32),
            pltpu.VMEM((BUFS, CHUNK, width), F32),
            pltpu.SemaphoreType.DMA((5,)),
            pltpu.SemaphoreType.DMA((BUFS,)),
            pltpu.SemaphoreType.DMA((BUFS,)),
        ],
        compiler_params=pltpu.CompilerParams(vmem_limit_bytes=62 * 1024 * 1024),
        name="normal_update",
    )(
        col, jnp.asarray(block_lists()), *facts, params, jnp.asarray(block_scales()), jnp.asarray(inverse_squares()),
        jnp.asarray(diagonal_logs()), right_side, normal_slab,
    )


def on_device(
    colatitude, longitude, radius_ratio, component, obs_weight, observed,
    unknown_map, slab_map, normal_slab, right_side,
):
    rows, width = normal_slab.shape
    col = lax.axis_index("col").astype(I32).reshape(1)
    entries = -(-(rows + width + 2 * PACE) // 1024) * 1024
    total = 1 << (rows + width - 1).bit_length()
    shape = (entries // 128, 128)
    count = lax.axis_size("row")
    vmem = pl.BlockSpec(memory_space=pltpu.VMEM)
    outs = pl.pallas_call(
        gather_kernel,
        out_shape=tuple(jax.ShapeDtypeStruct(shape, I32) for _ in range(3))
        + (jax.ShapeDtypeStruct(shape, F32), jax.ShapeDtypeStruct((64, 128), F32)),
        in_specs=[pl.BlockSpec(memory_space=pltpu.HBM)] * 8,
        out_specs=(vmem,) * 5,
        scratch_shapes=[
            pltpu.VMEM(colatitude.shape, F32),
            pltpu.VMEM(colatitude.shape, F32),
            pltpu.VMEM(colatitude.shape, F32),
            pltpu.VMEM(colatitude.shape, I32),
            pltpu.VMEM(colatitude.shape, F32),
            pltpu.VMEM(colatitude.shape, F32),
            pltpu.VMEM(slab_map.shape, I32),
            pltpu.VMEM((8, 128), F32),
            pltpu.VMEM((count, 8, 128), F32),
            pltpu.VMEM((3, rows), I32),
            pltpu.VMEM((total // 128, 128), I32),
            pltpu.VMEM((128, 128), I32),
            pltpu.SemaphoreType.DMA((count,)),
            pltpu.SemaphoreType.DMA((count,)),
            pltpu.SemaphoreType.DMA((1,)),
            pltpu.SemaphoreType.DMA((7,)),
        ],
        compiler_params=pltpu.CompilerParams(collective_id=0, has_side_effects=True),
        name="gather_observations",
    )(colatitude, longitude, radius_ratio, component, obs_weight, observed, unknown_map, slab_map)
    facts = tuple(x.reshape(entries) for x in outs[:4])
    return local_update(outs[4], col, facts, normal_slab, right_side)


def solution(mesh):
    return jax.shard_map(
        on_device,
        mesh=mesh,
        in_specs=(
            P("row"), P("row"), P("row"), P("row"), P("row"), P("row"),
            P(), P(None, "col"), P("row", "col"), P(("row", "col")),
        ),
        out_specs=(P("row", "col"), P(("row", "col"))),
        check_vma=False,
    )
```
